32 devices in a mesh: ctx: 16 (over z, x, core), tp: 2 (over y).
Axes of the slice: x: 2, y: 2, z: 4, core: 2. Of those that a mesh axis runs over, the one named last changes fastest.
Arguments:
- tokens_in: bfloat16 [2048, 8192], P('ctx', 'tp'), may hold values from -6 to 6
- w_query: bfloat16 [2, 4096, 8192], P(None, 'ctx', 'tp'), may hold values from -0.0625 to 0.0625
- w_key: bfloat16 [2, 4096, 8192], P(None, 'ctx', 'tp'), may hold values from -0.0625 to 0.0625
- w_value: bfloat16 [2, 4096, 8192], P(None, 'ctx', 'tp'), may hold values from -0.0625 to 0.0625
- short_taps: float32 [3, 2, 256, 3], P(None, 'tp', 'ctx'), may hold values from -2.5 to 2.5
- long_taps: float32 [2, 256, 128], P('tp', 'ctx'), may hold values from -0.5 to 0.5
- grad_out: bfloat16 [8192, 2048], P('tp', 'ctx'), may hold values from -6 to 6
Outputs:
- mixed_out: bfloat16 [8192, 2048], P('tp', 'ctx')
- grad_tokens: bfloat16 [2048, 8192], P('ctx', 'tp')
- grad_short: float32 [3, 2, 256, 3], P(None, 'tp', 'ctx')
- grad_long: float32 [2, 256, 128], P('tp', 'ctx')
The draws below stay inside these ranges and needn't reach their ends.
All inputs are finite; a program needn't handle non-finite values.
Results may differ from the reference program's by a relative error of at most 0.019.
Values may be sent and summed in bfloat16 or wider, within the bound.
No kernel may reach another device: no remote copies, remote signals or barrier semaphores. Data moves between devices by JAX's collectives and lax.ppermute only.
A program may use at most 192 MiB of HBM per device.

```python
import jax
import jax.numpy as jnp
from jax import lax

D = 8192
GROUP = 16
SHORT = 3
LONG = 128
TOKENS = 2048
N_CTX = 16
N_TP = 2


def steps_of(rng, shape, split, low, high):
    def one(dim, blocks):
        heights = jax.random.uniform(jax.random.fold_in(jax.random.fold_in(rng, 6), dim), (blocks,), jnp.float32, low / len(split), high / len(split))
        return jnp.repeat(jnp.exp(heights), shape[dim] // blocks).reshape((-1,) + (1,) * (len(shape) - dim - 1))

    factor_of = one(*split[0])
    for cut in split[1:]:
        factor_of = factor_of * one(*cut)
    return factor_of


def bell_draw(stream_key, dims, scale, bound, shards=(), dtype=jnp.bfloat16):
    drawn = jax.random.normal(stream_key, dims, jnp.float32) * scale
    if len(shards) > 0:
        drawn = steps_of(stream_key, dims, shards, -0.22, 0.18) * drawn
    return jnp.clip(drawn, min=-bound, max=bound).astype(dtype)


def setup_inputs(seed: int = 0) -> dict:
    keys = jax.random.split(jax.random.key(seed), 8)
    tokens_in = bell_draw(keys[0], (TOKENS, D), 1.0, 6.0, ((0, 16), (1, 2)))
    w_query = bell_draw(keys[1], (N_TP, D // N_TP, D), D ** -0.5, 0.0625, ((1, 16), (2, 2)))
    w_key = bell_draw(keys[2], (N_TP, D // N_TP, D), D ** -0.5, 0.0625, ((1, 16), (2, 2)))
    w_value = bell_draw(keys[3], (N_TP, D // N_TP, D), D ** -0.5, 0.0625, ((1, 16), (2, 2)))
    short_taps = bell_draw(keys[4], (3, N_TP, D // N_TP // GROUP, SHORT), 0.4, 2.5, ((1, 2), (2, 16)), jnp.float32)
    long_taps = bell_draw(keys[5], (N_TP, D // N_TP // GROUP, LONG), 0.09, 0.5, ((0, 2), (1, 16)), jnp.float32)
    grad_out = bell_draw(keys[6], (D, TOKENS), 1.0, 6.0, ((0, 2), (1, 16)))
    return {"tokens_in": tokens_in, "w_query": w_query, "w_key": w_key, "w_value": w_value, "short_taps": short_taps, "long_taps": long_taps, "grad_out": grad_out}


def short_filter(signal, kernel_taps):
    channels, length = signal.shape
    groups = kernel_taps.shape[0]
    grouped = signal.reshape(groups, GROUP, length)
    summed = kernel_taps[:, None, 0:1] * grouped
    for delay_step in range(1, SHORT):
        shifted = jnp.pad(grouped, ((0, 0), (0, 0), (delay_step, 0)))[:, :, :length]
        summed = summed + kernel_taps[:, None, delay_step:delay_step + 1] * shifted
    return summed.reshape(channels, length)

def long_filter(signal, kernel_taps):
    channels, length = signal.shape
    groups = kernel_taps.shape[0]
    blocks = signal.reshape(groups, GROUP, length // LONG, LONG)
    offsets = jnp.arange(LONG)[None, :] - jnp.arange(LONG)[:, None]
    wrapped = jnp.where(offsets >= 0, offsets, offsets + LONG)
    table = (wrapped[None, :, :] == jnp.arange(LONG)[:, None, None]).astype(jnp.float32)
    full = jnp.einsum('gk,kij->gij', kernel_taps, table, precision=lax.Precision.HIGHEST)
    nearby = jnp.where(offsets >= 0, full, 0.0)
    distant = jnp.where(offsets < 0, full, 0.0)
    earlier = jnp.pad(blocks, ((0, 0), (0, 0), (1, 0), (0, 0)))[:, :, :-1, :]
    summed = jnp.einsum('gcbi,gij->gcbj', blocks, nearby, precision=lax.Precision.HIGHEST)
    summed = summed + jnp.einsum('gcbi,gij->gcbj', earlier, distant, precision=lax.Precision.HIGHEST)
    return summed.reshape(channels, length)

def mixing(proj_query, proj_key, proj_value, short_kernel, long_kernel):
    feat_query = short_filter(proj_query, short_kernel[0])
    feat_key = short_filter(proj_key, short_kernel[1])
    feat_value = short_filter(proj_value, short_kernel[2])
    product = feat_key * feat_value
    inner_conv = long_filter(product, long_kernel)
    return feat_query * inner_conv

def reference(tokens_in, w_query, w_key, w_value, short_taps, long_taps, grad_out):
    block_width = D // N_TP

    def project(weight):
        matrix = weight.reshape(D, D)
        summed = jnp.zeros((D, TOKENS), jnp.float32)
        for column in range(N_TP):
            partial_sum = jnp.dot(matrix[:, column * block_width:(column + 1) * block_width], tokens_in[:, column * block_width:(column + 1) * block_width].T, preferred_element_type=jnp.float32)
            rounded = lax.optimization_barrier(partial_sum.astype(jnp.bfloat16))
            summed = summed + rounded.astype(jnp.float32)
        return summed
    short_kernel = short_taps.reshape(3, D // GROUP, SHORT)
    long_kernel = long_taps.reshape(D // GROUP, LONG)
    outputs, backward = jax.vjp(mixing, project(w_query), project(w_key), project(w_value), short_kernel, long_kernel)
    mixed_out = outputs.astype(jnp.bfloat16)
    gradients = backward(grad_out.astype(jnp.float32))
    grad_proj = jnp.stack([gradients[0], gradients[1], gradients[2]]).astype(jnp.bfloat16)
    grad_proj = grad_proj.reshape(3, N_TP, block_width, TOKENS)
    stacked = jnp.stack([w_query, w_key, w_value])
    slab_rows = D // (N_TP * N_CTX)
    summed = jnp.zeros((TOKENS, D), jnp.float32)
    for owner_block in range(N_CTX):
        rows_grad = grad_proj[:, :, owner_block * slab_rows:(owner_block + 1) * slab_rows, :]
        rows_grad = rows_grad.reshape(3 * N_TP * slab_rows, TOKENS)
        rows_weight = stacked[:, :, owner_block * slab_rows:(owner_block + 1) * slab_rows, :]
        rows_weight = rows_weight.reshape(3 * N_TP * slab_rows, D)
        partial_sum = lax.dot_general(rows_grad, rows_weight, (((0,), (0,)), ((), ())), preferred_element_type=jnp.float32)
        rounded = lax.optimization_barrier(partial_sum.astype(jnp.bfloat16))
        summed = summed + rounded.astype(jnp.float32)
    grad_tokens = summed.astype(jnp.bfloat16)
    grad_short = gradients[3].reshape(3, N_TP, D // N_TP // GROUP, SHORT)
    grad_long = gradients[4].reshape(N_TP, D // N_TP // GROUP, LONG)
    return (mixed_out, grad_tokens, grad_short, grad_long)
```

```python
import functools

import jax
import jax.numpy as jnp
import numpy as np
from jax import lax
from jax.experimental import pallas as pl
from jax.experimental.pallas import tpu as pltpu
from jax.sharding import PartitionSpec as P

GROUP = 16
SHORT = 3
LONG = 128
F32 = jnp.float32
BF16 = jnp.bfloat16


def ring_of(mesh):
    chips = mesh.shape["ctx"] // 2
    plain = list(range(chips))
    devices = np.asarray(mesh.devices).reshape(mesh.shape["ctx"], -1)[:, 0]
    places = [getattr(devices[2 * chip], "coords", None) for chip in plain]
    if any(place is None for place in places):
        return plain
    places = np.array([list(place)[:3] for place in places])
    axes = [axis for axis in range(3) if len(set(places[:, axis])) > 1]
    if len(axes) != 2:
        return plain
    rung = min(axes, key=lambda axis: len(set(places[:, axis])))
    along = axes[0] if rung == axes[1] else axes[1]
    sides = sorted(set(places[:, rung]))
    if len(sides) != 2:
        return plain
    there = [c for c in plain if places[c, rung] == sides[0]]
    back = [c for c in plain if places[c, rung] == sides[1]]
    there.sort(key=lambda c: places[c, along])
    back.sort(key=lambda c: -places[c, along])
    return there + back


def dot(a, b, dims):
    return lax.dot_general(a, b, (dims, ((), ())), preferred_element_type=F32)


def mix_body(count, sets, per_step, order, short_ref, long_ref, g_ref, *refs):
    proj_refs = [refs[s * count : (s + 1) * count] for s in range(sets)]
    refs = refs[sets * count :]
    mixed_ref, d_refs, gs_ref, gl_ref = refs[0], refs[1 : 1 + count], refs[1 + count], refs[2 + count]
    p_s, x_s, y_s, d_s, e_s = refs[3 + count :]
    blocks = g_ref.shape[0]
    rows = blocks * GROUP
    step = pl.program_id(0)

    @pl.when(step == 0)
    def _():
        p_s[:, :, 0:GROUP, :] = jnp.zeros((per_step, 3, GROUP, LONG), F32)
        x_s[:, 0:GROUP, :] = jnp.zeros((per_step, GROUP, LONG), BF16)
        y_s[:, rows:, :] = jnp.zeros((per_step, GROUP, LONG), BF16)
        d_s[:, :, rows:, :] = jnp.zeros((per_step, 3, GROUP, LONG), F32)

    lane = lax.broadcasted_iota(jnp.int32, (rows, LONG), 1)
    lane8 = lax.broadcasted_iota(jnp.int32, (8, LONG), 1)
    sub8 = lax.broadcasted_iota(jnp.int32, (8, LONG), 0)
    del lane8
    col = lax.broadcasted_iota(jnp.int32, (LONG, LONG), 1)
    row = lax.broadcasted_iota(jnp.int32, (LONG, LONG), 0)

    for j in range(per_step):
        group = step * per_step + j
        mine = slice(j * GROUP, (j + 1) * GROUP)
        for a in range(count):
            for h in range(2):
                at = pl.multiple_of((order[2 * a + h] + 1) * GROUP, GROUP)
                for i in range(3):
                    part = proj_refs[0][a][i, mine, h * LONG : (h + 1) * LONG].astype(F32)
                    for s in range(1, sets):
                        part = part + proj_refs[s][a][i, mine, h * LONG : (h + 1) * LONG].astype(F32)
                    p_s[j, i, pl.ds(at, GROUP), :] = part
        taps = [[short_ref[i, group, k] for k in range(SHORT)] for i in range(3)]
        feats = []
        for i in range(3):
            whole = p_s[j, i]
            one = pltpu.roll(whole, 1, 1)
            two = pltpu.roll(whole, 2, 1)
            one = jnp.where(lane < 1, one[:rows], one[GROUP:])
            two = jnp.where(lane < 2, two[:rows], two[GROUP:])
            feats.append(taps[i][0] * whole[GROUP:] + taps[i][1] * one + taps[i][2] * two)
        fq, fk, fv = feats
        x_s[j, GROUP:, :] = (fk * fv).astype(BF16)

        base = jnp.broadcast_to(long_ref[0, j : j + 1, :], (8, LONG))
        for bit in (1, 2, 4):
            base = jnp.where((sub8 & bit) != 0, pltpu.roll(base, bit, 1), base)
        full = jnp.concatenate([base] + [pltpu.roll(base, 8 * m, 1) for m in range(1, LONG // 8)], axis=0)
        near = jnp.where(col >= row, full, 0.0).astype(BF16)
        far = jnp.where(col < row, full, 0.0).astype(BF16)

        x_two = jnp.concatenate([x_s[j, GROUP:, :], x_s[j, :rows, :]], axis=1)
        inner = dot(x_two, jnp.concatenate([near, far], axis=0), ((1,), (0,)))
        g = g_ref[:, mine, :].reshape(rows, LONG).astype(F32)
        mixed_ref[:, mine, :] = (fq * inner).astype(BF16).reshape(blocks, GROUP, LONG)
        y_s[j, :rows, :] = (g * fq).astype(BF16)
        y_one = y_s[j, :rows, :]
        y_two = jnp.concatenate([y_one, y_s[j, GROUP:, :]], axis=1)
        d_product = dot(y_two, jnp.concatenate([near, far], axis=1), ((1,), (1,)))

        pairs = dot(x_two, y_one, ((0,), (0,)))
        fold = jnp.where(col >= row, pairs[:LONG], pairs[LONG:])
        width = LONG
        while width > 8:
            width //= 2
            fold = fold[:width] + pltpu.roll(fold[width:], LONG - width, 1)
        for bit in (4, 2, 1):
            fold = jnp.where((sub8 & bit) != 0, pltpu.roll(fold, LONG - bit, 1), fold)
        gl_ref[0, j : j + 1, :] = jnp.sum(fold, axis=0, keepdims=True)

        for i, d in enumerate((g * inner, d_product * fv, d_product * fk)):
            d_s[j, i, :rows, :] = d
            whole = d_s[j, i]
            one = pltpu.roll(whole, LONG - 1, 1)
            two = pltpu.roll(whole, LONG - 2, 1)
            one = jnp.where(lane >= LONG - 1, one[GROUP:], one[:rows])
            two = jnp.where(lane >= LONG - 2, two[GROUP:], two[:rows])
            p = p_s[j, i, GROUP:, :]
            for k, moved in enumerate((d, one, two)):
                gs_ref[0, j, 3 * i + k : 3 * i + k + 1, :] = jnp.sum(p * moved, axis=0, keepdims=True)
            e_s[j, i] = (taps[i][0] * d + taps[i][1] * one + taps[i][2] * two).astype(BF16)
        for a in range(count):
            for h in range(2):
                at = pl.multiple_of(order[2 * a + h] * GROUP, GROUP)
                for i in range(3):
                    d_refs[a][i, mine, h * LONG : (h + 1) * LONG] = e_s[j, i, pl.ds(at, GROUP), :]


def mix(order, short_kernel, long_kernel, g, proj_sets):
    blocks, channels, _ = g.shape
    count, sets = len(proj_sets[0]), len(proj_sets)
    groups = channels // GROUP
    per_step = 2 if groups % 2 == 0 else 1
    steps = groups // per_step
    rows = blocks * GROUP
    high = per_step * GROUP
    proj_spec = pl.BlockSpec((3, high, 2 * LONG), lambda i, o: (0, i, 0))
    token_spec = pl.BlockSpec((blocks, high, LONG), lambda i, o: (0, i, 0))
    outs = pl.pallas_call(
        functools.partial(mix_body, count, sets, per_step),
        grid_spec=pltpu.PrefetchScalarGridSpec(
            num_scalar_prefetch=1,
            grid=(steps,),
            in_specs=[
                pl.BlockSpec(memory_space=pltpu.SMEM),
                pl.BlockSpec((1, per_step, LONG), lambda i, o: (i, 0, 0)),
                token_spec,
            ]
            + [proj_spec] * (count * sets),
            out_specs=[token_spec]
            + [proj_spec] * count
            + [
                pl.BlockSpec((1, per_step, 3 * SHORT, LONG), lambda i, o: (i, 0, 0, 0)),
                pl.BlockSpec((1, per_step, LONG), lambda i, o: (i, 0, 0)),
            ],
            scratch_shapes=[
                pltpu.VMEM((per_step, 3, rows + GROUP, LONG), F32),
                pltpu.VMEM((per_step, rows + GROUP, LONG), BF16),
                pltpu.VMEM((per_step, rows + GROUP, LONG), BF16),
                pltpu.VMEM((per_step, 3, rows + GROUP, LONG), F32),
                pltpu.VMEM((per_step, 3, rows, LONG), BF16),
            ],
        ),
        out_shape=[jax.ShapeDtypeStruct((blocks, channels, LONG), BF16)]
        + [jax.ShapeDtypeStruct((3, channels, 2 * LONG), BF16)] * count
        + [
            jax.ShapeDtypeStruct((steps, per_step, 3 * SHORT, LONG), F32),
            jax.ShapeDtypeStruct((steps, per_step, LONG), F32),
        ],
        compiler_params=pltpu.CompilerParams(vmem_limit_bytes=32 * 1024 * 1024),
        cost_estimate=pl.CostEstimate(
            flops=5 * 2 * channels * blocks * LONG * LONG * 10,
            bytes_accessed=channels * blocks * LONG * 2 * (3 * sets + 5),
            transcendentals=0,
        ),
    )(order, short_kernel, long_kernel.reshape(steps, per_step, LONG), g, *[x for s in proj_sets for x in s])
    mixed, d_proj, gs, gl = outs[0], outs[1 : 1 + count], outs[1 + count], outs[2 + count]
    grad_short = jnp.sum(gs, axis=-1).reshape(groups, 3, SHORT).transpose(1, 0, 2)
    return mixed, d_proj, grad_short, gl.reshape(groups, LONG)


def on_device(ring, n_tp, tokens_in, w_query, w_key, w_value, short_taps, long_taps, grad_out):
    chips = len(ring)
    half = chips // 2
    n_ctx = 2 * chips
    held, width = tokens_in.shape
    channels = w_query.shape[1]
    weights = (w_query, w_key, w_value)

    def pairs(hop):
        return [(2 * ring[j] + k, 2 * ring[(j + hop) % chips] + k) for j in range(chips) for k in range(2)]

    ahead, behind = pairs(1), pairs(-1)
    mates = [(d, d ^ 1) for d in range(n_ctx)]

    def onward(x):
        return lax.ppermute(x, "ctx", ahead)

    def back(x):
        return lax.ppermute(x, "ctx", behind)

    def swap(x):
        return lax.ppermute(x, "ctx", mates)

    def across(x):
        return lax.ppermute(x, "tp", [(0, 1), (1, 0)])

    me = lax.axis_index("ctx")
    place_of = np.argsort(np.array(ring))
    place = jnp.asarray(place_of, jnp.int32)[me // 2]

    def block_at(hop, other):
        chip = jnp.asarray(ring, jnp.int32)[(place + hop + chips) % chips]
        return 2 * chip + (me % 2 + other) % 2

    lists = [[(0, 0), (0, 1)]]
    for s in range(1, half):
        lists += [[(-s, 0), (s, 0)], [(-s, 1), (s, 1)]]
    lists += [[(half, 0), (half, 1)]]
    order = jnp.stack([block_at(*item) for pair in lists for item in pair]).astype(jnp.int32)

    if n_tp == 2:
        t = lax.axis_index("tp")
        rows_of = [lax.dynamic_index_in_dim(w, b, 0, keepdims=False) for b in (t, 1 - t) for w in weights]
        flat = jnp.concatenate(rows_of, axis=0)
    else:
        flat = jnp.stack(weights).reshape(-1, width)
    stay = 3 * channels

    def project(x):
        if n_tp == 2:
            far = dot(flat[stay:], x, ((1,), (1,))).astype(BF16)
            far = across(far)
            near = dot(flat[:stay], x, ((1,), (1,))).astype(BF16)
            return [y.reshape(3, channels, -1) for y in (near, far)]
        y = dot(flat, x, ((1,), (1,))).astype(BF16).reshape(3, n_tp, channels, -1)
        return [lax.psum_scatter(y, "tp", scatter_dimension=1, tiled=True).reshape(3, channels, -1)]

    def unproject(d):
        if n_tp == 2:
            d = d.reshape(stay, -1)
            d = jnp.concatenate([d, across(d)], axis=0)
        else:
            d = lax.all_gather(d.reshape(3, 1, channels, -1), "tp", axis=1, tiled=True)
            d = d.reshape(-1, d.shape[-1])
        return dot(d, flat, ((0,), (0,))).astype(BF16)

    incoming = lax.all_to_all(
        grad_out.reshape(n_ctx, channels, held), "ctx", split_axis=0, concat_axis=0, tiled=True
    )

    projected = [project(jnp.concatenate([tokens_in, swap(tokens_in)], axis=0))]
    right = left = tokens_in
    for s in range(1, half):
        right, left = onward(right), back(left)
        both = jnp.concatenate([right, left], axis=0)
        projected += [project(both), project(swap(both))]
    cut = held // 2
    both = jnp.concatenate([onward(right[:cut]), back(left[cut:])], axis=0)
    projected.append(project(jnp.concatenate([both, swap(both)], axis=0)))

    mixed, d_proj, grad_short, grad_long = mix(
        order,
        short_taps.reshape(3, -1, SHORT),
        long_taps.reshape(-1, LONG),
        incoming,
        [list(s) for s in zip(*projected)],
    )
    mixed_out = lax.all_to_all(mixed, "ctx", split_axis=0, concat_axis=0, tiled=True).reshape(-1, held)

    far = unproject(d_proj[-1])
    total = (far[:held].astype(F32) + swap(far[held:]).astype(F32)).astype(BF16)
    from_behind = jnp.pad(onward(total[:cut]), ((0, held - cut), (0, 0)))
    from_ahead = jnp.pad(back(total[cut:]), ((cut, 0), (0, 0)))
    for s in range(half - 1, 0, -1):
        own = unproject(d_proj[2 * s - 1])
        given = swap(unproject(d_proj[2 * s]))
        fro = own[:held].astype(F32) + given[:held].astype(F32) + from_ahead.astype(F32)
        to = own[held:].astype(F32) + given[held:].astype(F32) + from_behind.astype(F32)
        from_behind = onward(to.astype(BF16))
        from_ahead = back(fro.astype(BF16))
    own = unproject(d_proj[0])
    total = own[:held].astype(F32) + swap(own[held:]).astype(F32)
    grad_tokens = (total + from_behind.astype(F32) + from_ahead.astype(F32)).astype(BF16)
    return (
        mixed_out,
        grad_tokens,
        grad_short.reshape(3, 1, -1, SHORT),
        grad_long.reshape(1, -1, LONG),
    )


def solution(mesh):
    placed = (
        P("ctx", "tp"),
        P(None, "ctx", "tp"),
        P(None, "ctx", "tp"),
        P(None, "ctx", "tp"),
        P(None, "tp", "ctx", None),
        P("tp", "ctx", None),
        P("tp", "ctx"),
    )
    return jax.shard_map(
        functools.partial(on_device, ring_of(mesh), mesh.shape["tp"]),
        mesh=mesh,
        in_specs=placed,
        out_specs=(
            P("tp", "ctx"),
            P("ctx", "tp"),
            P(None, "tp", "ctx", None),
            P("tp", "ctx", None),
        ),
        check_vma=False,
    )
```

```python
import functools

import jax
import jax.numpy as jnp
import numpy as np
from jax import lax
from jax.experimental import pallas as pl
from jax.experimental.pallas import tpu as pltpu
from jax.sharding import PartitionSpec as P

GROUP = 16
SHORT = 3
LONG = 128
F32 = jnp.float32
BF16 = jnp.bfloat16
VMEM = 58 * 1024 * 1024
VMEM_DOT = 24 * 1024 * 1024


def ring_of(mesh):
    chips = mesh.shape["ctx"] // 2
    plain = list(range(chips))
    devices = np.asarray(mesh.devices).reshape(mesh.shape["ctx"], -1)[:, 0]
    places = [getattr(devices[2 * chip], "coords", None) for chip in plain]
    if any(place is None for place in places):
        return plain
    places = np.array([list(place)[:3] for place in places])
    axes = [axis for axis in range(3) if len(set(places[:, axis])) > 1]
    if len(axes) != 2:
        return plain
    rung = min(axes, key=lambda axis: len(set(places[:, axis])))
    along = axes[0] if rung == axes[1] else axes[1]
    sides = sorted(set(places[:, rung]))
    if len(sides) != 2:
        return plain
    there = [c for c in plain if places[c, rung] == sides[0]]
    back = [c for c in plain if places[c, rung] == sides[1]]
    there.sort(key=lambda c: places[c, along])
    back.sort(key=lambda c: -places[c, along])
    return there + back


def dot(a, b, dims):
    return lax.dot_general(a, b, (dims, ((), ())), preferred_element_type=F32)


def mix_body(count, sets, per_step, order, short_ref, long_ref, g_ref, *refs):
    proj_refs = [refs[s * count : (s + 1) * count] for s in range(sets)]
    refs = refs[sets * count :]
    mixed_ref, d_refs, gs_ref, gl_ref = refs[0], refs[1 : 1 + count], refs[1 + count], refs[2 + count]
    p_s, x_s, y_s, d_s, e_s = refs[3 + count :]
    blocks = g_ref.shape[0]
    rows = blocks * GROUP
    step = pl.program_id(0)

    @pl.when(step == 0)
    def _():
        p_s[:, :, 0:GROUP, :] = jnp.zeros((per_step, 3, GROUP, LONG), F32)
        x_s[:, 0:GROUP, :] = jnp.zeros((per_step, GROUP, LONG), BF16)
        y_s[:, rows:, :] = jnp.zeros((per_step, GROUP, LONG), BF16)
        d_s[:, :, rows:, :] = jnp.zeros((per_step, 3, GROUP, LONG), F32)

    halves = [(a, h) for a in range(count) for h in range(proj_refs[0][a].shape[2] // LONG)]
    places = [(a, h, where) for where, (a, h) in enumerate(halves)]
    lane = lax.broadcasted_iota(jnp.int32, (rows, LONG), 1)
    sub8 = lax.broadcasted_iota(jnp.int32, (8, LONG), 0)
    col = lax.broadcasted_iota(jnp.int32, (LONG, LONG), 1)
    row = lax.broadcasted_iota(jnp.int32, (LONG, LONG), 0)

    for j in range(per_step):
        group = step * per_step + j
        mine = slice(j * GROUP, (j + 1) * GROUP)
        for a, h, where in places:
            at = pl.multiple_of((order[where] + 1) * GROUP, GROUP)
            for i in range(3):
                part = proj_refs[0][a][i, mine, h * LONG : (h + 1) * LONG].astype(F32)
                for s in range(1, sets):
                    part = part + proj_refs[s][a][i, mine, h * LONG : (h + 1) * LONG].astype(F32)
                p_s[j, i, pl.ds(at, GROUP), :] = part
        taps = [[short_ref[i, group, k] for k in range(SHORT)] for i in range(3)]
        feats = []
        for i in range(3):
            whole = p_s[j, i]
            one = pltpu.roll(whole, 1, 1)
            two = pltpu.roll(whole, 2, 1)
            one = jnp.where(lane < 1, one[:rows], one[GROUP:])
            two = jnp.where(lane < 2, two[:rows], two[GROUP:])
            feats.append(taps[i][0] * whole[GROUP:] + taps[i][1] * one + taps[i][2] * two)
        fq, fk, fv = feats
        x_s[j, GROUP:, :] = (fk * fv).astype(BF16)

        base = jnp.broadcast_to(long_ref[0, j : j + 1, :], (8, LONG))
        for bit in (1, 2, 4):
            base = jnp.where((sub8 & bit) != 0, pltpu.roll(base, bit, 1), base)
        full = jnp.concatenate([base] + [pltpu.roll(base, 8 * m, 1) for m in range(1, LONG // 8)], axis=0)
        near = jnp.where(col >= row, full, 0.0).astype(BF16)
        far = jnp.where(col < row, full, 0.0).astype(BF16)

        x_two = jnp.concatenate([x_s[j, GROUP:, :], x_s[j, :rows, :]], axis=1)
        inner = dot(x_two, jnp.concatenate([near, far], axis=0), ((1,), (0,)))
        g = g_ref[:, mine, :].reshape(rows, LONG).astype(F32)
        mixed_ref[:, mine, :] = (fq * inner).astype(BF16).reshape(blocks, GROUP, LONG)
        y_s[j, :rows, :] = (g * fq).astype(BF16)
        y_one = y_s[j, :rows, :]
        y_two = jnp.concatenate([y_one, y_s[j, GROUP:, :]], axis=1)
        d_product = dot(y_two, jnp.concatenate([near, far], axis=1), ((1,), (1,)))

        pairs = dot(x_two, y_one, ((0,), (0,)))
        fold = jnp.where(col >= row, pairs[:LONG], pairs[LONG:])
        width = LONG
        while width > 8:
            width //= 2
            fold = fold[:width] + pltpu.roll(fold[width:], LONG - width, 1)
        for bit in (4, 2, 1):
            fold = jnp.where((sub8 & bit) != 0, pltpu.roll(fold, LONG - bit, 1), fold)
        gl_ref[0, j : j + 1, :] = jnp.sum(fold, axis=0, keepdims=True)

        for i, d in enumerate((g * inner, d_product * fv, d_product * fk)):
            d_s[j, i, :rows, :] = d
            whole = d_s[j, i]
            one = pltpu.roll(whole, LONG - 1, 1)
            two = pltpu.roll(whole, LONG - 2, 1)
            one = jnp.where(lane >= LONG - 1, one[GROUP:], one[:rows])
            two = jnp.where(lane >= LONG - 2, two[GROUP:], two[:rows])
            p = p_s[j, i, GROUP:, :]
            for k, moved in enumerate((d, one, two)):
                gs_ref[0, j, 3 * i + k : 3 * i + k + 1, :] = jnp.sum(p * moved, axis=0, keepdims=True)
            e_s[j, i] = (taps[i][0] * d + taps[i][1] * one + taps[i][2] * two).astype(BF16)
        for a, h, where in places:
            at = pl.multiple_of(order[where] * GROUP, GROUP)
            for i in range(3):
                d_refs[a][i, mine, h * LONG : (h + 1) * LONG] = e_s[j, i, pl.ds(at, GROUP), :]


def mix(order, short_kernel, long_kernel, g, proj_sets):
    blocks, channels, _ = g.shape
    count, sets = len(proj_sets[0]), len(proj_sets)
    groups = channels // GROUP
    per_step = 2 if groups % 2 == 0 else 1
    steps = groups // per_step
    rows = blocks * GROUP
    high = per_step * GROUP
    proj_specs = [pl.BlockSpec((3, high, x.shape[2]), lambda i, o: (0, i, 0)) for x in proj_sets[0]]
    token_spec = pl.BlockSpec((blocks, high, LONG), lambda i, o: (0, i, 0))
    outs = pl.pallas_call(
        functools.partial(mix_body, count, sets, per_step),
        grid_spec=pltpu.PrefetchScalarGridSpec(
            num_scalar_prefetch=1,
            grid=(steps,),
            in_specs=[
                pl.BlockSpec(memory_space=pltpu.SMEM),
                pl.BlockSpec((1, per_step, LONG), lambda i, o: (i, 0, 0)),
                token_spec,
            ]
            + proj_specs * sets,
            out_specs=[token_spec]
            + proj_specs
            + [
                pl.BlockSpec((1, per_step, 3 * SHORT, LONG), lambda i, o: (i, 0, 0, 0)),
                pl.BlockSpec((1, per_step, LONG), lambda i, o: (i, 0, 0)),
            ],
            scratch_shapes=[
                pltpu.VMEM((per_step, 3, rows + GROUP, LONG), F32),
                pltpu.VMEM((per_step, rows + GROUP, LONG), BF16),
                pltpu.VMEM((per_step, rows + GROUP, LONG), BF16),
                pltpu.VMEM((per_step, 3, rows + GROUP, LONG), F32),
                pltpu.VMEM((per_step, 3, rows, LONG), BF16),
            ],
        ),
        out_shape=[jax.ShapeDtypeStruct((blocks, channels, LONG), BF16)]
        + [jax.ShapeDtypeStruct(x.shape, BF16) for x in proj_sets[0]]
        + [
            jax.ShapeDtypeStruct((steps, per_step, 3 * SHORT, LONG), F32),
            jax.ShapeDtypeStruct((steps, per_step, LONG), F32),
        ],
        compiler_params=pltpu.CompilerParams(vmem_limit_bytes=VMEM),
        cost_estimate=pl.CostEstimate(
            flops=5 * 2 * channels * blocks * LONG * LONG * 10,
            bytes_accessed=channels * blocks * LONG * 2 * (3 * sets + 5),
            transcendentals=0,
        ),
    )(order, short_kernel, long_kernel.reshape(steps, per_step, LONG), g, *[x for s in proj_sets for x in s])
    mixed, d_proj, gs, gl = outs[0], outs[1 : 1 + count], outs[1 + count], outs[2 + count]
    grad_short = jnp.sum(gs, axis=-1).reshape(groups, 3, SHORT).transpose(1, 0, 2)
    return mixed, d_proj, grad_short, gl.reshape(groups, LONG)


def restack_body(t_ref, *refs):
    w_refs, out_ref, sems = refs[:3], refs[3], refs[4]
    channels = w_refs[0].shape[1]
    copies = []
    for side in range(2):
        block = t_ref[0] if side == 0 else 1 - t_ref[0]
        for i in range(3):
            at = 3 * side + i
            rows = pl.ds(at * channels, channels)
            copies.append(pltpu.make_async_copy(w_refs[i].at[block], out_ref.at[rows], sems.at[at]))
    for copy in copies:
        copy.start()
    for copy in copies:
        copy.wait()


def restack(t, weights):
    _, channels, width = weights[0].shape
    return pl.pallas_call(
        restack_body,
        in_specs=[pl.BlockSpec(memory_space=pltpu.SMEM)] + [pl.BlockSpec(memory_space=pl.ANY)] * 3,
        out_specs=pl.BlockSpec(memory_space=pl.ANY),
        out_shape=jax.ShapeDtypeStruct((6 * channels, width), BF16),
        scratch_shapes=[pltpu.SemaphoreType.DMA((6,))],
        compiler_params=pltpu.CompilerParams(vmem_limit_bytes=VMEM),
        cost_estimate=pl.CostEstimate(flops=0, bytes_accessed=24 * channels * width, transcendentals=0),
    )(t.reshape(1), *weights)


def project_body(pieces, extras, *refs):
    x_refs, w_ref = refs[:pieces], refs[pieces]
    far_ref, near_ref, x_s, sems = refs[pieces + 1 + extras :]
    step, steps = pl.program_id(0), pl.num_programs(0)

    @pl.when(step == 0)
    def _():
        copies, at = [], 0
        for n, x in enumerate(x_refs):
            copies.append(pltpu.make_async_copy(x, x_s.at[pl.ds(at, x.shape[0])], sems.at[n]))
            at += x.shape[0]
        for copy in copies:
            copy.start()
        for copy in copies:
            copy.wait()

    got = dot(w_ref[...], x_s[...], ((1,), (1,))).astype(BF16)

    @pl.when(step < steps // 2)
    def _():
        far_ref[...] = got

    @pl.when(step >= steps // 2)
    def _():
        near_ref[...] = got


def project_kernel(flat, pieces, extras):
    rows, width = flat.shape
    tokens = sum(x.shape[0] for x in pieces)
    tile = rows // 4
    half = jax.ShapeDtypeStruct((rows // 2, tokens), BF16)
    return pl.pallas_call(
        functools.partial(project_body, len(pieces), len(extras)),
        grid=(4,),
        in_specs=[pl.BlockSpec(memory_space=pl.ANY)] * len(pieces)
        + [pl.BlockSpec((tile, width), lambda i: ((i + 2) % 4, 0))]
        + [pl.BlockSpec(memory_space=pl.ANY)] * len(extras),
        out_specs=[
            pl.BlockSpec((tile, tokens), lambda i: (jnp.minimum(i, 1), 0)),
            pl.BlockSpec((tile, tokens), lambda i: (jnp.maximum(i - 2, 0), 0)),
        ],
        out_shape=[half, half],
        scratch_shapes=[pltpu.VMEM((tokens, width), BF16), pltpu.SemaphoreType.DMA((len(pieces),))],
        compiler_params=pltpu.CompilerParams(vmem_limit_bytes=VMEM_DOT),
        cost_estimate=pl.CostEstimate(
            flops=2 * rows * width * tokens,
            bytes_accessed=2 * (rows * width + tokens * width + rows * tokens),
            transcendentals=0,
        ),
    )(*pieces, flat, *extras)


def unproject_body(extras, near_ref, far_ref, w_ref, *refs):
    keep_ref, give_ref, d_s = refs[extras:]
    stay = near_ref.shape[0]

    @pl.when(pl.program_id(0) == 0)
    def _():
        d_s[:, 0:stay] = near_ref[...].T
        d_s[:, stay:] = far_ref[...].T

    got = dot(d_s[...], w_ref[...], ((1,), (0,)))
    half = got.shape[0] // 2
    keep_ref[...] = got[:half].astype(BF16)
    give_ref[...] = got[half:].astype(BF16)


def unproject_kernel(flat, near, far, extras):
    rows, width = flat.shape
    tokens = near.shape[1]
    tile = min(512, width)
    half = jax.ShapeDtypeStruct((tokens // 2, width), BF16)
    return pl.pallas_call(
        functools.partial(unproject_body, len(extras)),
        grid=(width // tile,),
        in_specs=[
            pl.BlockSpec((rows // 2, tokens), lambda i: (0, 0)),
            pl.BlockSpec((rows // 2, tokens), lambda i: (0, 0)),
            pl.BlockSpec((rows, tile), lambda i: (0, i)),
        ]
        + [pl.BlockSpec(memory_space=pl.ANY)] * len(extras),
        out_specs=[pl.BlockSpec((tokens // 2, tile), lambda i: (0, i))] * 2,
        out_shape=[half, half],
        scratch_shapes=[pltpu.VMEM((tokens, rows), BF16)],
        compiler_params=pltpu.CompilerParams(vmem_limit_bytes=VMEM_DOT),
        cost_estimate=pl.CostEstimate(
            flops=2 * rows * width * tokens,
            bytes_accessed=2 * (rows * width + tokens * width + rows * tokens),
            transcendentals=0,
        ),
    )(near, far, flat, *extras)


def on_device(ring, n_tp, tokens_in, w_query, w_key, w_value, short_taps, long_taps, grad_out):
    chips = len(ring)
    half = chips // 2
    n_ctx = 2 * chips
    held, width = tokens_in.shape
    channels = w_query.shape[1]
    weights = (w_query, w_key, w_value)

    def pairs(hop):
        return [(2 * ring[j] + k, 2 * ring[(j + hop) % chips] + k) for j in range(chips) for k in range(2)]

    ahead, behind = pairs(1), pairs(-1)
    mates = [(d, d ^ 1) for d in range(n_ctx)]

    def onward(x):
        return lax.ppermute(x, "ctx", ahead)

    def back(x):
        return lax.ppermute(x, "ctx", behind)

    def swap(x):
        return lax.ppermute(x, "ctx", mates)

    def across(x):
        return lax.ppermute(x, "tp", [(0, 1), (1, 0)])

    me = lax.axis_index("ctx")
    place_of = np.argsort(np.array(ring))
    place = jnp.asarray(place_of, jnp.int32)[me // 2]

    def block_at(hop, other):
        chip = jnp.asarray(ring, jnp.int32)[(place + hop + chips) % chips]
        return 2 * chip + (me % 2 + other) % 2

    lists = [[(0, 0), (0, 1)]]
    lists += [[(-s, 0), (s, 0), (-s, 1), (s, 1)] for s in range(1, half)]
    lists += [[(half, 0), (half, 1)]]
    order = jnp.stack([block_at(*item) for chunk in lists for item in chunk]).astype(jnp.int32)

    stay = 3 * channels
    if n_tp == 2:
        flat = restack(lax.axis_index("tp").astype(jnp.int32), weights)
    else:
        flat = jnp.stack(weights).reshape(-1, width)

    def project(pieces, *extras):
        if n_tp == 2:
            far, near = project_kernel(flat, pieces, extras)
            return [y.reshape(3, channels, -1) for y in (near, across(far))]
        y = dot(flat, jnp.concatenate(pieces, axis=0), ((1,), (1,))).astype(BF16).reshape(3, n_tp, channels, -1)
        return [lax.psum_scatter(y, "tp", scatter_dimension=1, tiled=True).reshape(3, channels, -1)]

    def unproject(d, *extras):
        if n_tp == 2:
            return unproject_kernel(flat, *d, extras)
        y = dot(d[0], flat, ((0,), (0,))).astype(BF16)
        return y[: y.shape[0] // 2], y[y.shape[0] // 2 :]

    def meet(d):
        if n_tp == 2:
            d = d.reshape(stay, -1)
            return [d, across(d)]
        d = lax.all_gather(d.reshape(3, 1, channels, -1), "tp", axis=1, tiled=True)
        return [d.reshape(-1, d.shape[-1])]

    incoming = lax.all_to_all(
        grad_out.reshape(n_ctx, channels, held), "ctx", split_axis=0, concat_axis=0, tiled=True
    )

    cut = held // 2
    projected = []
    right, left = onward(tokens_in), back(tokens_in)
    projected.append(project([tokens_in, swap(tokens_in)]))
    for s in range(1, half + 1):
        late = [projected[-1][-1]] if s < half else [projected[-1][0], projected[-2][-1]]
        if s < half:
            right, left, _ = lax.optimization_barrier((right, left, projected[-1][0]))
        if s < half - 1:
            moving = onward(right), back(left)
        elif s < half:
            moving = onward(right[:cut]), back(left[cut:])
        projected.append(project([right, left, swap(right), swap(left)], *late))
        right, left = moving

    mixed, d_proj, grad_short, grad_long = mix(
        order,
        short_taps.reshape(3, -1, SHORT),
        long_taps.reshape(-1, LONG),
        incoming,
        [list(s) for s in zip(*projected)],
    )

    met = {}
    for s in range(half, -1, -1):
        d = d_proj[s]
        if s + 2 in met:
            d, met[s + 2][-1] = lax.optimization_barrier((d, met[s + 2][-1]))
        met[s] = meet(d)
    mixed_out = lax.all_to_all(mixed, "ctx", split_axis=0, concat_axis=0, tiled=True).reshape(-1, held)
    keep, give = unproject(met[half])
    total = (keep.astype(F32) + swap(give).astype(F32)).astype(BF16)
    from_behind = jnp.pad(onward(total[:cut]), ((0, held - cut), (0, 0)))
    from_ahead = jnp.pad(back(total[cut:]), ((cut, 0), (0, 0)))
    before = [keep]
    for s in range(half - 1, 0, -1):
        keep, give = unproject(met[s], *before)
        give = swap(give)
        fro = (keep[:held].astype(F32) + give[:held].astype(F32) + from_ahead.astype(F32)).astype(BF16)
        to = (keep[held:].astype(F32) + give[held:].astype(F32) + from_behind.astype(F32)).astype(BF16)
        from_behind, from_ahead = onward(to), back(fro)
        before = [keep]
    keep, give = unproject(met[0], *before)
    total = keep.astype(F32) + swap(give).astype(F32)
    grad_tokens = (total + from_behind.astype(F32) + from_ahead.astype(F32)).astype(BF16)
    return (
        mixed_out,
        grad_tokens,
        grad_short.reshape(3, 1, -1, SHORT),
        grad_long.reshape(1, -1, LONG),
    )


def solution(mesh):
    placed = (
        P("ctx", "tp"),
        P(None, "ctx", "tp"),
        P(None, "ctx", "tp"),
        P(None, "ctx", "tp"),
        P(None, "tp", "ctx", None),
        P("tp", "ctx", None),
        P("tp", "ctx"),
    )
    return jax.shard_map(
        functools.partial(on_device, ring_of(mesh), mesh.shape["tp"]),
        mesh=mesh,
        in_specs=placed,
        out_specs=(
            P("tp", "ctx"),
            P("ctx", "tp"),
            P(None, "tp", "ctx", None),
            P("tp", "ctx", None),
        ),
        check_vma=False,
    )
```

```python
import functools

import jax
import jax.numpy as jnp
import numpy as np
from jax import lax
from jax.experimental import pallas as pl
from jax.experimental.pallas import tpu as pltpu
from jax.sharding import PartitionSpec as P

GROUP = 16
SHORT = 3
LONG = 128
F32 = jnp.float32
BF16 = jnp.bfloat16
VMEM = 58 * 1024 * 1024
VMEM_DOT = 54 * 1024 * 1024
SMALL = pl.CostEstimate(flops=1, bytes_accessed=1, transcendentals=0)


def ring_of(mesh):
    chips = mesh.shape["ctx"] // 2
    plain = list(range(chips))
    devices = np.asarray(mesh.devices).reshape(mesh.shape["ctx"], -1)[:, 0]
    places = [getattr(devices[2 * chip], "coords", None) for chip in plain]
    if any(place is None for place in places):
        return plain
    places = np.array([list(place)[:3] for place in places])
    axes = [axis for axis in range(3) if len(set(places[:, axis])) > 1]
    if len(axes) != 2:
        return plain
    rung = min(axes, key=lambda axis: len(set(places[:, axis])))
    along = axes[0] if rung == axes[1] else axes[1]
    sides = sorted(set(places[:, rung]))
    if len(sides) != 2:
        return plain
    there = [c for c in plain if places[c, rung] == sides[0]]
    back = [c for c in plain if places[c, rung] == sides[1]]
    there.sort(key=lambda c: places[c, along])
    back.sort(key=lambda c: -places[c, along])
    return there + back


def dot(a, b, dims):
    return lax.dot_general(a, b, (dims, ((), ())), preferred_element_type=F32)


def mix_body(count, sets, per_step, grouped, order, short_ref, long_ref, g_ref, *refs):
    proj_refs = [refs[s * count : (s + 1) * count] for s in range(sets)]
    refs = refs[sets * count :]
    d_count = len(grouped)
    mixed_ref, d_refs, gs_ref, gl_ref = refs[0], refs[1 : 1 + d_count], refs[1 + d_count], refs[2 + d_count]
    p_s, x_s, y_s, d_s, e_s = refs[3 + d_count :]
    blocks = g_ref.shape[0]
    rows = blocks * GROUP
    step = pl.program_id(0)

    @pl.when(step == 0)
    def _():
        p_s[:, :, 0:GROUP, :] = jnp.zeros((per_step, 3, GROUP, LONG), F32)
        x_s[:, 0:GROUP, :] = jnp.zeros((per_step, GROUP, LONG), BF16)
        y_s[:, rows:, :] = jnp.zeros((per_step, GROUP, LONG), BF16)
        d_s[:, :, rows:, :] = jnp.zeros((per_step, 3, GROUP, LONG), F32)

    halves = [(a, h) for a in range(count) for h in range(proj_refs[0][a].shape[2] // LONG)]
    places = [(a, h, where) for where, (a, h) in enumerate(halves)]
    d_places = []
    for b, arrays in enumerate(grouped):
        inside = [where for array in arrays for a, _, where in places if a == array]
        d_places += [(b, h, where) for h, where in enumerate(inside)]
    lane = lax.broadcasted_iota(jnp.int32, (rows, LONG), 1)
    sub8 = lax.broadcasted_iota(jnp.int32, (8, LONG), 0)
    col = lax.broadcasted_iota(jnp.int32, (LONG, LONG), 1)
    row = lax.broadcasted_iota(jnp.int32, (LONG, LONG), 0)

    for j in range(per_step):
        group = step * per_step + j
        mine = slice(j * GROUP, (j + 1) * GROUP)
        for a, h, where in places:
            at = pl.multiple_of((order[where] + 1) * GROUP, GROUP)
            for i in range(3):
                part = proj_refs[0][a][i, mine, h * LONG : (h + 1) * LONG].astype(F32)
                for s in range(1, sets):
                    part = part + proj_refs[s][a][i, mine, h * LONG : (h + 1) * LONG].astype(F32)
                p_s[j, i, pl.ds(at, GROUP), :] = part
        taps = [[short_ref[i, group, k] for k in range(SHORT)] for i in range(3)]
        feats = []
        for i in range(3):
            whole = p_s[j, i]
            one = pltpu.roll(whole, 1, 1)
            two = pltpu.roll(whole, 2, 1)
            one = jnp.where(lane < 1, one[:rows], one[GROUP:])
            two = jnp.where(lane < 2, two[:rows], two[GROUP:])
            feats.append(taps[i][0] * whole[GROUP:] + taps[i][1] * one + taps[i][2] * two)
        fq, fk, fv = feats
        x_s[j, GROUP:, :] = (fk * fv).astype(BF16)

        base = jnp.broadcast_to(long_ref[0, j : j + 1, :], (8, LONG))
        for bit in (1, 2, 4):
            base = jnp.where((sub8 & bit) != 0, pltpu.roll(base, bit, 1), base)
        full = jnp.concatenate([base] + [pltpu.roll(base, 8 * m, 1) for m in range(1, LONG // 8)], axis=0)
        near = jnp.where(col >= row, full, 0.0).astype(BF16)
        far = jnp.where(col < row, full, 0.0).astype(BF16)

        x_two = jnp.concatenate([x_s[j, GROUP:, :], x_s[j, :rows, :]], axis=1)
        inner = dot(x_two, jnp.concatenate([near, far], axis=0), ((1,), (0,)))
        g = g_ref[:, mine, :].reshape(rows, LONG).astype(F32)
        mixed_ref[:, mine, :] = (fq * inner).astype(BF16).reshape(blocks, GROUP, LONG)
        y_s[j, :rows, :] = (g * fq).astype(BF16)
        y_one = y_s[j, :rows, :]
        y_two = jnp.concatenate([y_one, y_s[j, GROUP:, :]], axis=1)
        d_product = dot(y_two, jnp.concatenate([near, far], axis=1), ((1,), (1,)))

        pairs = dot(x_two, y_one, ((0,), (0,)))
        fold = jnp.where(col >= row, pairs[:LONG], pairs[LONG:])
        width = LONG
        while width > 8:
            width //= 2
            fold = fold[:width] + pltpu.roll(fold[width:], LONG - width, 1)
        for bit in (4, 2, 1):
            fold = jnp.where((sub8 & bit) != 0, pltpu.roll(fold, LONG - bit, 1), fold)
        gl_ref[0, j : j + 1, :] = jnp.sum(fold, axis=0, keepdims=True)

        for i, d in enumerate((g * inner, d_product * fv, d_product * fk)):
            d_s[j, i, :rows, :] = d
            whole = d_s[j, i]
            one = pltpu.roll(whole, LONG - 1, 1)
            two = pltpu.roll(whole, LONG - 2, 1)
            one = jnp.where(lane >= LONG - 1, one[GROUP:], one[:rows])
            two = jnp.where(lane >= LONG - 2, two[GROUP:], two[:rows])
            p = p_s[j, i, GROUP:, :]
            for k, moved in enumerate((d, one, two)):
                gs_ref[0, j, 3 * i + k : 3 * i + k + 1, :] = jnp.sum(p * moved, axis=0, keepdims=True)
            e_s[j, i] = (taps[i][0] * d + taps[i][1] * one + taps[i][2] * two).astype(BF16)
        for a, h, where in d_places:
            at = pl.multiple_of(order[where] * GROUP, GROUP)
            for i in range(3):
                d_refs[a][i, mine, h * LONG : (h + 1) * LONG] = e_s[j, i, pl.ds(at, GROUP), :]


def mix(order, short_kernel, long_kernel, g, proj_sets, grouped):
    blocks, channels, _ = g.shape
    count, sets = len(proj_sets[0]), len(proj_sets)
    groups = channels // GROUP
    per_step = 2 if groups % 2 == 0 else 1
    steps = groups // per_step
    rows = blocks * GROUP
    high = per_step * GROUP
    proj_specs = [pl.BlockSpec((3, high, x.shape[2]), lambda i, o: (0, i, 0)) for x in proj_sets[0]]
    d_widths = [sum(proj_sets[0][a].shape[2] for a in arrays) for arrays in grouped]
    d_specs = [pl.BlockSpec((3, high, w), lambda i, o: (0, i, 0)) for w in d_widths]
    token_spec = pl.BlockSpec((blocks, high, LONG), lambda i, o: (0, i, 0))
    outs = pl.pallas_call(
        functools.partial(mix_body, count, sets, per_step, grouped),
        grid_spec=pltpu.PrefetchScalarGridSpec(
            num_scalar_prefetch=1,
            grid=(steps,),
            in_specs=[
                pl.BlockSpec(memory_space=pltpu.SMEM),
                pl.BlockSpec((1, per_step, LONG), lambda i, o: (i, 0, 0)),
                token_spec,
            ]
            + proj_specs * sets,
            out_specs=[token_spec]
            + d_specs
            + [
                pl.BlockSpec((1, per_step, 3 * SHORT, LONG), lambda i, o: (i, 0, 0, 0)),
                pl.BlockSpec((1, per_step, LONG), lambda i, o: (i, 0, 0)),
            ],
            scratch_shapes=[
                pltpu.VMEM((per_step, 3, rows + GROUP, LONG), F32),
                pltpu.VMEM((per_step, rows + GROUP, LONG), BF16),
                pltpu.VMEM((per_step, rows + GROUP, LONG), BF16),
                pltpu.VMEM((per_step, 3, rows + GROUP, LONG), F32),
                pltpu.VMEM((per_step, 3, rows, LONG), BF16),
            ],
        ),
        out_shape=[jax.ShapeDtypeStruct((blocks, channels, LONG), BF16)]
        + [jax.ShapeDtypeStruct((3, channels, w), BF16) for w in d_widths]
        + [
            jax.ShapeDtypeStruct((steps, per_step, 3 * SHORT, LONG), F32),
            jax.ShapeDtypeStruct((steps, per_step, LONG), F32),
        ],
        compiler_params=pltpu.CompilerParams(vmem_limit_bytes=VMEM),
        cost_estimate=SMALL,
    )(order, short_kernel, long_kernel.reshape(steps, per_step, LONG), g, *[x for s in proj_sets for x in s])
    mixed, d_proj, (gs, gl) = outs[0], outs[1:-2], outs[-2:]
    grad_short = jnp.sum(gs, axis=-1).reshape(groups, 3, SHORT).transpose(1, 0, 2)
    return mixed, d_proj, grad_short, gl.reshape(groups, LONG)


def restack_body(t_ref, *refs):
    out_ref = refs[3]
    for i in range(3):
        out_ref[0, i] = refs[i][0]


def restack(t, weights):
    _, channels, width = weights[0].shape
    tile = min(128, channels)

    def source(side, part, t):
        return (jnp.where(side == 0, t[0], 1 - t[0]), part, 0)

    return pl.pallas_call(
        restack_body,
        grid_spec=pltpu.PrefetchScalarGridSpec(
            num_scalar_prefetch=1,
            grid=(2, channels // tile),
            in_specs=[pl.BlockSpec((1, tile, width), source)] * 3,
            out_specs=pl.BlockSpec((1, 3, tile, width), lambda side, part, t: (side, 0, part, 0)),
        ),
        out_shape=jax.ShapeDtypeStruct((2, 3, channels, width), BF16),
        compiler_params=pltpu.CompilerParams(vmem_limit_bytes=VMEM_DOT),
        cost_estimate=SMALL,
    )(t.reshape(1), *weights).reshape(6 * channels, width)


def project_body(pieces, *refs):
    x_refs, w_ref = refs[:pieces], refs[pieces]
    far_ref, near_ref, x_s, sems = refs[pieces + 1 :]
    step, steps = pl.program_id(0), pl.num_programs(0)

    @pl.when(step == 0)
    def _():
        copies, at = [], 0
        for n, x in enumerate(x_refs):
            copies.append(pltpu.make_async_copy(x, x_s.at[pl.ds(at, x.shape[0])], sems.at[n]))
            at += x.shape[0]
        for copy in copies:
            copy.start()
        for copy in copies:
            copy.wait()

    got = dot(w_ref[...], x_s[...], ((1,), (1,))).astype(BF16)

    @pl.when(step < steps // 2)
    def _():
        far_ref[...] = got

    @pl.when(step >= steps // 2)
    def _():
        near_ref[...] = got


def project_kernel(flat, pieces):
    rows, width = flat.shape
    tokens = sum(x.shape[0] for x in pieces)
    tile = rows // 4
    half = jax.ShapeDtypeStruct((rows // 2, tokens), BF16)
    far, near = pl.pallas_call(
        functools.partial(project_body, len(pieces)),
        grid=(4,),
        in_specs=[pl.BlockSpec(memory_space=pl.ANY)] * len(pieces)
        + [pl.BlockSpec((tile, width), lambda i: ((i + 2) % 4, 0))],
        out_specs=[
            pl.BlockSpec((tile, tokens), lambda i: (jnp.minimum(i, 1), 0)),
            pl.BlockSpec((tile, tokens), lambda i: (jnp.maximum(i - 2, 0), 0)),
        ],
        out_shape=[half, half],
        scratch_shapes=[pltpu.VMEM((tokens, width), BF16), pltpu.SemaphoreType.DMA((len(pieces),))],
        compiler_params=pltpu.CompilerParams(vmem_limit_bytes=VMEM_DOT),
        cost_estimate=SMALL,
    )(*pieces, flat)
    return near, far


def unproject_body(near_ref, far_ref, w_ref, keep_ref, give_ref, d_s):
    stay = near_ref.shape[0]

    @pl.when(pl.program_id(0) == 0)
    def _():
        d_s[:, 0:stay] = near_ref[...].T
        d_s[:, stay:] = far_ref[...].T

    got = dot(d_s[...], w_ref[...], ((1,), (0,)))
    half = got.shape[0] // 2
    keep_ref[...] = got[:half].astype(BF16)
    give_ref[...] = got[half:].astype(BF16)


def unproject_kernel(flat, near, far):
    rows, width = flat.shape
    tokens = near.shape[1]
    tile = min(512, width)
    half = jax.ShapeDtypeStruct((tokens // 2, width), BF16)
    return pl.pallas_call(
        unproject_body,
        grid=(width // tile,),
        in_specs=[
            pl.BlockSpec((rows // 2, tokens), lambda i: (0, 0)),
            pl.BlockSpec((rows // 2, tokens), lambda i: (0, 0)),
            pl.BlockSpec((rows, tile), lambda i: (0, i)),
        ],
        out_specs=[pl.BlockSpec((tokens // 2, tile), lambda i: (0, i))] * 2,
        out_shape=[half, half],
        scratch_shapes=[pltpu.VMEM((tokens, rows), BF16)],
        compiler_params=pltpu.CompilerParams(vmem_limit_bytes=VMEM_DOT),
        cost_estimate=SMALL,
    )(near, far, flat)


def on_device(ring, n_tp, tokens_in, w_query, w_key, w_value, short_taps, long_taps, grad_out):
    chips = len(ring)
    half = chips // 2
    n_ctx = 2 * chips
    held, width = tokens_in.shape
    channels = w_query.shape[1]
    weights = (w_query, w_key, w_value)

    def pairs(hop):
        return [(2 * ring[j] + k, 2 * ring[(j + hop) % chips] + k) for j in range(chips) for k in range(2)]

    ahead, behind = pairs(1), pairs(-1)
    mates = [(d, d ^ 1) for d in range(n_ctx)]

    def onward(x):
        return lax.ppermute(x, "ctx", ahead)

    def back(x):
        return lax.ppermute(x, "ctx", behind)

    def swap(x):
        return lax.ppermute(x, "ctx", mates)

    me = lax.axis_index("ctx")
    place_of = np.argsort(np.array(ring))
    place = jnp.asarray(place_of, jnp.int32)[me // 2]

    def block_at(hop, other):
        chip = jnp.asarray(ring, jnp.int32)[(place + hop + chips) % chips]
        return 2 * chip + (me % 2 + other) % 2

    lists = [[(0, 0), (0, 1)]]
    lists += [[(-s, 0), (s, 0), (-s, 1), (s, 1)] for s in range(1, half)]
    lists += [[(half, 0), (half, 1)]]
    order = jnp.stack([block_at(*item) for chunk in lists for item in chunk]).astype(jnp.int32)

    stay = 3 * channels
    if n_tp == 2:
        flat = restack(lax.axis_index("tp").astype(jnp.int32), weights)
    else:
        flat = jnp.stack(weights).reshape(-1, width)

    def project(pieces):
        if n_tp == 2:
            return project_kernel(flat, pieces)
        y = dot(flat, jnp.concatenate(pieces, axis=0), ((1,), (1,))).astype(BF16).reshape(3, n_tp, channels, -1)
        return lax.psum_scatter(y, "tp", scatter_dimension=1, tiled=True).reshape(stay, -1), None

    def across(x):
        return None if x is None else lax.ppermute(x, "tp", [(0, 1), (1, 0)])

    def meet(d):
        if n_tp == 2:
            return d.reshape(stay, -1), across(d.reshape(stay, -1))
        d = lax.all_gather(d.reshape(3, 1, channels, -1), "tp", axis=1, tiled=True)
        return (d.reshape(-1, d.shape[-1]),)

    def unproject(d):
        if n_tp == 2:
            return unproject_kernel(flat, *d)
        y = dot(d[0], flat, ((0,), (0,))).astype(BF16)
        return y[: y.shape[0] // 2], y[y.shape[0] // 2 :]

    stage = lax.optimization_barrier

    cut = held // 2
    right, left = onward(tokens_in), back(tokens_in)
    near, far = project([tokens_in, swap(tokens_in)])
    right, left, near, far = stage((right, left, near, far))
    projected = []
    for s in range(1, half):
        if s == half - 1:
            ahead_x, behind_x = onward(right[:cut]), back(left[cut:])
            right, left, grad_out = stage((right, left, grad_out))
            incoming = lax.all_to_all(
                grad_out.reshape(n_ctx, channels, held), "ctx", split_axis=0, concat_axis=0, tiled=True
            )
        else:
            ahead_x, behind_x = onward(right), back(left)
        projected.append((near, across(far)))
        near, far = project([right, left, swap(right), swap(left)])
        right, left, near, far, projected[-1] = stage((ahead_x, behind_x, near, far, projected[-1]))
    projected.append((near, across(far)))
    near, far = project([right, left, swap(right), swap(left)])
    near, far, projected[-1], incoming = stage((near, far, projected[-1], incoming))
    projected.append((near, across(far)))

    mixed, d_proj, grad_short, grad_long = mix(
        order,
        short_taps.reshape(3, -1, SHORT),
        long_taps.reshape(-1, LONG),
        incoming,
        [[y.reshape(3, channels, -1) for y in side] for side in zip(*projected) if side[0] is not None],
        [[s] for s in range(half + 1)],
    )

    def add(*parts):
        return functools.reduce(lambda a, b: a + b, [part.astype(F32) for part in parts]).astype(BF16)

    mixed_out = lax.all_to_all(mixed, "ctx", split_axis=0, concat_axis=0, tiled=True).reshape(-1, held)
    met, rest = stage((meet(d_proj[half]), d_proj[:half]))
    keep, give = unproject(met)
    total = add(keep, swap(give))
    total, met, rest = stage((total, meet(rest[-1]), rest[:-1]))
    from_behind = jnp.pad(onward(total[:cut]), ((0, held - cut), (0, 0)))
    from_ahead = jnp.pad(back(total[cut:]), ((cut, 0), (0, 0)))
    for s in range(half - 1, 0, -1):
        later = meet(rest[-1])
        keep, give = unproject(met)
        give = swap(give)
        fro, to = add(keep[:held], give[:held], from_ahead), add(keep[held:], give[held:], from_behind)
        fro, to, met, rest, mixed_out = stage((fro, to, later, rest[:-1], mixed_out))
        from_behind, from_ahead = onward(to), back(fro)
    keep, give = unproject(met)
    grad_tokens = add(keep, swap(give), from_behind, from_ahead)
    return (
        mixed_out,
        grad_tokens,
        grad_short.reshape(3, 1, -1, SHORT),
        grad_long.reshape(1, -1, LONG),
    )


def solution(mesh):
    placed = (
        P("ctx", "tp"),
        P(None, "ctx", "tp"),
        P(None, "ctx", "tp"),
        P(None, "ctx", "tp"),
        P(None, "tp", "ctx", None),
        P("tp", "ctx", None),
        P("tp", "ctx"),
    )
    return jax.shard_map(
        functools.partial(on_device, ring_of(mesh), mesh.shape["tp"]),
        mesh=mesh,
        in_specs=placed,
        out_specs=(
            P("tp", "ctx"),
            P("ctx", "tp"),
            P(None, "tp", "ctx", None),
            P("tp", "ctx", None),
        ),
        check_vma=False,
    )
```

```python
import functools

import jax
import jax.numpy as jnp
import numpy as np
from jax import lax
from jax.experimental import pallas as pl
from jax.experimental.pallas import tpu as pltpu
from jax.sharding import PartitionSpec as P

GROUP = 16
SHORT = 3
LONG = 128
F32 = jnp.float32
BF16 = jnp.bfloat16
VMEM = 44 * 1024 * 1024
VMEM_DOT = 20 * 1024 * 1024
SMALL = pl.CostEstimate(flops=1, bytes_accessed=1, transcendentals=0)


def ring_of(mesh):
    chips = mesh.shape["ctx"] // 2
    plain = list(range(chips))
    devices = np.asarray(mesh.devices).reshape(mesh.shape["ctx"], -1)[:, 0]
    places = [getattr(devices[2 * chip], "coords", None) for chip in plain]
    if any(place is None for place in places):
        return plain
    places = np.array([list(place)[:3] for place in places])
    axes = [axis for axis in range(3) if len(set(places[:, axis])) > 1]
    if len(axes) != 2:
        return plain
    rung = min(axes, key=lambda axis: len(set(places[:, axis])))
    along = axes[0] if rung == axes[1] else axes[1]
    sides = sorted(set(places[:, rung]))
    if len(sides) != 2:
        return plain
    there = [c for c in plain if places[c, rung] == sides[0]]
    back = [c for c in plain if places[c, rung] == sides[1]]
    there.sort(key=lambda c: places[c, along])
    back.sort(key=lambda c: -places[c, along])
    return there + back


def dot(a, b, dims):
    return lax.dot_general(a, b, (dims, ((), ())), preferred_element_type=F32)


def mix_body(count, sets, per_step, grouped, order, short_ref, long_ref, g_ref, *refs):
    proj_refs = [refs[s * count : (s + 1) * count] for s in range(sets)]
    refs = refs[sets * count :]
    d_count = len(grouped)
    mixed_ref, d_refs, gs_ref, gl_ref = refs[0], refs[1 : 1 + d_count], refs[1 + d_count], refs[2 + d_count]
    p_s, x_s, y_s, d_s, e_s = refs[3 + d_count :]
    blocks = g_ref.shape[0]
    rows = blocks * GROUP
    step = pl.program_id(0)

    @pl.when(step == 0)
    def _():
        p_s[:, :, 0:GROUP, :] = jnp.zeros((per_step, 3, GROUP, LONG), F32)
        x_s[:, 0:GROUP, :] = jnp.zeros((per_step, GROUP, LONG), BF16)
        y_s[:, rows:, :] = jnp.zeros((per_step, GROUP, LONG), BF16)
        d_s[:, :, rows:, :] = jnp.zeros((per_step, 3, GROUP, LONG), F32)

    halves = [(a, h) for a in range(count) for h in range(proj_refs[0][a].shape[2] // LONG)]
    places = [(a, h, where) for where, (a, h) in enumerate(halves)]
    d_places = []
    for b, arrays in enumerate(grouped):
        inside = [where for array in arrays for a, _, where in places if a == array]
        d_places += [(b, h, where) for h, where in enumerate(inside)]
    lane = lax.broadcasted_iota(jnp.int32, (rows, LONG), 1)
    sub8 = lax.broadcasted_iota(jnp.int32, (8, LONG), 0)
    col = lax.broadcasted_iota(jnp.int32, (LONG, LONG), 1)
    row = lax.broadcasted_iota(jnp.int32, (LONG, LONG), 0)

    for j in range(per_step):
        group = step * per_step + j
        mine = slice(j * GROUP, (j + 1) * GROUP)
        for a, h, where in places:
            at = pl.multiple_of((order[where] + 1) * GROUP, GROUP)
            for i in range(3):
                part = proj_refs[0][a][i, mine, h * LONG : (h + 1) * LONG].astype(F32)
                for s in range(1, sets):
                    part = part + proj_refs[s][a][i, mine, h * LONG : (h + 1) * LONG].astype(F32)
                p_s[j, i, pl.ds(at, GROUP), :] = part
        taps = [[short_ref[i, group, k] for k in range(SHORT)] for i in range(3)]
        feats = []
        for i in range(3):
            whole = p_s[j, i]
            one = pltpu.roll(whole, 1, 1)
            two = pltpu.roll(whole, 2, 1)
            one = jnp.where(lane < 1, one[:rows], one[GROUP:])
            two = jnp.where(lane < 2, two[:rows], two[GROUP:])
            feats.append(taps[i][0] * whole[GROUP:] + taps[i][1] * one + taps[i][2] * two)
        fq, fk, fv = feats
        x_s[j, GROUP:, :] = (fk * fv).astype(BF16)

        base = jnp.broadcast_to(long_ref[0, j : j + 1, :], (8, LONG))
        for bit in (1, 2, 4):
            base = jnp.where((sub8 & bit) != 0, pltpu.roll(base, bit, 1), base)
        full = jnp.concatenate([base] + [pltpu.roll(base, 8 * m, 1) for m in range(1, LONG // 8)], axis=0)
        near = jnp.where(col >= row, full, 0.0).astype(BF16)
        far = jnp.where(col < row, full, 0.0).astype(BF16)

        x_two = jnp.concatenate([x_s[j, GROUP:, :], x_s[j, :rows, :]], axis=1)
        inner = dot(x_two, jnp.concatenate([near, far], axis=0), ((1,), (0,)))
        g = g_ref[:, mine, :].reshape(rows, LONG).astype(F32)
        mixed_ref[:, mine, :] = (fq * inner).astype(BF16).reshape(blocks, GROUP, LONG)
        y_s[j, :rows, :] = (g * fq).astype(BF16)
        y_one = y_s[j, :rows, :]
        y_two = jnp.concatenate([y_one, y_s[j, GROUP:, :]], axis=1)
        d_product = dot(y_two, jnp.concatenate([near, far], axis=1), ((1,), (1,)))

        pairs = dot(x_two, y_one, ((0,), (0,)))
        fold = jnp.where(col >= row, pairs[:LONG], pairs[LONG:])
        width = LONG
        while width > 8:
            width //= 2
            fold = fold[:width] + pltpu.roll(fold[width:], LONG - width, 1)
        for bit in (4, 2, 1):
            fold = jnp.where((sub8 & bit) != 0, pltpu.roll(fold, LONG - bit, 1), fold)
        gl_ref[0, j : j + 1, :] = jnp.sum(fold, axis=0, keepdims=True)

        for i, d in enumerate((g * inner, d_product * fv, d_product * fk)):
            d_s[j, i, :rows, :] = d
            whole = d_s[j, i]
            one = pltpu.roll(whole, LONG - 1, 1)
            two = pltpu.roll(whole, LONG - 2, 1)
            one = jnp.where(lane >= LONG - 1, one[GROUP:], one[:rows])
            two = jnp.where(lane >= LONG - 2, two[GROUP:], two[:rows])
            p = p_s[j, i, GROUP:, :]
            for k, moved in enumerate((d, one, two)):
                gs_ref[0, j, 3 * i + k : 3 * i + k + 1, :] = jnp.sum(p * moved, axis=0, keepdims=True)
            e_s[j, i] = (taps[i][0] * d + taps[i][1] * one + taps[i][2] * two).astype(BF16)
        for a, h, where in d_places:
            at = pl.multiple_of(order[where] * GROUP, GROUP)
            for i in range(3):
                d_refs[a][i, mine, h * LONG : (h + 1) * LONG] = e_s[j, i, pl.ds(at, GROUP), :]


def mix(order, short_kernel, long_kernel, g, proj_sets, grouped):
    blocks, channels, _ = g.shape
    count, sets = len(proj_sets[0]), len(proj_sets)
    groups = channels // GROUP
    per_step = 2 if groups % 2 == 0 else 1
    steps = groups // per_step
    rows = blocks * GROUP
    high = per_step * GROUP
    proj_specs = [pl.BlockSpec((3, high, x.shape[2]), lambda i, o: (0, i, 0)) for x in proj_sets[0]]
    d_widths = [sum(proj_sets[0][a].shape[2] for a in arrays) for arrays in grouped]
    d_specs = [pl.BlockSpec((3, high, w), lambda i, o: (0, i, 0)) for w in d_widths]
    token_spec = pl.BlockSpec((blocks, high, LONG), lambda i, o: (0, i, 0))
    outs = pl.pallas_call(
        functools.partial(mix_body, count, sets, per_step, grouped),
        grid_spec=pltpu.PrefetchScalarGridSpec(
            num_scalar_prefetch=1,
            grid=(steps,),
            in_specs=[
                pl.BlockSpec(memory_space=pltpu.SMEM),
                pl.BlockSpec((1, per_step, LONG), lambda i, o: (i, 0, 0)),
                token_spec,
            ]
            + proj_specs * sets,
            out_specs=[token_spec]
            + d_specs
            + [
                pl.BlockSpec((1, per_step, 3 * SHORT, LONG), lambda i, o: (i, 0, 0, 0)),
                pl.BlockSpec((1, per_step, LONG), lambda i, o: (i, 0, 0)),
            ],
            scratch_shapes=[
                pltpu.VMEM((per_step, 3, rows + GROUP, LONG), F32),
                pltpu.VMEM((per_step, rows + GROUP, LONG), BF16),
                pltpu.VMEM((per_step, rows + GROUP, LONG), BF16),
                pltpu.VMEM((per_step, 3, rows + GROUP, LONG), F32),
                pltpu.VMEM((per_step, 3, rows, LONG), BF16),
            ],
        ),
        out_shape=[jax.ShapeDtypeStruct((blocks, channels, LONG), BF16)]
        + [jax.ShapeDtypeStruct((3, channels, w), BF16) for w in d_widths]
        + [
            jax.ShapeDtypeStruct((steps, per_step, 3 * SHORT, LONG), F32),
            jax.ShapeDtypeStruct((steps, per_step, LONG), F32),
        ],
        compiler_params=pltpu.CompilerParams(vmem_limit_bytes=VMEM),
        cost_estimate=SMALL,
    )(order, short_kernel, long_kernel.reshape(steps, per_step, LONG), g, *[x for s in proj_sets for x in s])
    mixed, d_proj, (gs, gl) = outs[0], outs[1:-2], outs[-2:]
    grad_short = jnp.sum(gs, axis=-1).reshape(groups, 3, SHORT).transpose(1, 0, 2)
    return mixed, d_proj, grad_short, gl.reshape(groups, LONG)


def restack_body(t_ref, *refs):
    out_ref = refs[3]
    for i in range(3):
        out_ref[0, i] = refs[i][0]


def restack(t, weights):
    _, channels, width = weights[0].shape
    tile = min(128, channels)

    def source(side, part, t):
        return (jnp.where(side == 0, t[0], 1 - t[0]), part, 0)

    return pl.pallas_call(
        restack_body,
        grid_spec=pltpu.PrefetchScalarGridSpec(
            num_scalar_prefetch=1,
            grid=(2, channels // tile),
            in_specs=[pl.BlockSpec((1, tile, width), source)] * 3,
            out_specs=pl.BlockSpec((1, 3, tile, width), lambda side, part, t: (side, 0, part, 0)),
        ),
        out_shape=jax.ShapeDtypeStruct((2, 3, channels, width), BF16),
        compiler_params=pltpu.CompilerParams(vmem_limit_bytes=VMEM_DOT),
        cost_estimate=SMALL,
    )(t.reshape(1), *weights).reshape(6 * channels, width)


def project_body(pieces, *refs):
    x_refs, w_ref = refs[:pieces], refs[pieces]
    far_ref, near_ref, x_s, sems = refs[pieces + 1 :]
    step, steps = pl.program_id(0), pl.num_programs(0)

    @pl.when(step == 0)
    def _():
        copies, at = [], 0
        for n, x in enumerate(x_refs):
            copies.append(pltpu.make_async_copy(x, x_s.at[pl.ds(at, x.shape[0])], sems.at[n]))
            at += x.shape[0]
        for copy in copies:
            copy.start()
        for copy in copies:
            copy.wait()

    got = dot(w_ref[...], x_s[...], ((1,), (1,))).astype(BF16)

    @pl.when(step < steps // 2)
    def _():
        far_ref[...] = got

    @pl.when(step >= steps // 2)
    def _():
        near_ref[...] = got


def project_kernel(flat, pieces):
    rows, width = flat.shape
    tokens = sum(x.shape[0] for x in pieces)
    tile = rows // 4
    half = jax.ShapeDtypeStruct((rows // 2, tokens), BF16)
    far, near = pl.pallas_call(
        functools.partial(project_body, len(pieces)),
        grid=(4,),
        in_specs=[pl.BlockSpec(memory_space=pl.ANY)] * len(pieces)
        + [pl.BlockSpec((tile, width), lambda i: ((i + 2) % 4, 0))],
        out_specs=[
            pl.BlockSpec((tile, tokens), lambda i: (jnp.minimum(i, 1), 0)),
            pl.BlockSpec((tile, tokens), lambda i: (jnp.maximum(i - 2, 0), 0)),
        ],
        out_shape=[half, half],
        scratch_shapes=[pltpu.VMEM((tokens, width), BF16), pltpu.SemaphoreType.DMA((len(pieces),))],
        compiler_params=pltpu.CompilerParams(vmem_limit_bytes=VMEM_DOT),
        cost_estimate=SMALL,
    )(*pieces, flat)
    return near, far


def unproject_body(near_ref, far_ref, w_ref, *refs):
    out_refs, d_s = refs[:-1], refs[-1]
    stay = near_ref.shape[0]

    @pl.when(pl.program_id(0) == 0)
    def _():
        d_s[:, 0:stay] = near_ref[...].T
        d_s[:, stay:] = far_ref[...].T

    got = dot(d_s[...], w_ref[...], ((1,), (0,)))
    at = 0
    for out_ref in out_refs:
        out_ref[...] = got[at : at + out_ref.shape[0]].astype(BF16)
        at += out_ref.shape[0]


def unproject_kernel(flat, near, far, cuts):
    rows, width = flat.shape
    tokens = near.shape[1]
    tile = min(512, width)
    return pl.pallas_call(
        unproject_body,
        grid=(width // tile,),
        in_specs=[
            pl.BlockSpec((rows // 2, tokens), lambda i: (0, 0)),
            pl.BlockSpec((rows // 2, tokens), lambda i: (0, 0)),
            pl.BlockSpec((rows, tile), lambda i: (0, i)),
        ],
        out_specs=[pl.BlockSpec((cut, tile), lambda i: (0, i)) for cut in cuts],
        out_shape=[jax.ShapeDtypeStruct((cut, width), BF16) for cut in cuts],
        scratch_shapes=[pltpu.VMEM((tokens, rows), BF16)],
        compiler_params=pltpu.CompilerParams(vmem_limit_bytes=VMEM_DOT),
        cost_estimate=SMALL,
    )(near, far, flat)


def add_body(heights, *refs):
    out_ref = refs[-1]
    groups, at = [], 0
    for height in heights:
        groups.append(refs[at : at + height])
        at += height
    tops = [[sum(r.shape[0] for r in group[:n]) for n in range(len(group) + 1)] for group in groups]
    edges = sorted({edge for top in tops for edge in top} | {out_ref.shape[0]})
    for low, high in zip(edges[:-1], edges[1:]):
        total = None
        for group, top in zip(groups, tops):
            for n, ref in enumerate(group):
                if top[n] <= low and high <= top[n + 1]:
                    part = ref[low - top[n] : high - top[n], :].astype(F32)
                    total = part if total is None else total + part
        out_ref[low:high, :] = total.astype(BF16)


def add_kernel(*groups):
    rows, width = sum(x.shape[0] for x in groups[0]), groups[0][0].shape[1]
    tile = min(1024, width)
    arrays = [x for group in groups for x in group]
    return pl.pallas_call(
        functools.partial(add_body, [len(group) for group in groups]),
        grid=(width // tile,),
        in_specs=[pl.BlockSpec((x.shape[0], tile), lambda i: (0, i)) for x in arrays],
        out_specs=pl.BlockSpec((rows, tile), lambda i: (0, i)),
        out_shape=jax.ShapeDtypeStruct((rows, width), BF16),
        compiler_params=pltpu.CompilerParams(vmem_limit_bytes=VMEM_DOT),
        cost_estimate=SMALL,
    )(*arrays)


def on_device(ring, n_tp, tokens_in, w_query, w_key, w_value, short_taps, long_taps, grad_out):
    chips = len(ring)
    half = chips // 2
    n_ctx = 2 * chips
    held, width = tokens_in.shape
    channels = w_query.shape[1]
    weights = (w_query, w_key, w_value)

    def one_way(x, turned=False, to_mate=False):
        hops = []
        for j in range(chips):
            for core in range(2):
                chip = ring[(j + (1 if (core == 0) != turned else -1)) % chips]
                hops.append((2 * ring[j] + core, 2 * chip + (core ^ int(to_mate))))
        return lax.ppermute(x, "ctx", hops)

    def swap(x):
        return lax.ppermute(x, "ctx", [(d, d ^ 1) for d in range(n_ctx)])

    table = np.zeros((n_ctx, n_ctx), np.int32)
    for device in range(n_ctx):
        place, core = ring.index(device // 2), device % 2
        way = -1 if core == 0 else 1
        items = [(0, 0), (0, 1)]
        for s in range(1, half):
            items += [(way * s, 0), (way * s, 1), (-way * s, 1), (-way * s, 0)]
        items += [(half, 0), (half, 1)]
        table[device] = [2 * ring[(place + hop) % chips] + (core ^ other) for hop, other in items]
    order = lax.dynamic_index_in_dim(jnp.asarray(table), lax.axis_index("ctx"), 0, keepdims=False)
    short_kernel, long_kernel = short_taps.reshape(3, -1, SHORT), long_taps.reshape(-1, LONG)

    stay = 3 * channels
    if n_tp == 2:
        flat = restack(lax.axis_index("tp").astype(jnp.int32), weights)
    else:
        flat = jnp.stack(weights).reshape(-1, width)

    def project(pieces):
        if n_tp == 2:
            return project_kernel(flat, pieces)
        y = dot(flat, jnp.concatenate(pieces, axis=0), ((1,), (1,))).astype(BF16).reshape(3, n_tp, channels, -1)
        return lax.psum_scatter(y, "tp", scatter_dimension=1, tiled=True).reshape(stay, -1), None

    def across(x):
        return None if x is None else lax.ppermute(x, "tp", [(0, 1), (1, 0)])

    def meet(d):
        if n_tp == 2:
            return d.reshape(stay, -1), across(d.reshape(stay, -1))
        d = lax.all_gather(d.reshape(3, 1, channels, -1), "tp", axis=1, tiled=True)
        return (d.reshape(-1, d.shape[-1]),)

    def unproject(d, *cuts):
        if n_tp == 2:
            return unproject_kernel(flat, *d, cuts)
        y = dot(d[0], flat, ((0,), (0,))).astype(BF16)
        return jnp.split(y, np.cumsum(cuts)[:-1], axis=0)

    stage = lax.optimization_barrier

    arrived = [one_way(tokens_in), one_way(tokens_in, to_mate=True, turned=True)]
    near, far = project([tokens_in, swap(tokens_in)])
    arrived, near, far, order, short_kernel, long_kernel = stage((arrived, near, far, order, short_kernel, long_kernel))
    arrived = jnp.concatenate(arrived, axis=0)
    projected = []
    for s in range(1, half):
        coming = one_way(arrived if s < half - 1 else arrived[:held])
        projected.append((near, across(far)))
        near, far = project([arrived, swap(arrived)])
        arrived, near, far, projected[-1], grad_out = stage((coming, near, far, projected[-1], grad_out))
    projected.append((near, across(far)))
    incoming = lax.all_to_all(
        grad_out.reshape(n_ctx, channels, held), "ctx", split_axis=0, concat_axis=0, tiled=True
    )
    near, far = project([arrived, swap(arrived)])
    projected.append((near, across(far)))

    mixed, d_proj, grad_short, grad_long = mix(
        order,
        short_kernel,
        long_kernel,
        incoming,
        [[y.reshape(3, channels, -1) for y in side] for side in zip(*projected) if side[0] is not None],
        [[s] for s in range(half + 1)],
    )

    mixed_out = lax.all_to_all(mixed, "ctx", split_axis=0, concat_axis=0, tiled=True).reshape(-1, held)
    met = meet(d_proj[half - 1])
    keep, *give = unproject(meet(d_proj[half]), held, held // 2, held // 2)
    total = add_kernel([keep], [swap(x) for x in give])
    total, met, rest, mixed_out = stage((total, met, d_proj[: half - 1], mixed_out))
    for s in range(half - 1, 0, -1):
        coming = one_way(total, turned=True)
        later = meet(rest[-1])
        cuts = (96, 80, 80) if s == half - 1 and held == 128 else (held, held)
        keep, *give = unproject(met, 2 * held, *cuts)
        total = add_kernel([keep], [swap(x) for x in give], [coming])
        total, met, rest = stage((total, later, rest[:-1]))
    coming = [one_way(total[:held], turned=True), one_way(total[held:], turned=True, to_mate=True)]
    keep, *give = unproject(met, held, held // 2, held // 2)
    grad_tokens = add_kernel([keep], [swap(x) for x in give], coming[:1], coming[1:])
    return (
        mixed_out,
        grad_tokens,
        grad_short.reshape(3, 1, -1, SHORT),
        grad_long.reshape(1, -1, LONG),
    )


def solution(mesh):
    placed = (
        P("ctx", "tp"),
        P(None, "ctx", "tp"),
        P(None, "ctx", "tp"),
        P(None, "ctx", "tp"),
        P(None, "tp", "ctx", None),
        P("tp", "ctx", None),
        P("tp", "ctx"),
    )
    return jax.shard_map(
        functools.partial(on_device, ring_of(mesh), mesh.shape["tp"]),
        mesh=mesh,
        in_specs=placed,
        out_specs=(
            P("tp", "ctx"),
            P("ctx", "tp"),
            P(None, "tp", "ctx", None),
            P("tp", "ctx", None),
        ),
        check_vma=False,
    )
```

```python
import functools

import jax
import jax.numpy as jnp
import numpy as np
from jax import lax
from jax.experimental import pallas as pl
from jax.experimental.pallas import tpu as pltpu
from jax.sharding import PartitionSpec as P

GROUP = 16
SHORT = 3
LONG = 128
F32 = jnp.float32
BF16 = jnp.bfloat16
MIB = 1024 * 1024
SMALL = pl.CostEstimate(flops=1, bytes_accessed=1, transcendentals=0)


def ring_of(mesh):
    chips = mesh.shape["ctx"] // 2
    plain = list(range(chips))
    devices = np.asarray(mesh.devices).reshape(mesh.shape["ctx"], -1)[:, 0]
    places = [getattr(devices[2 * chip], "coords", None) for chip in plain]
    if any(place is None for place in places):
        return plain
    places = np.array([list(place)[:3] for place in places])
    axes = [axis for axis in range(3) if len(set(places[:, axis])) > 1]
    if len(axes) != 2:
        return plain
    rung = min(axes, key=lambda axis: len(set(places[:, axis])))
    along = axes[0] if rung == axes[1] else axes[1]
    sides = sorted(set(places[:, rung]))
    if len(sides) != 2:
        return plain
    there = [c for c in plain if places[c, rung] == sides[0]]
    back = [c for c in plain if places[c, rung] == sides[1]]
    there.sort(key=lambda c: places[c, along])
    back.sort(key=lambda c: -places[c, along])
    return there + back


def dot(a, b, dims):
    return lax.dot_general(a, b, (dims, ((), ())), preferred_element_type=F32)


def mix_body(count, sets, per_step, grouped, order, short_ref, long_ref, g_ref, *refs):
    proj_refs = [refs[s * count : (s + 1) * count] for s in range(sets)]
    refs = refs[sets * count :]
    d_count = len(grouped)
    mixed_ref, d_refs, gs_ref, gl_ref = refs[0], refs[1 : 1 + d_count], refs[1 + d_count], refs[2 + d_count]
    p_s, x_s, y_s, d_s, e_s = refs[3 + d_count :]
    blocks = g_ref.shape[0]
    rows = blocks * GROUP
    step = pl.program_id(0)

    @pl.when(step == 0)
    def _():
        p_s[:, :, 0:GROUP, :] = jnp.zeros((per_step, 3, GROUP, LONG), F32)
        x_s[:, 0:GROUP, :] = jnp.zeros((per_step, GROUP, LONG), BF16)
        y_s[:, rows:, :] = jnp.zeros((per_step, GROUP, LONG), BF16)
        d_s[:, :, rows:, :] = jnp.zeros((per_step, 3, GROUP, LONG), F32)

    halves = [(a, h) for a in range(count) for h in range(proj_refs[0][a].shape[2] // LONG)]
    places = [(a, h, where) for where, (a, h) in enumerate(halves)]
    d_places = []
    for b, arrays in enumerate(grouped):
        inside = [where for array in arrays for a, _, where in places if a == array]
        d_places += [(b, h, where) for h, where in enumerate(inside)]
    lane = lax.broadcasted_iota(jnp.int32, (rows, LONG), 1)
    sub8 = lax.broadcasted_iota(jnp.int32, (8, LONG), 0)
    col = lax.broadcasted_iota(jnp.int32, (LONG, LONG), 1)
    row = lax.broadcasted_iota(jnp.int32, (LONG, LONG), 0)

    for j in range(per_step):
        group = step * per_step + j
        mine = slice(j * GROUP, (j + 1) * GROUP)
        for a, h, where in places:
            at = pl.multiple_of((order[where] + 1) * GROUP, GROUP)
            for i in range(3):
                part = proj_refs[0][a][i, mine, h * LONG : (h + 1) * LONG].astype(F32)
                for s in range(1, sets):
                    part = part + proj_refs[s][a][i, mine, h * LONG : (h + 1) * LONG].astype(F32)
                p_s[j, i, pl.ds(at, GROUP), :] = part
        taps = [[short_ref[i, group, k] for k in range(SHORT)] for i in range(3)]
        feats = []
        for i in range(3):
            whole = p_s[j, i]
            one = pltpu.roll(whole, 1, 1)
            two = pltpu.roll(whole, 2, 1)
            one = jnp.where(lane < 1, one[:rows], one[GROUP:])
            two = jnp.where(lane < 2, two[:rows], two[GROUP:])
            feats.append(taps[i][0] * whole[GROUP:] + taps[i][1] * one + taps[i][2] * two)
        fq, fk, fv = feats
        x_s[j, GROUP:, :] = (fk * fv).astype(BF16)

        base = jnp.broadcast_to(long_ref[0, j : j + 1, :], (8, LONG))
        for bit in (1, 2, 4):
            base = jnp.where((sub8 & bit) != 0, pltpu.roll(base, bit, 1), base)
        full = jnp.concatenate([base] + [pltpu.roll(base, 8 * m, 1) for m in range(1, LONG // 8)], axis=0)
        near = jnp.where(col >= row, full, 0.0).astype(BF16)
        far = jnp.where(col < row, full, 0.0).astype(BF16)

        x_two = jnp.concatenate([x_s[j, GROUP:, :], x_s[j, :rows, :]], axis=1)
        inner = dot(x_two, jnp.concatenate([near, far], axis=0), ((1,), (0,)))
        g = g_ref[:, mine, :].reshape(rows, LONG).astype(F32)
        mixed_ref[:, mine, :] = (fq * inner).astype(BF16).reshape(blocks, GROUP, LONG)
        y_s[j, :rows, :] = (g * fq).astype(BF16)
        y_one = y_s[j, :rows, :]
        y_two = jnp.concatenate([y_one, y_s[j, GROUP:, :]], axis=1)
        d_product = dot(y_two, jnp.concatenate([near, far], axis=1), ((1,), (1,)))

        pairs = dot(x_two, y_one, ((0,), (0,)))
        fold = jnp.where(col >= row, pairs[:LONG], pairs[LONG:])
        width = LONG
        while width > 8:
            width //= 2
            fold = fold[:width] + pltpu.roll(fold[width:], LONG - width, 1)
        for bit in (4, 2, 1):
            fold = jnp.where((sub8 & bit) != 0, pltpu.roll(fold, LONG - bit, 1), fold)
        gl_ref[0, j : j + 1, :] = jnp.sum(fold, axis=0, keepdims=True)

        for i, d in enumerate((g * inner, d_product * fv, d_product * fk)):
            d_s[j, i, :rows, :] = d
            whole = d_s[j, i]
            one = pltpu.roll(whole, LONG - 1, 1)
            two = pltpu.roll(whole, LONG - 2, 1)
            one = jnp.where(lane >= LONG - 1, one[GROUP:], one[:rows])
            two = jnp.where(lane >= LONG - 2, two[GROUP:], two[:rows])
            p = p_s[j, i, GROUP:, :]
            for k, moved in enumerate((d, one, two)):
                gs_ref[0, j, 3 * i + k : 3 * i + k + 1, :] = jnp.sum(p * moved, axis=0, keepdims=True)
            e_s[j, i] = (taps[i][0] * d + taps[i][1] * one + taps[i][2] * two).astype(BF16)
        for a, h, where in d_places:
            at = pl.multiple_of(order[where] * GROUP, GROUP)
            for i in range(3):
                d_refs[a][i, mine, h * LONG : (h + 1) * LONG] = e_s[j, i, pl.ds(at, GROUP), :]


def mix(order, short_kernel, long_kernel, g, proj_sets, grouped):
    blocks, channels, _ = g.shape
    count, sets = len(proj_sets[0]), len(proj_sets)
    groups = channels // GROUP
    per_step = 2 if groups % 2 == 0 else 1
    steps = groups // per_step
    rows = blocks * GROUP
    high = per_step * GROUP
    proj_specs = [pl.BlockSpec((3, high, x.shape[2]), lambda i, o: (0, i, 0)) for x in proj_sets[0]]
    d_widths = [sum(proj_sets[0][a].shape[2] for a in arrays) for arrays in grouped]
    d_specs = [pl.BlockSpec((3, high, w), lambda i, o: (0, i, 0)) for w in d_widths]
    token_spec = pl.BlockSpec((blocks, high, LONG), lambda i, o: (0, i, 0))
    outs = pl.pallas_call(
        functools.partial(mix_body, count, sets, per_step, grouped),
        grid_spec=pltpu.PrefetchScalarGridSpec(
            num_scalar_prefetch=1,
            grid=(steps,),
            in_specs=[
                pl.BlockSpec(memory_space=pltpu.SMEM),
                pl.BlockSpec((1, per_step, LONG), lambda i, o: (i, 0, 0)),
                token_spec,
            ]
            + proj_specs * sets,
            out_specs=[token_spec]
            + d_specs
            + [
                pl.BlockSpec((1, per_step, 3 * SHORT, LONG), lambda i, o: (i, 0, 0, 0)),
                pl.BlockSpec((1, per_step, LONG), lambda i, o: (i, 0, 0)),
            ],
            scratch_shapes=[
                pltpu.VMEM((per_step, 3, rows + GROUP, LONG), F32),
                pltpu.VMEM((per_step, rows + GROUP, LONG), BF16),
                pltpu.VMEM((per_step, rows + GROUP, LONG), BF16),
                pltpu.VMEM((per_step, 3, rows + GROUP, LONG), F32),
                pltpu.VMEM((per_step, 3, rows, LONG), BF16),
            ],
        ),
        out_shape=[jax.ShapeDtypeStruct((blocks, channels, LONG), BF16)]
        + [jax.ShapeDtypeStruct((3, channels, w), BF16) for w in d_widths]
        + [
            jax.ShapeDtypeStruct((steps, per_step, 3 * SHORT, LONG), F32),
            jax.ShapeDtypeStruct((steps, per_step, LONG), F32),
        ],
        compiler_params=pltpu.CompilerParams(vmem_limit_bytes=20 * MIB),
        cost_estimate=SMALL,
    )(order, short_kernel, long_kernel.reshape(steps, per_step, LONG), g, *[x for s in proj_sets for x in s])
    mixed, d_proj, (gs, gl) = outs[0], outs[1:-2], outs[-2:]
    grad_short = jnp.sum(gs, axis=-1).reshape(groups, 3, SHORT).transpose(1, 0, 2)
    return mixed, d_proj, grad_short, gl.reshape(groups, LONG)


def restack_body(t_ref, *refs):
    out_ref = refs[3]
    for i in range(3):
        out_ref[0, i] = refs[i][0]


def restack(t, weights):
    _, channels, width = weights[0].shape
    tile = min(128, channels)

    def source(side, part, t):
        return (jnp.where(side == 0, t[0], 1 - t[0]), part, 0)

    return pl.pallas_call(
        restack_body,
        grid_spec=pltpu.PrefetchScalarGridSpec(
            num_scalar_prefetch=1,
            grid=(2, channels // tile),
            in_specs=[pl.BlockSpec((1, tile, width), source)] * 3,
            out_specs=pl.BlockSpec((1, 3, tile, width), lambda side, part, t: (side, 0, part, 0)),
        ),
        out_shape=jax.ShapeDtypeStruct((2, 3, channels, width), BF16),
        compiler_params=pltpu.CompilerParams(vmem_limit_bytes=16 * MIB),
        cost_estimate=SMALL,
    )(t.reshape(1), *weights).reshape(6 * channels, width)


def project_body(pieces, *refs):
    x_refs, w_ref = refs[:pieces], refs[pieces]
    far_ref, near_ref, x_s, sems = refs[pieces + 1 :]
    step, steps = pl.program_id(0), pl.num_programs(0)

    @pl.when(step == 0)
    def _():
        copies, at = [], 0
        for n, x in enumerate(x_refs):
            copies.append(pltpu.make_async_copy(x, x_s.at[pl.ds(at, x.shape[0])], sems.at[n]))
            at += x.shape[0]
        for copy in copies:
            copy.start()
        for copy in copies:
            copy.wait()

    got = dot(w_ref[...], x_s[...], ((1,), (1,))).astype(BF16)

    @pl.when(step < steps // 2)
    def _():
        far_ref[...] = got

    @pl.when(step >= steps // 2)
    def _():
        near_ref[...] = got


def project_kernel(flat, pieces):
    rows, width = flat.shape
    tokens = sum(x.shape[0] for x in pieces)
    tile = rows // 4
    half = jax.ShapeDtypeStruct((rows // 2, tokens), BF16)
    far, near = pl.pallas_call(
        functools.partial(project_body, len(pieces)),
        grid=(4,),
        in_specs=[pl.BlockSpec(memory_space=pl.ANY)] * len(pieces)
        + [pl.BlockSpec((tile, width), lambda i: ((i + 2) % 4, 0))],
        out_specs=[
            pl.BlockSpec((tile, tokens), lambda i: (jnp.minimum(i, 1), 0)),
            pl.BlockSpec((tile, tokens), lambda i: (jnp.maximum(i - 2, 0), 0)),
        ],
        out_shape=[half, half],
        scratch_shapes=[pltpu.VMEM((tokens, width), BF16), pltpu.SemaphoreType.DMA((len(pieces),))],
        compiler_params=pltpu.CompilerParams(vmem_limit_bytes=16 * MIB),
        cost_estimate=SMALL,
    )(*pieces, flat)
    return near, far


def unproject_body(near_ref, far_ref, w_ref, *refs):
    out_refs, d_s = refs[:-1], refs[-1]
    stay = near_ref.shape[0]

    @pl.when(pl.program_id(0) == 0)
    def _():
        d_s[:, 0:stay] = near_ref[...].T
        d_s[:, stay:] = far_ref[...].T

    got = dot(d_s[...], w_ref[...], ((1,), (0,)))
    at = 0
    for out_ref in out_refs:
        out_ref[...] = got[at : at + out_ref.shape[0]].astype(BF16)
        at += out_ref.shape[0]


def unproject_kernel(flat, near, far, cuts):
    rows, width = flat.shape
    tokens = near.shape[1]
    tile = min(512, width)
    return pl.pallas_call(
        unproject_body,
        grid=(width // tile,),
        in_specs=[
            pl.BlockSpec((rows // 2, tokens), lambda i: (0, 0)),
            pl.BlockSpec((rows // 2, tokens), lambda i: (0, 0)),
            pl.BlockSpec((rows, tile), lambda i: (0, i)),
        ],
        out_specs=[pl.BlockSpec((cut, tile), lambda i: (0, i)) for cut in cuts],
        out_shape=[jax.ShapeDtypeStruct((cut, width), BF16) for cut in cuts],
        scratch_shapes=[pltpu.VMEM((tokens, rows), BF16)],
        compiler_params=pltpu.CompilerParams(vmem_limit_bytes=14 * MIB),
        cost_estimate=SMALL,
    )(near, far, flat)


def add_body(heights, *refs):
    out_refs = refs[sum(heights) :]
    groups, at = [], 0
    for height in heights:
        groups.append(refs[at : at + height])
        at += height
    tops = [[sum(r.shape[0] for r in group[:n]) for n in range(len(group) + 1)] for group in groups]
    height = out_refs[0].shape[0]
    edges = {edge for top in tops for edge in top} | {n * height for n in range(len(out_refs) + 1)}
    edges = sorted(edges)
    for low, high in zip(edges[:-1], edges[1:]):
        total = None
        for group, top in zip(groups, tops):
            for n, ref in enumerate(group):
                if top[n] <= low and high <= top[n + 1]:
                    part = ref[low - top[n] : high - top[n], :].astype(F32)
                    total = part if total is None else total + part
        out_refs[low // height][low % height : low % height + high - low, :] = total.astype(BF16)


def add_kernel(*groups, cut=1):
    rows, width = sum(x.shape[0] for x in groups[0]) // cut, groups[0][0].shape[1]
    tile = min(1024, width)
    arrays = [x for group in groups for x in group]
    return pl.pallas_call(
        functools.partial(add_body, [len(group) for group in groups]),
        grid=(width // tile,),
        in_specs=[pl.BlockSpec((x.shape[0], tile), lambda i: (0, i)) for x in arrays],
        out_specs=[pl.BlockSpec((rows, tile), lambda i: (0, i))] * cut,
        out_shape=[jax.ShapeDtypeStruct((rows, width), BF16)] * cut,
        compiler_params=pltpu.CompilerParams(vmem_limit_bytes=8 * MIB),
        cost_estimate=SMALL,
    )(*arrays)


def on_device(ring, n_tp, tokens_in, w_query, w_key, w_value, short_taps, long_taps, grad_out):
    chips = len(ring)
    half = chips // 2
    n_ctx = 2 * chips
    held, width = tokens_in.shape
    channels = w_query.shape[1]
    weights = (w_query, w_key, w_value)

    def one_way(x, turned=False, to_mate=False):
        hops = []
        for j in range(chips):
            for core in range(2):
                chip = ring[(j + (1 if (core == 0) != turned else -1)) % chips]
                hops.append((2 * ring[j] + core, 2 * chip + (core ^ int(to_mate))))
        return lax.ppermute(x, "ctx", hops)

    def swap(x):
        return lax.ppermute(x, "ctx", [(d, d ^ 1) for d in range(n_ctx)])

    table = np.zeros((n_ctx, n_ctx), np.int32)
    for device in range(n_ctx):
        place, core = ring.index(device // 2), device % 2
        way = -1 if core == 0 else 1
        items = [(0, 0), (0, 1)]
        for s in range(1, half):
            items += [(way * s, 0), (way * s, 1), (-way * s, 1), (-way * s, 0)]
        items += [(half, 0), (half, 1)]
        table[device] = [2 * ring[(place + hop) % chips] + (core ^ other) for hop, other in items]
    order = lax.dynamic_index_in_dim(jnp.asarray(table), lax.axis_index("ctx"), 0, keepdims=False)
    short_kernel, long_kernel = short_taps.reshape(3, -1, SHORT), long_taps.reshape(-1, LONG)

    stay = 3 * channels
    if n_tp == 2:
        flat = restack(lax.axis_index("tp").astype(jnp.int32), weights)
    else:
        flat = jnp.stack(weights).reshape(-1, width)

    def project(pieces):
        if n_tp == 2:
            return project_kernel(flat, pieces)
        y = dot(flat, jnp.concatenate(pieces, axis=0), ((1,), (1,))).astype(BF16).reshape(3, n_tp, channels, -1)
        return lax.psum_scatter(y, "tp", scatter_dimension=1, tiled=True).reshape(stay, -1), None

    def across(x):
        return None if x is None else lax.ppermute(x, "tp", [(0, 1), (1, 0)])

    def meet(d):
        if n_tp == 2:
            return d.reshape(stay, -1), across(d.reshape(stay, -1))
        d = lax.all_gather(d.reshape(3, 1, channels, -1), "tp", axis=1, tiled=True)
        return (d.reshape(-1, d.shape[-1]),)

    def unproject(d, *cuts):
        if n_tp == 2:
            return unproject_kernel(flat, *d, cuts)
        y = dot(d[0], flat, ((0,), (0,))).astype(BF16)
        return jnp.split(y, np.cumsum(cuts)[:-1], axis=0)

    stage = lax.optimization_barrier

    arrived = [one_way(tokens_in), one_way(tokens_in, to_mate=True, turned=True)]
    near, far = project([tokens_in, swap(tokens_in)])
    arrived, near, far, order, short_kernel, long_kernel = stage((arrived, near, far, order, short_kernel, long_kernel))
    arrived = jnp.concatenate(arrived, axis=0)
    projected = []
    for s in range(1, half):
        coming = one_way(arrived if s < half - 1 else arrived[:held])
        projected.append((near, across(far)))
        near, far = project([arrived, swap(arrived)])
        if s < half - 1:
            arrived, near, far, projected[-1] = stage((coming, near, far, projected[-1]))
    crossed = across(far)
    arrived, near, grad_out = stage((coming, near, grad_out))
    incoming = lax.all_to_all(
        grad_out.reshape(n_ctx, channels, held), "ctx", split_axis=0, concat_axis=0, tiled=True
    )
    shared, projected[-1] = stage((arrived, projected[-1]))
    last, far = project([arrived, swap(shared[: held // 2]), swap(shared[held // 2 :])])
    far, crossed = stage((far, crossed))
    projected += [(near, crossed), (last, across(far))]

    mixed, d_proj, grad_short, grad_long = mix(
        order,
        short_kernel,
        long_kernel,
        incoming,
        [[y.reshape(3, channels, -1) for y in side] for side in zip(*projected) if side[0] is not None],
        [[s] for s in range(half + 1)],
    )

    first, met, later = [meet(d_proj[s]) for s in (half, half - 1, half - 2)]
    mixed_out = lax.all_to_all(mixed, "ctx", split_axis=0, concat_axis=0, tiled=True).reshape(-1, held)
    keep, *give = unproject(first, held, held // 2, held // 2)
    total = add_kernel([keep], [swap(x) for x in give])
    total, met, rest, mixed_out = stage((total, met, d_proj[: half - 2], mixed_out))
    for s in range(half - 1, 0, -1):
        coming = one_way(total[0], turned=True)
        if s < half - 1:
            later = meet(rest[-1])
            rest = rest[:-1]
        cuts = (96, 80, 80) if s == half - 1 and held == 128 else (held, held)
        keep, *give = unproject(met, 2 * held, *cuts)
        give, later = stage((give, later))
        total = add_kernel([keep], [swap(x) for x in give], [coming], cut=2 if s == 1 else 1)
        total, met, rest = stage((total, later, rest))
    coming = [one_way(total[0], turned=True), one_way(total[1], turned=True, to_mate=True)]
    keep, *give = unproject(met, held, held // 2, held // 2)
    (grad_tokens,) = add_kernel([keep], [swap(x) for x in give], coming[:1], coming[1:])
    return (
        mixed_out,
        grad_tokens,
        grad_short.reshape(3, 1, -1, SHORT),
        grad_long.reshape(1, -1, LONG),
    )


def solution(mesh):
    placed = (
        P("ctx", "tp"),
        P(None, "ctx", "tp"),
        P(None, "ctx", "tp"),
        P(None, "ctx", "tp"),
        P(None, "tp", "ctx", None),
        P("tp", "ctx", None),
        P("tp", "ctx"),
    )
    return jax.shard_map(
        functools.partial(on_device, ring_of(mesh), mesh.shape["tp"]),
        mesh=mesh,
        in_specs=placed,
        out_specs=(
            P("tp", "ctx"),
            P("ctx", "tp"),
            P(None, "tp", "ctx", None),
            P("tp", "ctx", None),
        ),
        check_vma=False,
    )
```

```python
import functools

import jax
import jax.numpy as jnp
import numpy as np
from jax import lax
from jax.experimental import pallas as pl
from jax.experimental.pallas import tpu as pltpu
from jax.sharding import PartitionSpec as P

GROUP = 16
SHORT = 3
LONG = 128
F32 = jnp.float32
BF16 = jnp.bfloat16
MIB = 1024 * 1024
SMALL = pl.CostEstimate(flops=1, bytes_accessed=1, transcendentals=0)


def ring_of(mesh):
    chips = mesh.shape["ctx"] // 2
    plain = list(range(chips))
    devices = np.asarray(mesh.devices).reshape(mesh.shape["ctx"], -1)[:, 0]
    places = [getattr(devices[2 * chip], "coords", None) for chip in plain]
    if any(place is None for place in places):
        return plain
    places = np.array([list(place)[:3] for place in places])
    axes = [axis for axis in range(3) if len(set(places[:, axis])) > 1]
    if len(axes) != 2:
        return plain
    rung = min(axes, key=lambda axis: len(set(places[:, axis])))
    along = axes[0] if rung == axes[1] else axes[1]
    sides = sorted(set(places[:, rung]))
    if len(sides) != 2:
        return plain
    there = [c for c in plain if places[c, rung] == sides[0]]
    back = [c for c in plain if places[c, rung] == sides[1]]
    there.sort(key=lambda c: places[c, along])
    back.sort(key=lambda c: -places[c, along])
    return there + back


def dot(a, b, dims):
    return lax.dot_general(a, b, (dims, ((), ())), preferred_element_type=F32)


def mix_body(count, sets, per_step, grouped, order, short_ref, long_ref, g_ref, *refs):
    proj_refs = [refs[s * count : (s + 1) * count] for s in range(sets)]
    refs = refs[sets * count :]
    d_count = len(grouped)
    mixed_ref, d_refs, gs_ref, gl_ref = refs[0], refs[1 : 1 + d_count], refs[1 + d_count], refs[2 + d_count]
    p_s, x_s, y_s, d_s, e_s = refs[3 + d_count :]
    blocks = g_ref.shape[0]
    rows = blocks * GROUP
    step = pl.program_id(0)

    @pl.when(step == 0)
    def _():
        p_s[:, :, 0:GROUP, :] = jnp.zeros((per_step, 3, GROUP, LONG), F32)
        x_s[:, 0:GROUP, :] = jnp.zeros((per_step, GROUP, LONG), BF16)
        y_s[:, rows:, :] = jnp.zeros((per_step, GROUP, LONG), BF16)
        d_s[:, :, rows:, :] = jnp.zeros((per_step, 3, GROUP, LONG), F32)

    halves = [(a, h) for a in range(count) for h in range(proj_refs[0][a].shape[2] // LONG)]
    places = [(a, h, where) for where, (a, h) in enumerate(halves)]
    d_places = []
    for b, arrays in enumerate(grouped):
        inside = [where for array in arrays for a, _, where in places if a == array]
        d_places += [(b, h, where) for h, where in enumerate(inside)]
    lane = lax.broadcasted_iota(jnp.int32, (rows, LONG), 1)
    sub8 = lax.broadcasted_iota(jnp.int32, (8, LONG), 0)
    col = lax.broadcasted_iota(jnp.int32, (LONG, LONG), 1)
    row = lax.broadcasted_iota(jnp.int32, (LONG, LONG), 0)

    every = range(per_step)
    mine = [slice(j * GROUP, (j + 1) * GROUP) for j in every]
    taps = [
        [[short_ref[i, step * per_step + j, k] for k in range(SHORT)] for i in range(3)] for j in every
    ]
    for a, h, where in places:
        at = pl.multiple_of((order[where] + 1) * GROUP, GROUP)
        for j in every:
            for i in range(3):
                part = proj_refs[0][a][i, mine[j], h * LONG : (h + 1) * LONG].astype(F32)
                for s in range(1, sets):
                    part = part + proj_refs[s][a][i, mine[j], h * LONG : (h + 1) * LONG].astype(F32)
                p_s[j, i, pl.ds(at, GROUP), :] = part

    feats = []
    for j in every:
        feat = []
        for i in range(3):
            whole = p_s[j, i]
            one = pltpu.roll(whole, 1, 1)
            two = pltpu.roll(whole, 2, 1)
            one = jnp.where(lane < 1, one[:rows], one[GROUP:])
            two = jnp.where(lane < 2, two[:rows], two[GROUP:])
            feat.append(taps[j][i][0] * whole[GROUP:] + taps[j][i][1] * one + taps[j][i][2] * two)
        feats.append(feat)
        x_s[j, GROUP:, :] = (feat[1] * feat[2]).astype(BF16)

    filters = []
    for j in every:
        base = jnp.broadcast_to(long_ref[0, j : j + 1, :], (8, LONG))
        for bit in (1, 2, 4):
            base = jnp.where((sub8 & bit) != 0, pltpu.roll(base, bit, 1), base)
        full = jnp.concatenate([base] + [pltpu.roll(base, 8 * m, 1) for m in range(1, LONG // 8)], axis=0)
        near = jnp.where(col >= row, full, 0.0).astype(BF16)
        far = jnp.where(col < row, full, 0.0).astype(BF16)
        filters.append((near, far))

    x_twos = [jnp.concatenate([x_s[j, GROUP:, :], x_s[j, :rows, :]], axis=1) for j in every]
    inners = [dot(x_twos[j], jnp.concatenate(filters[j], axis=0), ((1,), (0,))) for j in every]
    d_queries = []
    for j in every:
        g = g_ref[:, mine[j], :].reshape(rows, LONG).astype(F32)
        mixed_ref[:, mine[j], :] = (feats[j][0] * inners[j]).astype(BF16).reshape(blocks, GROUP, LONG)
        y_s[j, :rows, :] = (g * feats[j][0]).astype(BF16)
        d_queries.append(g * inners[j])
    d_products = []
    for j in every:
        y_two = jnp.concatenate([y_s[j, :rows, :], y_s[j, GROUP:, :]], axis=1)
        d_products.append(dot(y_two, jnp.concatenate(filters[j], axis=1), ((1,), (1,))))
    folds = [dot(x_twos[j], y_s[j, :rows, :], ((0,), (0,))) for j in every]
    for j in every:
        fold = jnp.where(col >= row, folds[j][:LONG], folds[j][LONG:])
        width = LONG
        while width > 8:
            width //= 2
            fold = fold[:width] + pltpu.roll(fold[width:], LONG - width, 1)
        for bit in (4, 2, 1):
            fold = jnp.where((sub8 & bit) != 0, pltpu.roll(fold, LONG - bit, 1), fold)
        gl_ref[0, j : j + 1, :] = jnp.sum(fold, axis=0, keepdims=True)

    for j in every:
        for i, d in enumerate((d_queries[j], d_products[j] * feats[j][2], d_products[j] * feats[j][1])):
            d_s[j, i, :rows, :] = d
            whole = d_s[j, i]
            one = pltpu.roll(whole, LONG - 1, 1)
            two = pltpu.roll(whole, LONG - 2, 1)
            one = jnp.where(lane >= LONG - 1, one[GROUP:], one[:rows])
            two = jnp.where(lane >= LONG - 2, two[GROUP:], two[:rows])
            p = p_s[j, i, GROUP:, :]
            for k, moved in enumerate((d, one, two)):
                gs_ref[0, j, 3 * i + k : 3 * i + k + 1, :] = jnp.sum(p * moved, axis=0, keepdims=True)
            e_s[j, i] = (taps[j][i][0] * d + taps[j][i][1] * one + taps[j][i][2] * two).astype(BF16)
    for a, h, where in d_places:
        at = pl.multiple_of(order[where] * GROUP, GROUP)
        for j in every:
            for i in range(3):
                d_refs[a][i, mine[j], h * LONG : (h + 1) * LONG] = e_s[j, i, pl.ds(at, GROUP), :]


def mix(order, short_kernel, long_kernel, g, proj_sets, grouped):
    blocks, channels, _ = g.shape
    count, sets = len(proj_sets[0]), len(proj_sets)
    groups = channels // GROUP
    per_step = next(n for n in (4, 2, 1) if groups % n == 0)
    steps = groups // per_step
    rows = blocks * GROUP
    high = per_step * GROUP
    proj_specs = [pl.BlockSpec((3, high, x.shape[2]), lambda i, o: (0, i, 0)) for x in proj_sets[0]]
    d_widths = [sum(proj_sets[0][a].shape[2] for a in arrays) for arrays in grouped]
    d_specs = [pl.BlockSpec((3, high, w), lambda i, o: (0, i, 0)) for w in d_widths]
    token_spec = pl.BlockSpec((blocks, high, LONG), lambda i, o: (0, i, 0))
    outs = pl.pallas_call(
        functools.partial(mix_body, count, sets, per_step, grouped),
        grid_spec=pltpu.PrefetchScalarGridSpec(
            num_scalar_prefetch=1,
            grid=(steps,),
            in_specs=[
                pl.BlockSpec(memory_space=pltpu.SMEM),
                pl.BlockSpec((1, per_step, LONG), lambda i, o: (i, 0, 0)),
                token_spec,
            ]
            + proj_specs * sets,
            out_specs=[token_spec]
            + d_specs
            + [
                pl.BlockSpec((1, per_step, 3 * SHORT, LONG), lambda i, o: (i, 0, 0, 0)),
                pl.BlockSpec((1, per_step, LONG), lambda i, o: (i, 0, 0)),
            ],
            scratch_shapes=[
                pltpu.VMEM((per_step, 3, rows + GROUP, LONG), F32),
                pltpu.VMEM((per_step, rows + GROUP, LONG), BF16),
                pltpu.VMEM((per_step, rows + GROUP, LONG), BF16),
                pltpu.VMEM((per_step, 3, rows + GROUP, LONG), F32),
                pltpu.VMEM((per_step, 3, rows, LONG), BF16),
            ],
        ),
        out_shape=[jax.ShapeDtypeStruct((blocks, channels, LONG), BF16)]
        + [jax.ShapeDtypeStruct((3, channels, w), BF16) for w in d_widths]
        + [
            jax.ShapeDtypeStruct((steps, per_step, 3 * SHORT, LONG), F32),
            jax.ShapeDtypeStruct((steps, per_step, LONG), F32),
        ],
        compiler_params=pltpu.CompilerParams(vmem_limit_bytes=58 * MIB),
        cost_estimate=SMALL,
    )(order, short_kernel, long_kernel.reshape(steps, per_step, LONG), g, *[x for s in proj_sets for x in s])
    mixed, d_proj, (gs, gl) = outs[0], outs[1:-2], outs[-2:]
    grad_short = jnp.sum(gs, axis=-1).reshape(groups, 3, SHORT).transpose(1, 0, 2)
    return mixed, d_proj, grad_short, gl.reshape(groups, LONG)


def restack_body(t_ref, *refs):
    out_ref = refs[3]
    for i in range(3):
        out_ref[0, i] = refs[i][0]


def restack(t, weights):
    _, channels, width = weights[0].shape
    tile = min(128, channels)

    def source(side, part, t):
        return (jnp.where(side == 0, t[0], 1 - t[0]), part, 0)

    return pl.pallas_call(
        restack_body,
        grid_spec=pltpu.PrefetchScalarGridSpec(
            num_scalar_prefetch=1,
            grid=(2, channels // tile),
            in_specs=[pl.BlockSpec((1, tile, width), source)] * 3,
            out_specs=pl.BlockSpec((1, 3, tile, width), lambda side, part, t: (side, 0, part, 0)),
        ),
        out_shape=jax.ShapeDtypeStruct((2, 3, channels, width), BF16),
        compiler_params=pltpu.CompilerParams(vmem_limit_bytes=16 * MIB),
        cost_estimate=SMALL,
    )(t.reshape(1), *weights).reshape(6 * channels, width)


def project_body(pieces, *refs):
    x_refs, w_ref = refs[:pieces], refs[pieces]
    far_ref, near_ref, x_s, sems = refs[pieces + 1 :]
    step, steps = pl.program_id(0), pl.num_programs(0)

    @pl.when(step == 0)
    def _():
        copies, at = [], 0
        for n, x in enumerate(x_refs):
            copies.append(pltpu.make_async_copy(x, x_s.at[pl.ds(at, x.shape[0])], sems.at[n]))
            at += x.shape[0]
        for copy in copies:
            copy.start()
        for copy in copies:
            copy.wait()

    got = dot(w_ref[...], x_s[...], ((1,), (1,))).astype(BF16)

    @pl.when(step < steps // 2)
    def _():
        far_ref[...] = got

    @pl.when(step >= steps // 2)
    def _():
        near_ref[...] = got


def project_kernel(flat, pieces):
    rows, width = flat.shape
    tokens = sum(x.shape[0] for x in pieces)
    tile = rows // 4
    half = jax.ShapeDtypeStruct((rows // 2, tokens), BF16)
    far, near = pl.pallas_call(
        functools.partial(project_body, len(pieces)),
        grid=(4,),
        in_specs=[pl.BlockSpec(memory_space=pl.ANY)] * len(pieces)
        + [pl.BlockSpec((tile, width), lambda i: ((i + 2) % 4, 0))],
        out_specs=[
            pl.BlockSpec((tile, tokens), lambda i: (jnp.minimum(i, 1), 0)),
            pl.BlockSpec((tile, tokens), lambda i: (jnp.maximum(i - 2, 0), 0)),
        ],
        out_shape=[half, half],
        scratch_shapes=[pltpu.VMEM((tokens, width), BF16), pltpu.SemaphoreType.DMA((len(pieces),))],
        compiler_params=pltpu.CompilerParams(vmem_limit_bytes=16 * MIB),
        cost_estimate=SMALL,
    )(*pieces, flat)
    return near, far


def unproject_body(near_ref, far_ref, w_ref, *refs):
    out_refs, d_s = refs[:-1], refs[-1]
    stay = near_ref.shape[0]

    @pl.when(pl.program_id(0) == 0)
    def _():
        d_s[:, 0:stay] = near_ref[...].T
        d_s[:, stay:] = far_ref[...].T

    got = dot(d_s[...], w_ref[...], ((1,), (0,)))
    at = 0
    for out_ref in out_refs:
        out_ref[...] = got[at : at + out_ref.shape[0]].astype(BF16)
        at += out_ref.shape[0]


def unproject_kernel(flat, near, far, cuts):
    rows, width = flat.shape
    tokens = near.shape[1]
    tile = min(512, width)
    return pl.pallas_call(
        unproject_body,
        grid=(width // tile,),
        in_specs=[
            pl.BlockSpec((rows // 2, tokens), lambda i: (0, 0)),
            pl.BlockSpec((rows // 2, tokens), lambda i: (0, 0)),
            pl.BlockSpec((rows, tile), lambda i: (0, i)),
        ],
        out_specs=[pl.BlockSpec((cut, tile), lambda i: (0, i)) for cut in cuts],
        out_shape=[jax.ShapeDtypeStruct((cut, width), BF16) for cut in cuts],
        scratch_shapes=[pltpu.VMEM((tokens, rows), BF16)],
        compiler_params=pltpu.CompilerParams(vmem_limit_bytes=14 * MIB),
        cost_estimate=SMALL,
    )(near, far, flat)


def add_body(heights, *refs):
    out_refs = refs[sum(heights) :]
    groups, at = [], 0
    for height in heights:
        groups.append(refs[at : at + height])
        at += height
    tops = [[sum(r.shape[0] for r in group[:n]) for n in range(len(group) + 1)] for group in groups]
    height = out_refs[0].shape[0]
    edges = {edge for top in tops for edge in top} | {n * height for n in range(len(out_refs) + 1)}
    edges = sorted(edges)
    for low, high in zip(edges[:-1], edges[1:]):
        total = None
        for group, top in zip(groups, tops):
            for n, ref in enumerate(group):
                if top[n] <= low and high <= top[n + 1]:
                    part = ref[low - top[n] : high - top[n], :].astype(F32)
                    total = part if total is None else total + part
        out_refs[low // height][low % height : low % height + high - low, :] = total.astype(BF16)


def add_kernel(*groups, cut=1):
    rows, width = sum(x.shape[0] for x in groups[0]) // cut, groups[0][0].shape[1]
    tile = min(1024, width)
    arrays = [x for group in groups for x in group]
    return pl.pallas_call(
        functools.partial(add_body, [len(group) for group in groups]),
        grid=(width // tile,),
        in_specs=[pl.BlockSpec((x.shape[0], tile), lambda i: (0, i)) for x in arrays],
        out_specs=[pl.BlockSpec((rows, tile), lambda i: (0, i))] * cut,
        out_shape=[jax.ShapeDtypeStruct((rows, width), BF16)] * cut,
        compiler_params=pltpu.CompilerParams(vmem_limit_bytes=8 * MIB),
        cost_estimate=SMALL,
    )(*arrays)


def copy_body(in_ref, out_ref):
    out_ref[...] = in_ref[...]


def copy_kernel(x):
    rows, width = x.shape
    tile = rows // 4
    return pl.pallas_call(
        copy_body,
        grid=(4,),
        in_specs=[pl.BlockSpec((tile, width), lambda i: (i, 0))],
        out_specs=pl.BlockSpec((tile, width), lambda i: (i, 0)),
        out_shape=jax.ShapeDtypeStruct(x.shape, x.dtype),
        compiler_params=pltpu.CompilerParams(vmem_limit_bytes=8 * MIB),
        cost_estimate=SMALL,
    )(x)


def on_device(ring, n_tp, tokens_in, w_query, w_key, w_value, short_taps, long_taps, grad_out):
    chips = len(ring)
    half = chips // 2
    n_ctx = 2 * chips
    held, width = tokens_in.shape
    channels = w_query.shape[1]
    weights = (w_query, w_key, w_value)

    def one_way(x, turned=False, to_mate=False):
        hops = []
        for j in range(chips):
            for core in range(2):
                chip = ring[(j + (1 if (core == 0) != turned else -1)) % chips]
                hops.append((2 * ring[j] + core, 2 * chip + (core ^ int(to_mate))))
        return lax.ppermute(x, "ctx", hops)

    def swap(x):
        return lax.ppermute(x, "ctx", [(d, d ^ 1) for d in range(n_ctx)])

    table = np.zeros((n_ctx, n_ctx), np.int32)
    for device in range(n_ctx):
        place, core = ring.index(device // 2), device % 2
        way = -1 if core == 0 else 1
        items = [(0, 0), (0, 1)]
        for s in range(1, half):
            items += [(way * s, 0), (way * s, 1), (-way * s, 1), (-way * s, 0)]
        items += [(half, 0), (half, 1)]
        table[device] = [2 * ring[(place + hop) % chips] + (core ^ other) for hop, other in items]
    order = lax.dynamic_index_in_dim(jnp.asarray(table), lax.axis_index("ctx"), 0, keepdims=False)
    short_kernel, long_kernel = short_taps.reshape(3, -1, SHORT), long_taps.reshape(-1, LONG)

    stay = 3 * channels
    if n_tp == 2:
        t = lax.axis_index("tp").astype(jnp.int32)
        t, order, short_kernel, long_kernel = lax.optimization_barrier((t, order, short_kernel, long_kernel))
        flat = restack(t, weights)
    else:
        flat = jnp.stack(weights).reshape(-1, width)

    def project(pieces):
        if n_tp == 2:
            return project_kernel(flat, pieces)
        y = dot(flat, jnp.concatenate(pieces, axis=0), ((1,), (1,))).astype(BF16).reshape(3, n_tp, channels, -1)
        return lax.psum_scatter(y, "tp", scatter_dimension=1, tiled=True).reshape(stay, -1), None

    def across(x):
        return None if x is None else lax.ppermute(x, "tp", [(0, 1), (1, 0)])

    def meet(d):
        if n_tp == 2:
            return d.reshape(stay, -1), across(d.reshape(stay, -1))
        d = lax.all_gather(d.reshape(3, 1, channels, -1), "tp", axis=1, tiled=True)
        return (d.reshape(-1, d.shape[-1]),)

    def unproject(d, *cuts):
        if n_tp == 2:
            return unproject_kernel(flat, *d, cuts)
        y = dot(d[0], flat, ((0,), (0,))).astype(BF16)
        return jnp.split(y, np.cumsum(cuts)[:-1], axis=0)

    stage = lax.optimization_barrier

    arrived = [one_way(tokens_in), one_way(tokens_in, to_mate=True, turned=True)]
    near, far = project([tokens_in, swap(tokens_in)])
    arrived, near, far = stage((arrived, near, far))
    arrived = jnp.concatenate(arrived, axis=0)
    projected = []
    for s in range(1, half):
        coming = one_way(arrived if s < half - 1 else arrived[:held])
        projected.append((near, across(far)))
        near, far = project([arrived, swap(arrived)])
        if s < half - 1:
            arrived, near, far, projected[-1] = stage((coming, near, far, projected[-1]))
    crossed = across(far)
    arrived, near = stage((coming, near))
    shared, projected[-1] = stage((arrived, projected[-1]))
    mates = [swap(shared[: held // 2]), swap(shared[held // 2 :])]
    grad_out, mates = stage((grad_out, mates))
    incoming = lax.all_to_all(
        grad_out.reshape(n_ctx, channels, held), "ctx", split_axis=0, concat_axis=0, tiled=True
    )
    last, far = project([arrived, *mates])
    far, crossed = stage((far, crossed))
    projected += [(near, crossed), (last, across(far))]

    mixed, d_proj, grad_short, grad_long = mix(
        order,
        short_kernel,
        long_kernel,
        incoming,
        [[y.reshape(3, channels, -1) for y in side] for side in zip(*projected) if side[0] is not None],
        [[s] for s in range(half + 1)],
    )

    first, met, later = [meet(d_proj[s]) for s in (half, half - 1, half - 2)]
    mixed, first = stage((mixed, first))
    mixed_out = lax.all_to_all(mixed, "ctx", split_axis=0, concat_axis=0, tiled=True).reshape(-1, held)
    keep, *give = unproject(first, held, held // 2, held // 2)
    total = add_kernel([keep], [swap(x) for x in give])
    total, met, rest = stage((total, met, d_proj[: half - 2]))
    for s in range(half - 1, 0, -1):
        coming = one_way(total[0], turned=True)
        if s < half - 1:
            later = meet(rest[-1])
            rest = rest[:-1]
        cuts = (96, 80, 80) if s == half - 1 and held == 128 else (held, held)
        keep, *give = unproject(met, 2 * held, *cuts)
        give, later = stage((give, later))
        total = add_kernel([keep], [swap(x) for x in give], [coming], cut=2 if s == 1 else 1)
        if s == half - 2:
            mixed_out = copy_kernel(mixed_out)
        total, met, rest, mixed_out = stage((total, later, rest, mixed_out))
    coming = [one_way(total[0], turned=True), one_way(total[1], turned=True, to_mate=True)]
    keep, *give = unproject(met, held, held // 2, held // 2)
    (grad_tokens,) = add_kernel([keep], [swap(x) for x in give], coming[:1], coming[1:])
    return (
        mixed_out,
        grad_tokens,
        grad_short.reshape(3, 1, -1, SHORT),
        grad_long.reshape(1, -1, LONG),
    )


def solution(mesh):
    placed = (
        P("ctx", "tp"),
        P(None, "ctx", "tp"),
        P(None, "ctx", "tp"),
        P(None, "ctx", "tp"),
        P(None, "tp", "ctx", None),
        P("tp", "ctx", None),
        P("tp", "ctx"),
    )
    return jax.shard_map(
        functools.partial(on_device, ring_of(mesh), mesh.shape["tp"]),
        mesh=mesh,
        in_specs=placed,
        out_specs=(
            P("tp", "ctx"),
            P("ctx", "tp"),
            P(None, "tp", "ctx", None),
            P("tp", "ctx", None),
        ),
        check_vma=False,
    )
```

```python
import functools

import jax
import jax.numpy as jnp
import numpy as np
from jax import lax
from jax.experimental import pallas as pl
from jax.experimental.pallas import tpu as pltpu
from jax.sharding import PartitionSpec as P

GROUP = 16
SHORT = 3
LONG = 128
F32 = jnp.float32
BF16 = jnp.bfloat16
MIB = 1024 * 1024
SMALL = pl.CostEstimate(flops=1, bytes_accessed=1, transcendentals=0)


def ring_of(mesh):
    chips = mesh.shape["ctx"] // 2
    plain = list(range(chips))
    devices = np.asarray(mesh.devices).reshape(mesh.shape["ctx"], -1)[:, 0]
    places = [getattr(devices[2 * chip], "coords", None) for chip in plain]
    if any(place is None for place in places):
        return plain
    places = np.array([list(place)[:3] for place in places])
    axes = [axis for axis in range(3) if len(set(places[:, axis])) > 1]
    if len(axes) != 2:
        return plain
    rung = min(axes, key=lambda axis: len(set(places[:, axis])))
    along = axes[0] if rung == axes[1] else axes[1]
    sides = sorted(set(places[:, rung]))
    if len(sides) != 2:
        return plain
    there = [c for c in plain if places[c, rung] == sides[0]]
    back = [c for c in plain if places[c, rung] == sides[1]]
    there.sort(key=lambda c: places[c, along])
    back.sort(key=lambda c: -places[c, along])
    return there + back


def dot(a, b, dims):
    return lax.dot_general(a, b, (dims, ((), ())), preferred_element_type=F32)


def mix_body(count, sets, per_step, grouped, order, short_ref, long_ref, g_ref, *refs):
    proj_refs = [refs[s * count : (s + 1) * count] for s in range(sets)]
    refs = refs[sets * count :]
    d_count = len(grouped)
    mixed_ref, d_refs, gs_ref, gl_ref = refs[0], refs[1 : 1 + d_count], refs[1 + d_count], refs[2 + d_count]
    p_s, x_s, y_s, d_s, e_s = refs[3 + d_count :]
    blocks = g_ref.shape[0]
    rows = blocks * GROUP
    step = pl.program_id(0)

    @pl.when(step == 0)
    def _():
        p_s[:, :, 0:GROUP, :] = jnp.zeros((per_step, 3, GROUP, LONG), F32)
        x_s[:, 0:GROUP, :] = jnp.zeros((per_step, GROUP, LONG), BF16)
        y_s[:, rows:, :] = jnp.zeros((per_step, GROUP, LONG), BF16)
        d_s[:, :, rows:, :] = jnp.zeros((per_step, 3, GROUP, LONG), F32)

    halves = [(a, h) for a in range(count) for h in range(proj_refs[0][a].shape[2] // LONG)]
    places = [(a, h, where) for where, (a, h) in enumerate(halves)]
    d_places = []
    for b, arrays in enumerate(grouped):
        inside = [where for array in arrays for a, _, where in places if a == array]
        d_places += [(b, h, where) for h, where in enumerate(inside)]
    lane = lax.broadcasted_iota(jnp.int32, (rows, LONG), 1)
    sub8 = lax.broadcasted_iota(jnp.int32, (8, LONG), 0)
    col = lax.broadcasted_iota(jnp.int32, (LONG, LONG), 1)
    row = lax.broadcasted_iota(jnp.int32, (LONG, LONG), 0)

    every = range(per_step)
    mine = [slice(j * GROUP, (j + 1) * GROUP) for j in every]
    taps = [
        [[short_ref[i, step * per_step + j, k] for k in range(SHORT)] for i in range(3)] for j in every
    ]
    for a, h, where in places:
        at = pl.multiple_of((order[where] + 1) * GROUP, GROUP)
        for j in every:
            for i in range(3):
                part = proj_refs[0][a][i, mine[j], h * LONG : (h + 1) * LONG].astype(F32)
                for s in range(1, sets):
                    part = part + proj_refs[s][a][i, mine[j], h * LONG : (h + 1) * LONG].astype(F32)
                p_s[j, i, pl.ds(at, GROUP), :] = part

    feats = []
    for j in every:
        feat = []
        for i in range(3):
            whole = p_s[j, i]
            one = pltpu.roll(whole, 1, 1)
            two = pltpu.roll(whole, 2, 1)
            one = jnp.where(lane < 1, one[:rows], one[GROUP:])
            two = jnp.where(lane < 2, two[:rows], two[GROUP:])
            feat.append(taps[j][i][0] * whole[GROUP:] + taps[j][i][1] * one + taps[j][i][2] * two)
        feats.append(feat)
        x_s[j, GROUP:, :] = (feat[1] * feat[2]).astype(BF16)

    filters = []
    for j in every:
        base = jnp.broadcast_to(long_ref[0, j : j + 1, :], (8, LONG))
        for bit in (1, 2, 4):
            base = jnp.where((sub8 & bit) != 0, pltpu.roll(base, bit, 1), base)
        full = jnp.concatenate([base] + [pltpu.roll(base, 8 * m, 1) for m in range(1, LONG // 8)], axis=0)
        near = jnp.where(col >= row, full, 0.0).astype(BF16)
        far = jnp.where(col < row, full, 0.0).astype(BF16)
        filters.append((near, far))

    x_twos = [jnp.concatenate([x_s[j, GROUP:, :], x_s[j, :rows, :]], axis=1) for j in every]
    inners = [dot(x_twos[j], jnp.concatenate(filters[j], axis=0), ((1,), (0,))) for j in every]
    d_queries = []
    for j in every:
        g = g_ref[:, mine[j], :].reshape(rows, LONG).astype(F32)
        mixed_ref[:, mine[j], :] = (feats[j][0] * inners[j]).astype(BF16).reshape(blocks, GROUP, LONG)
        y_s[j, :rows, :] = (g * feats[j][0]).astype(BF16)
        d_queries.append(g * inners[j])
    d_products = []
    for j in every:
        y_two = jnp.concatenate([y_s[j, :rows, :], y_s[j, GROUP:, :]], axis=1)
        d_products.append(dot(y_two, jnp.concatenate(filters[j], axis=1), ((1,), (1,))))
    folds = [dot(y_s[j, :rows, :], x_twos[j], ((0,), (0,))) for j in every]
    for j in every:
        fold = jnp.where(col <= row, folds[j][:, :LONG], folds[j][:, LONG:])
        width = LONG
        while width > 8:
            width //= 2
            fold = fold[:width] + pltpu.roll(fold[width:], LONG - width, 1)
        for bit in (4, 2, 1):
            fold = jnp.where((sub8 & bit) != 0, pltpu.roll(fold, LONG - bit, 1), fold)
        gl_ref[0, j : j + 1, :] = jnp.sum(fold, axis=0, keepdims=True)

    for j in every:
        for i, d in enumerate((d_queries[j], d_products[j] * feats[j][2], d_products[j] * feats[j][1])):
            d_s[j, i, :rows, :] = d
            whole = d_s[j, i]
            one = pltpu.roll(whole, LONG - 1, 1)
            two = pltpu.roll(whole, LONG - 2, 1)
            one = jnp.where(lane >= LONG - 1, one[GROUP:], one[:rows])
            two = jnp.where(lane >= LONG - 2, two[GROUP:], two[:rows])
            p = p_s[j, i, GROUP:, :]
            for k, moved in enumerate((d, one, two)):
                gs_ref[0, j, 3 * i + k : 3 * i + k + 1, :] = jnp.sum(p * moved, axis=0, keepdims=True)
            e_s[j, i] = (taps[j][i][0] * d + taps[j][i][1] * one + taps[j][i][2] * two).astype(BF16)
    for a, h, where in d_places:
        at = pl.multiple_of(order[where] * GROUP, GROUP)
        for j in every:
            for i in range(3):
                d_refs[a][i, mine[j], h * LONG : (h + 1) * LONG] = e_s[j, i, pl.ds(at, GROUP), :]


def mix(order, short_kernel, long_kernel, g, proj_sets, grouped):
    blocks, channels, _ = g.shape
    count, sets = len(proj_sets[0]), len(proj_sets)
    groups = channels // GROUP
    per_step = next(n for n in (2, 1) if groups % n == 0)
    steps = groups // per_step
    rows = blocks * GROUP
    high = per_step * GROUP
    proj_specs = [pl.BlockSpec((3, high, x.shape[2]), lambda i, o: (0, i, 0)) for x in proj_sets[0]]
    d_widths = [sum(proj_sets[0][a].shape[2] for a in arrays) for arrays in grouped]
    d_specs = [pl.BlockSpec((3, high, w), lambda i, o: (0, i, 0)) for w in d_widths]
    token_spec = pl.BlockSpec((blocks, high, LONG), lambda i, o: (0, i, 0))
    outs = pl.pallas_call(
        functools.partial(mix_body, count, sets, per_step, grouped),
        grid_spec=pltpu.PrefetchScalarGridSpec(
            num_scalar_prefetch=1,
            grid=(steps,),
            in_specs=[
                pl.BlockSpec(memory_space=pltpu.SMEM),
                pl.BlockSpec((1, per_step, LONG), lambda i, o: (i, 0, 0)),
                token_spec,
            ]
            + proj_specs * sets,
            out_specs=[token_spec]
            + d_specs
            + [
                pl.BlockSpec((1, per_step, 3 * SHORT, LONG), lambda i, o: (i, 0, 0, 0)),
                pl.BlockSpec((1, per_step, LONG), lambda i, o: (i, 0, 0)),
            ],
            scratch_shapes=[
                pltpu.VMEM((per_step, 3, rows + GROUP, LONG), F32),
                pltpu.VMEM((per_step, rows + GROUP, LONG), BF16),
                pltpu.VMEM((per_step, rows + GROUP, LONG), BF16),
                pltpu.VMEM((per_step, 3, rows + GROUP, LONG), F32),
                pltpu.VMEM((per_step, 3, rows, LONG), BF16),
            ],
        ),
        out_shape=[jax.ShapeDtypeStruct((blocks, channels, LONG), BF16)]
        + [jax.ShapeDtypeStruct((3, channels, w), BF16) for w in d_widths]
        + [
            jax.ShapeDtypeStruct((steps, per_step, 3 * SHORT, LONG), F32),
            jax.ShapeDtypeStruct((steps, per_step, LONG), F32),
        ],
        compiler_params=pltpu.CompilerParams(vmem_limit_bytes=58 * MIB),
        cost_estimate=SMALL,
    )(order, short_kernel, long_kernel.reshape(steps, per_step, LONG), g, *[x for s in proj_sets for x in s])
    mixed, d_proj, (gs, gl) = outs[0], outs[1:-2], outs[-2:]
    grad_short = jnp.sum(gs, axis=-1).reshape(groups, 3, SHORT).transpose(1, 0, 2)
    grad_long = jnp.roll(jnp.flip(gl.reshape(groups, LONG), axis=1), 1, axis=1)
    return mixed, d_proj, grad_short, grad_long


def restack_body(t_ref, *refs):
    out_ref = refs[3]
    for i in range(3):
        out_ref[0, i] = refs[i][0]


def restack(t, weights):
    _, channels, width = weights[0].shape
    tile = min(128, channels)

    def source(side, part, t):
        return (jnp.where(side == 0, t[0], 1 - t[0]), part, 0)

    return pl.pallas_call(
        restack_body,
        grid_spec=pltpu.PrefetchScalarGridSpec(
            num_scalar_prefetch=1,
            grid=(2, channels // tile),
            in_specs=[pl.BlockSpec((1, tile, width), source)] * 3,
            out_specs=pl.BlockSpec((1, 3, tile, width), lambda side, part, t: (side, 0, part, 0)),
        ),
        out_shape=jax.ShapeDtypeStruct((2, 3, channels, width), BF16),
        compiler_params=pltpu.CompilerParams(vmem_limit_bytes=16 * MIB),
        cost_estimate=SMALL,
    )(t.reshape(1), *weights).reshape(6 * channels, width)


def project_body(pieces, *refs):
    x_refs, w_ref = refs[:pieces], refs[pieces]
    far_ref, near_ref, x_s, sems = refs[pieces + 1 :]
    step, steps = pl.program_id(0), pl.num_programs(0)

    @pl.when(step == 0)
    def _():
        copies, at = [], 0
        for n, x in enumerate(x_refs):
            copies.append(pltpu.make_async_copy(x, x_s.at[pl.ds(at, x.shape[0])], sems.at[n]))
            at += x.shape[0]
        for copy in copies:
            copy.start()
        for copy in copies:
            copy.wait()

    got = dot(w_ref[...], x_s[...], ((1,), (1,))).astype(BF16)

    @pl.when(step < steps // 2)
    def _():
        far_ref[...] = got

    @pl.when(step >= steps // 2)
    def _():
        near_ref[...] = got


def project_kernel(flat, pieces):
    rows, width = flat.shape
    tokens = sum(x.shape[0] for x in pieces)
    tile = rows // 4
    half = jax.ShapeDtypeStruct((rows // 2, tokens), BF16)
    far, near = pl.pallas_call(
        functools.partial(project_body, len(pieces)),
        grid=(4,),
        in_specs=[pl.BlockSpec(memory_space=pl.ANY)] * len(pieces)
        + [pl.BlockSpec((tile, width), lambda i: ((i + 2) % 4, 0))],
        out_specs=[
            pl.BlockSpec((tile, tokens), lambda i: (jnp.minimum(i, 1), 0)),
            pl.BlockSpec((tile, tokens), lambda i: (jnp.maximum(i - 2, 0), 0)),
        ],
        out_shape=[half, half],
        scratch_shapes=[pltpu.VMEM((tokens, width), BF16), pltpu.SemaphoreType.DMA((len(pieces),))],
        compiler_params=pltpu.CompilerParams(vmem_limit_bytes=16 * MIB),
        cost_estimate=SMALL,
    )(*pieces, flat)
    return near, far


def unproject_body(near_ref, far_ref, w_ref, *refs):
    out_refs, d_s = refs[:-1], refs[-1]
    stay = near_ref.shape[0]

    @pl.when(pl.program_id(0) == 0)
    def _():
        d_s[:, 0:stay] = near_ref[...].T
        d_s[:, stay:] = far_ref[...].T

    got = dot(d_s[...], w_ref[...], ((1,), (0,)))
    at = 0
    for out_ref in out_refs:
        out_ref[...] = got[at : at + out_ref.shape[0]].astype(BF16)
        at += out_ref.shape[0]


def unproject_kernel(flat, near, far, cuts):
    rows, width = flat.shape
    tokens = near.shape[1]
    tile = min(512, width)
    return pl.pallas_call(
        unproject_body,
        grid=(width // tile,),
        in_specs=[
            pl.BlockSpec((rows // 2, tokens), lambda i: (0, 0)),
            pl.BlockSpec((rows // 2, tokens), lambda i: (0, 0)),
            pl.BlockSpec((rows, tile), lambda i: (0, i)),
        ],
        out_specs=[pl.BlockSpec((cut, tile), lambda i: (0, i)) for cut in cuts],
        out_shape=[jax.ShapeDtypeStruct((cut, width), BF16) for cut in cuts],
        scratch_shapes=[pltpu.VMEM((tokens, rows), BF16)],
        compiler_params=pltpu.CompilerParams(vmem_limit_bytes=14 * MIB),
        cost_estimate=SMALL,
    )(near, far, flat)


def add_body(heights, *refs):
    out_refs = refs[sum(heights) :]
    groups, at = [], 0
    for height in heights:
        groups.append(refs[at : at + height])
        at += height
    tops = [[sum(r.shape[0] for r in group[:n]) for n in range(len(group) + 1)] for group in groups]
    height = out_refs[0].shape[0]
    edges = {edge for top in tops for edge in top} | {n * height for n in range(len(out_refs) + 1)}
    edges = sorted(edges)
    for low, high in zip(edges[:-1], edges[1:]):
        total = None
        for group, top in zip(groups, tops):
            for n, ref in enumerate(group):
                if top[n] <= low and high <= top[n + 1]:
                    part = ref[low - top[n] : high - top[n], :].astype(F32)
                    total = part if total is None else total + part
        out_refs[low // height][low % height : low % height + high - low, :] = total.astype(BF16)


def add_kernel(*groups, cut=1):
    rows, width = sum(x.shape[0] for x in groups[0]) // cut, groups[0][0].shape[1]
    tile = min(1024, width)
    arrays = [x for group in groups for x in group]
    return pl.pallas_call(
        functools.partial(add_body, [len(group) for group in groups]),
        grid=(width // tile,),
        in_specs=[pl.BlockSpec((x.shape[0], tile), lambda i: (0, i)) for x in arrays],
        out_specs=[pl.BlockSpec((rows, tile), lambda i: (0, i))] * cut,
        out_shape=[jax.ShapeDtypeStruct((rows, width), BF16)] * cut,
        compiler_params=pltpu.CompilerParams(vmem_limit_bytes=8 * MIB),
        cost_estimate=SMALL,
    )(*arrays)


def copy_body(in_ref, out_ref):
    out_ref[...] = in_ref[...]


def copy_kernel(x):
    rows, width = x.shape
    tile = rows // 4
    return pl.pallas_call(
        copy_body,
        grid=(4,),
        in_specs=[pl.BlockSpec((tile, width), lambda i: (i, 0))],
        out_specs=pl.BlockSpec((tile, width), lambda i: (i, 0)),
        out_shape=jax.ShapeDtypeStruct(x.shape, x.dtype),
        compiler_params=pltpu.CompilerParams(vmem_limit_bytes=8 * MIB),
        cost_estimate=SMALL,
    )(x)


def on_device(ring, n_tp, tokens_in, w_query, w_key, w_value, short_taps, long_taps, grad_out):
    chips = len(ring)
    half = chips // 2
    n_ctx = 2 * chips
    held, width = tokens_in.shape
    channels = w_query.shape[1]
    weights = (w_query, w_key, w_value)

    def one_way(x, turned=False, to_mate=False):
        hops = []
        for j in range(chips):
            for core in range(2):
                chip = ring[(j + (1 if (core == 0) != turned else -1)) % chips]
                hops.append((2 * ring[j] + core, 2 * chip + (core ^ int(to_mate))))
        return lax.ppermute(x, "ctx", hops)

    def swap(x):
        return lax.ppermute(x, "ctx", [(d, d ^ 1) for d in range(n_ctx)])

    table = np.zeros((n_ctx, n_ctx), np.int32)
    for device in range(n_ctx):
        place, core = ring.index(device // 2), device % 2
        way = -1 if core == 0 else 1
        items = [(0, 0), (0, 1)]
        for s in range(1, half):
            items += [(way * s, 0), (way * s, 1), (-way * s, 1), (-way * s, 0)]
        items += [(half, 0), (half, 1)]
        table[device] = [2 * ring[(place + hop) % chips] + (core ^ other) for hop, other in items]
    order = lax.dynamic_index_in_dim(jnp.asarray(table), lax.axis_index("ctx"), 0, keepdims=False)
    short_kernel, long_kernel = short_taps.reshape(3, -1, SHORT), long_taps.reshape(-1, LONG)

    stay = 3 * channels
    if n_tp == 2:
        t = lax.axis_index("tp").astype(jnp.int32)
        t, order, short_kernel, long_kernel = lax.optimization_barrier((t, order, short_kernel, long_kernel))
        flat = restack(t, weights)
    else:
        flat = jnp.stack(weights).reshape(-1, width)

    def project(pieces):
        if n_tp == 2:
            return project_kernel(flat, pieces)
        y = dot(flat, jnp.concatenate(pieces, axis=0), ((1,), (1,))).astype(BF16).reshape(3, n_tp, channels, -1)
        return lax.psum_scatter(y, "tp", scatter_dimension=1, tiled=True).reshape(stay, -1), None

    def across(x):
        return None if x is None else lax.ppermute(x, "tp", [(0, 1), (1, 0)])

    def meet(d):
        if n_tp == 2:
            return d.reshape(stay, -1), across(d.reshape(stay, -1))
        d = lax.all_gather(d.reshape(3, 1, channels, -1), "tp", axis=1, tiled=True)
        return (d.reshape(-1, d.shape[-1]),)

    def unproject(d, *cuts):
        if n_tp == 2:
            return unproject_kernel(flat, *d, cuts)
        y = dot(d[0], flat, ((0,), (0,))).astype(BF16)
        return jnp.split(y, np.cumsum(cuts)[:-1], axis=0)

    stage = lax.optimization_barrier

    arrived = [one_way(tokens_in), one_way(tokens_in, to_mate=True, turned=True)]
    near, far = project([tokens_in, swap(tokens_in)])
    arrived, near, far = stage((arrived, near, far))
    arrived = jnp.concatenate(arrived, axis=0)
    projected = []
    for s in range(1, half):
        coming = one_way(arrived if s < half - 1 else arrived[:held])
        projected.append((near, across(far)))
        near, far = project([arrived, swap(arrived)])
        if s < half - 1:
            arrived, near, far, projected[-1] = stage((coming, near, far, projected[-1]))
    crossed = across(far)
    arrived, near, grad_out = stage((coming, near, grad_out))
    incoming = lax.all_to_all(
        grad_out.reshape(n_ctx, channels, held), "ctx", split_axis=0, concat_axis=0, tiled=True
    )
    shared, projected[-1] = stage((arrived, projected[-1]))
    last, far = project([arrived, swap(shared[: held // 2]), swap(shared[held // 2 :])])
    far, crossed = stage((far, crossed))
    projected += [(near, crossed), (last, across(far))]

    mixed, d_proj, grad_short, grad_long = mix(
        order,
        short_kernel,
        long_kernel,
        incoming,
        [[y.reshape(3, channels, -1) for y in side] for side in zip(*projected) if side[0] is not None],
        [[s] for s in range(half + 1)],
    )

    first, met, later = [meet(d_proj[s]) for s in (half, half - 1, half - 2)]
    mixed_out = lax.all_to_all(mixed, "ctx", split_axis=0, concat_axis=0, tiled=True).reshape(-1, held)
    keep, *give = unproject(first, held, *((80, 48) if held == 128 else (held // 2, held // 2)))
    total = add_kernel([keep], [swap(x) for x in give])
    total, met, rest = stage((total, met, d_proj[: half - 2]))
    for s in range(half - 1, 0, -1):
        coming = one_way(total[0], turned=True)
        if s < half - 1:
            later = meet(rest[-1])
            rest = rest[:-1]
        cuts = (96, 80, 80) if s == half - 1 and held == 128 else (held, held)
        keep, *give = unproject(met, 2 * held, *cuts)
        give, later = stage((give, later))
        total = add_kernel([keep], [swap(x) for x in give], [coming], cut=2 if s == 1 else 1)
        if s == half - 2:
            mixed_out = copy_kernel(mixed_out)
        total, met, rest, mixed_out = stage((total, later, rest, mixed_out))
    coming = [one_way(total[0], turned=True), one_way(total[1], turned=True, to_mate=True)]
    keep, *give = unproject(met, held, held // 2, held // 2)
    (grad_tokens,) = add_kernel([keep], [swap(x) for x in give], coming[:1], coming[1:])
    return (
        mixed_out,
        grad_tokens,
        grad_short.reshape(3, 1, -1, SHORT),
        grad_long.reshape(1, -1, LONG),
    )


def solution(mesh):
    placed = (
        P("ctx", "tp"),
        P(None, "ctx", "tp"),
        P(None, "ctx", "tp"),
        P(None, "ctx", "tp"),
        P(None, "tp", "ctx", None),
        P("tp", "ctx", None),
        P("tp", "ctx"),
    )
    return jax.shard_map(
        functools.partial(on_device, ring_of(mesh), mesh.shape["tp"]),
        mesh=mesh,
        in_specs=placed,
        out_specs=(
            P("tp", "ctx"),
            P("ctx", "tp"),
            P(None, "tp", "ctx", None),
            P("tp", "ctx", None),
        ),
        check_vma=False,
    )
```

```python
import functools

import jax
import jax.numpy as jnp
import numpy as np
from jax import lax
from jax.experimental import pallas as pl
from jax.experimental.pallas import tpu as pltpu
from jax.sharding import PartitionSpec as P

GROUP = 16
SHORT = 3
LONG = 128
F32 = jnp.float32
BF16 = jnp.bfloat16
MIB = 1024 * 1024
SMALL = pl.CostEstimate(flops=1, bytes_accessed=1, transcendentals=0)


def ring_of(mesh):
    chips = mesh.shape["ctx"] // 2
    plain = list(range(chips))
    devices = np.asarray(mesh.devices).reshape(mesh.shape["ctx"], -1)[:, 0]
    places = [getattr(devices[2 * chip], "coords", None) for chip in plain]
    if any(place is None for place in places):
        return plain
    places = np.array([list(place)[:3] for place in places])
    axes = [axis for axis in range(3) if len(set(places[:, axis])) > 1]
    if len(axes) != 2:
        return plain
    rung = min(axes, key=lambda axis: len(set(places[:, axis])))
    along = axes[0] if rung == axes[1] else axes[1]
    sides = sorted(set(places[:, rung]))
    if len(sides) != 2:
        return plain
    there = [c for c in plain if places[c, rung] == sides[0]]
    back = [c for c in plain if places[c, rung] == sides[1]]
    there.sort(key=lambda c: places[c, along])
    back.sort(key=lambda c: -places[c, along])
    return there + back


def dot(a, b, dims):
    return lax.dot_general(a, b, (dims, ((), ())), preferred_element_type=F32)


def mix_body(count, sets, per_step, grouped, order, short_ref, long_ref, g_ref, *refs):
    proj_refs = [refs[s * count : (s + 1) * count] for s in range(sets)]
    refs = refs[sets * count :]
    d_count = len(grouped)
    mixed_ref, d_refs, gs_ref, gl_ref = refs[0], refs[1 : 1 + d_count], refs[1 + d_count], refs[2 + d_count]
    p_s, f_s, x_s, y_s, d_s, e_s = refs[3 + d_count :]
    blocks = g_ref.shape[0]
    rows = blocks * GROUP
    step = pl.program_id(0)

    @pl.when(step == 0)
    def _():
        x_s[:, 0:GROUP, :] = jnp.zeros((per_step, GROUP, LONG), BF16)
        y_s[:, rows:, :] = jnp.zeros((per_step, GROUP, LONG), BF16)

    halves = [(a, h) for a in range(count) for h in range(proj_refs[0][a].shape[2] // LONG)]
    places = [(a, h, where) for where, (a, h) in enumerate(halves)]
    d_places = []
    for b, arrays in enumerate(grouped):
        inside = [where for array in arrays for a, _, where in places if a == array]
        d_places += [(b, h, where) for h, where in enumerate(inside)]
    lane = lax.broadcasted_iota(jnp.int32, (GROUP, LONG), 1)
    zero = jnp.zeros((GROUP, LONG), F32)
    at_block = [slice(n * GROUP, (n + 1) * GROUP) for n in range(blocks)]
    sub8 = lax.broadcasted_iota(jnp.int32, (8, LONG), 0)
    col = lax.broadcasted_iota(jnp.int32, (LONG, LONG), 1)
    row = lax.broadcasted_iota(jnp.int32, (LONG, LONG), 0)

    every = range(per_step)
    mine = [slice(j * GROUP, (j + 1) * GROUP) for j in every]
    taps = [
        [[short_ref[i, step * per_step + j, k] for k in range(SHORT)] for i in range(3)] for j in every
    ]
    for a, h, where in places:
        at = pl.multiple_of(order[where] * GROUP, GROUP)
        for j in every:
            for i in range(3):
                part = proj_refs[0][a][i, mine[j], h * LONG : (h + 1) * LONG].astype(F32)
                for s in range(1, sets):
                    part = part + proj_refs[s][a][i, mine[j], h * LONG : (h + 1) * LONG].astype(F32)
                p_s[j, i, pl.ds(at, GROUP), :] = part

    for j in every:
        before = [(zero, zero)] * 3
        for at in at_block:
            feat = []
            for i in range(3):
                here = p_s[j, i, at, :]
                one = pltpu.roll(here, 1, 1)
                two = pltpu.roll(here, 2, 1)
                past_one = jnp.where(lane < 1, before[i][0], one)
                past_two = jnp.where(lane < 2, before[i][1], two)
                before[i] = (one, two)
                feat.append(taps[j][i][0] * here + taps[j][i][1] * past_one + taps[j][i][2] * past_two)
                f_s[j, i, at, :] = feat[i]
            x_s[j, at.stop : at.stop + GROUP, :] = (feat[1] * feat[2]).astype(BF16)

    filters = []
    for j in every:
        base = jnp.broadcast_to(long_ref[0, j : j + 1, :], (8, LONG))
        for bit in (1, 2, 4):
            base = jnp.where((sub8 & bit) != 0, pltpu.roll(base, bit, 1), base)
        full = jnp.concatenate([base] + [pltpu.roll(base, 8 * m, 1) for m in range(1, LONG // 8)], axis=0)
        near = jnp.where(col >= row, full, 0.0).astype(BF16)
        far = jnp.where(col < row, full, 0.0).astype(BF16)
        filters.append((near, far))

    x_twos = [jnp.concatenate([x_s[j, GROUP:, :], x_s[j, :rows, :]], axis=1) for j in every]
    inners = [dot(x_twos[j], jnp.concatenate(filters[j], axis=0), ((1,), (0,))) for j in every]
    for j in every:
        for n, at in enumerate(at_block):
            g = g_ref[n, mine[j], :].astype(F32)
            feat, inner = f_s[j, 0, at, :], inners[j][at]
            mixed_ref[n, mine[j], :] = (feat * inner).astype(BF16)
            y_s[j, at, :] = (g * feat).astype(BF16)
            d_s[j, at, :] = g * inner
    d_products = []
    for j in every:
        y_two = jnp.concatenate([y_s[j, :rows, :], y_s[j, GROUP:, :]], axis=1)
        d_products.append(dot(y_two, jnp.concatenate(filters[j], axis=1), ((1,), (1,))))
    folds = [dot(y_s[j, :rows, :], x_twos[j], ((0,), (0,))) for j in every]
    for j in every:
        fold = jnp.where(col <= row, folds[j][:, :LONG], folds[j][:, LONG:])
        width = LONG
        while width > 8:
            width //= 2
            fold = fold[:width] + pltpu.roll(fold[width:], LONG - width, 1)
        for bit in (4, 2, 1):
            fold = jnp.where((sub8 & bit) != 0, pltpu.roll(fold, LONG - bit, 1), fold)
        gl_ref[0, j : j + 1, :] = jnp.sum(fold, axis=0, keepdims=True)

    for j in every:
        after = [(zero, zero)] * 3
        sums = [[zero] * SHORT for _ in range(3)]
        for at in at_block[::-1]:
            d_product = d_products[j][at]
            for i, d in enumerate((d_s[j, at, :], d_product * f_s[j, 2, at, :], d_product * f_s[j, 1, at, :])):
                one = pltpu.roll(d, LONG - 1, 1)
                two = pltpu.roll(d, LONG - 2, 1)
                next_one = jnp.where(lane >= LONG - 1, after[i][0], one)
                next_two = jnp.where(lane >= LONG - 2, after[i][1], two)
                after[i] = (one, two)
                p = p_s[j, i, at, :]
                sums[i] = [total + p * moved for total, moved in zip(sums[i], (d, next_one, next_two))]
                e_s[j, i, at, :] = (
                    taps[j][i][0] * d + taps[j][i][1] * next_one + taps[j][i][2] * next_two
                ).astype(BF16)
        for i in range(3):
            for k in range(SHORT):
                gs_ref[0, j, 3 * i + k : 3 * i + k + 1, :] = jnp.sum(sums[i][k], axis=0, keepdims=True)
    for a, h, where in d_places:
        at = pl.multiple_of(order[where] * GROUP, GROUP)
        for j in every:
            for i in range(3):
                d_refs[a][i, mine[j], h * LONG : (h + 1) * LONG] = e_s[j, i, pl.ds(at, GROUP), :]


def mix(order, short_kernel, long_kernel, g, proj_sets, grouped):
    blocks, channels, _ = g.shape
    count, sets = len(proj_sets[0]), len(proj_sets)
    groups = channels // GROUP
    per_step = next(n for n in (2, 1) if groups % n == 0)
    steps = groups // per_step
    rows = blocks * GROUP
    high = per_step * GROUP
    proj_specs = [pl.BlockSpec((3, high, x.shape[2]), lambda i, o: (0, i, 0)) for x in proj_sets[0]]
    d_widths = [sum(proj_sets[0][a].shape[2] for a in arrays) for arrays in grouped]
    d_specs = [pl.BlockSpec((3, high, w), lambda i, o: (0, i, 0)) for w in d_widths]
    token_spec = pl.BlockSpec((blocks, high, LONG), lambda i, o: (0, i, 0))
    outs = pl.pallas_call(
        functools.partial(mix_body, count, sets, per_step, grouped),
        grid_spec=pltpu.PrefetchScalarGridSpec(
            num_scalar_prefetch=1,
            grid=(steps,),
            in_specs=[
                pl.BlockSpec(memory_space=pltpu.SMEM),
                pl.BlockSpec((1, per_step, LONG), lambda i, o: (i, 0, 0)),
                token_spec,
            ]
            + proj_specs * sets,
            out_specs=[token_spec]
            + d_specs
            + [
                pl.BlockSpec((1, per_step, 3 * SHORT, LONG), lambda i, o: (i, 0, 0, 0)),
                pl.BlockSpec((1, per_step, LONG), lambda i, o: (i, 0, 0)),
            ],
            scratch_shapes=[
                pltpu.VMEM((per_step, 3, rows, LONG), F32),
                pltpu.VMEM((per_step, 3, rows, LONG), F32),
                pltpu.VMEM((per_step, rows + GROUP, LONG), BF16),
                pltpu.VMEM((per_step, rows + GROUP, LONG), BF16),
                pltpu.VMEM((per_step, rows, LONG), F32),
                pltpu.VMEM((per_step, 3, rows, LONG), BF16),
            ],
        ),
        out_shape=[jax.ShapeDtypeStruct((blocks, channels, LONG), BF16)]
        + [jax.ShapeDtypeStruct((3, channels, w), BF16) for w in d_widths]
        + [
            jax.ShapeDtypeStruct((steps, per_step, 3 * SHORT, LONG), F32),
            jax.ShapeDtypeStruct((steps, per_step, LONG), F32),
        ],
        compiler_params=pltpu.CompilerParams(vmem_limit_bytes=58 * MIB),
        cost_estimate=SMALL,
    )(order, short_kernel, long_kernel.reshape(steps, per_step, LONG), g, *[x for s in proj_sets for x in s])
    mixed, d_proj, (gs, gl) = outs[0], outs[1:-2], outs[-2:]
    grad_short = jnp.sum(gs, axis=-1).reshape(groups, 3, SHORT).transpose(1, 0, 2)
    grad_long = jnp.roll(jnp.flip(gl.reshape(groups, LONG), axis=1), 1, axis=1)
    return mixed, d_proj, grad_short, grad_long


def restack_body(t_ref, *refs):
    out_ref = refs[3]
    for i in range(3):
        out_ref[0, i] = refs[i][0]


def restack(t, weights):
    _, channels, width = weights[0].shape
    tile = min(128, channels)

    def source(side, part, t):
        return (jnp.where(side == 0, t[0], 1 - t[0]), part, 0)

    return pl.pallas_call(
        restack_body,
        grid_spec=pltpu.PrefetchScalarGridSpec(
            num_scalar_prefetch=1,
            grid=(2, channels // tile),
            in_specs=[pl.BlockSpec((1, tile, width), source)] * 3,
            out_specs=pl.BlockSpec((1, 3, tile, width), lambda side, part, t: (side, 0, part, 0)),
        ),
        out_shape=jax.ShapeDtypeStruct((2, 3, channels, width), BF16),
        compiler_params=pltpu.CompilerParams(vmem_limit_bytes=16 * MIB),
        cost_estimate=SMALL,
    )(t.reshape(1), *weights).reshape(6 * channels, width)


def project_body(pieces, *refs):
    x_refs, w_ref = refs[:pieces], refs[pieces]
    far_ref, near_ref, x_s, sems = refs[pieces + 1 :]
    step, steps = pl.program_id(0), pl.num_programs(0)

    @pl.when(step == 0)
    def _():
        copies, at = [], 0
        for n, x in enumerate(x_refs):
            copies.append(pltpu.make_async_copy(x, x_s.at[pl.ds(at, x.shape[0])], sems.at[n]))
            at += x.shape[0]
        for copy in copies:
            copy.start()
        for copy in copies:
            copy.wait()

    got = dot(w_ref[...], x_s[...], ((1,), (1,))).astype(BF16)

    @pl.when(step < steps // 2)
    def _():
        far_ref[...] = got

    @pl.when(step >= steps // 2)
    def _():
        near_ref[...] = got


def project_kernel(flat, pieces):
    rows, width = flat.shape
    tokens = sum(x.shape[0] for x in pieces)
    tile = rows // 4
    half = jax.ShapeDtypeStruct((rows // 2, tokens), BF16)
    far, near = pl.pallas_call(
        functools.partial(project_body, len(pieces)),
        grid=(4,),
        in_specs=[pl.BlockSpec(memory_space=pl.ANY)] * len(pieces)
        + [pl.BlockSpec((tile, width), lambda i: ((i + 2) % 4, 0))],
        out_specs=[
            pl.BlockSpec((tile, tokens), lambda i: (jnp.minimum(i, 1), 0)),
            pl.BlockSpec((tile, tokens), lambda i: (jnp.maximum(i - 2, 0), 0)),
        ],
        out_shape=[half, half],
        scratch_shapes=[pltpu.VMEM((tokens, width), BF16), pltpu.SemaphoreType.DMA((len(pieces),))],
        compiler_params=pltpu.CompilerParams(vmem_limit_bytes=16 * MIB),
        cost_estimate=SMALL,
    )(*pieces, flat)
    return near, far


def unproject_body(near_ref, far_ref, w_ref, *refs):
    out_refs, d_s = refs[:-1], refs[-1]
    stay = near_ref.shape[0]

    @pl.when(pl.program_id(0) == 0)
    def _():
        d_s[:, 0:stay] = near_ref[...].T
        d_s[:, stay:] = far_ref[...].T

    got = dot(d_s[...], w_ref[...], ((1,), (0,)))
    at = 0
    for out_ref in out_refs:
        out_ref[...] = got[at : at + out_ref.shape[0]].astype(BF16)
        at += out_ref.shape[0]


def unproject_kernel(flat, near, far, cuts):
    rows, width = flat.shape
    tokens = near.shape[1]
    tile = min(1024, width)
    return pl.pallas_call(
        unproject_body,
        grid=(width // tile,),
        in_specs=[
            pl.BlockSpec((rows // 2, tokens), lambda i: (0, 0)),
            pl.BlockSpec((rows // 2, tokens), lambda i: (0, 0)),
            pl.BlockSpec((rows, tile), lambda i: (0, i)),
        ],
        out_specs=[pl.BlockSpec((cut, tile), lambda i: (0, i)) for cut in cuts],
        out_shape=[jax.ShapeDtypeStruct((cut, width), BF16) for cut in cuts],
        scratch_shapes=[pltpu.VMEM((tokens, rows), BF16)],
        compiler_params=pltpu.CompilerParams(vmem_limit_bytes=20 * MIB),
        cost_estimate=SMALL,
    )(near, far, flat)


def add_body(heights, *refs):
    out_refs = refs[sum(heights) :]
    groups, at = [], 0
    for height in heights:
        groups.append(refs[at : at + height])
        at += height
    tops = [[sum(r.shape[0] for r in group[:n]) for n in range(len(group) + 1)] for group in groups]
    height = out_refs[0].shape[0]
    edges = {edge for top in tops for edge in top} | {n * height for n in range(len(out_refs) + 1)}
    edges = sorted(edges)
    for low, high in zip(edges[:-1], edges[1:]):
        total = None
        for group, top in zip(groups, tops):
            for n, ref in enumerate(group):
                if top[n] <= low and high <= top[n + 1]:
                    part = ref[low - top[n] : high - top[n], :].astype(F32)
                    total = part if total is None else total + part
        out_refs[low // height][low % height : low % height + high - low, :] = total.astype(BF16)


def add_kernel(*groups, cut=1):
    rows, width = sum(x.shape[0] for x in groups[0]) // cut, groups[0][0].shape[1]
    tile = min(1024, width)
    arrays = [x for group in groups for x in group]
    return pl.pallas_call(
        functools.partial(add_body, [len(group) for group in groups]),
        grid=(width // tile,),
        in_specs=[pl.BlockSpec((x.shape[0], tile), lambda i: (0, i)) for x in arrays],
        out_specs=[pl.BlockSpec((rows, tile), lambda i: (0, i))] * cut,
        out_shape=[jax.ShapeDtypeStruct((rows, width), BF16)] * cut,
        compiler_params=pltpu.CompilerParams(vmem_limit_bytes=8 * MIB),
        cost_estimate=SMALL,
    )(*arrays)


def copy_body(in_ref, out_ref):
    out_ref[...] = in_ref[...]


def copy_kernel(x):
    rows, width = x.shape
    tile = rows // 4
    return pl.pallas_call(
        copy_body,
        grid=(4,),
        in_specs=[pl.BlockSpec((tile, width), lambda i: (i, 0))],
        out_specs=pl.BlockSpec((tile, width), lambda i: (i, 0)),
        out_shape=jax.ShapeDtypeStruct(x.shape, x.dtype),
        compiler_params=pltpu.CompilerParams(vmem_limit_bytes=8 * MIB),
        cost_estimate=SMALL,
    )(x)


def on_device(ring, n_tp, tokens_in, w_query, w_key, w_value, short_taps, long_taps, grad_out):
    chips = len(ring)
    half = chips // 2
    n_ctx = 2 * chips
    held, width = tokens_in.shape
    channels = w_query.shape[1]
    weights = (w_query, w_key, w_value)

    def one_way(x, turned=False, to_mate=False):
        hops = []
        for j in range(chips):
            for core in range(2):
                chip = ring[(j + (1 if (core == 0) != turned else -1)) % chips]
                hops.append((2 * ring[j] + core, 2 * chip + (core ^ int(to_mate))))
        return lax.ppermute(x, "ctx", hops)

    def swap(x):
        return lax.ppermute(x, "ctx", [(d, d ^ 1) for d in range(n_ctx)])

    table = np.zeros((n_ctx, n_ctx), np.int32)
    for device in range(n_ctx):
        place, core = ring.index(device // 2), device % 2
        way = -1 if core == 0 else 1
        items = [(0, 0), (0, 1)]
        for s in range(1, half):
            items += [(way * s, 0), (way * s, 1), (-way * s, 1), (-way * s, 0)]
        items += [(half, 0), (half, 1)]
        table[device] = [2 * ring[(place + hop) % chips] + (core ^ other) for hop, other in items]
    order = lax.dynamic_index_in_dim(jnp.asarray(table), lax.axis_index("ctx"), 0, keepdims=False)
    short_kernel, long_kernel = short_taps.reshape(3, -1, SHORT), long_taps.reshape(-1, LONG)

    stay = 3 * channels
    if n_tp == 2:
        t = lax.axis_index("tp").astype(jnp.int32)
        t, order, short_kernel, long_kernel = lax.optimization_barrier((t, order, short_kernel, long_kernel))
        flat = restack(t, weights)
    else:
        flat = jnp.stack(weights).reshape(-1, width)

    def project(pieces):
        if n_tp == 2:
            return project_kernel(flat, pieces)
        y = dot(flat, jnp.concatenate(pieces, axis=0), ((1,), (1,))).astype(BF16).reshape(3, n_tp, channels, -1)
        return lax.psum_scatter(y, "tp", scatter_dimension=1, tiled=True).reshape(stay, -1), None

    def across(x):
        return None if x is None else lax.ppermute(x, "tp", [(0, 1), (1, 0)])

    def meet(d):
        if n_tp == 2:
            return d.reshape(stay, -1), across(d.reshape(stay, -1))
        d = lax.all_gather(d.reshape(3, 1, channels, -1), "tp", axis=1, tiled=True)
        return (d.reshape(-1, d.shape[-1]),)

    def unproject(d, *cuts):
        if n_tp == 2:
            return unproject_kernel(flat, *d, cuts)
        y = dot(d[0], flat, ((0,), (0,))).astype(BF16)
        return jnp.split(y, np.cumsum(cuts)[:-1], axis=0)

    stage = lax.optimization_barrier

    arrived = [one_way(tokens_in), one_way(tokens_in, to_mate=True, turned=True)]
    near, far = project([tokens_in, swap(tokens_in)])
    arrived, near, far = stage((arrived, near, far))
    arrived = jnp.concatenate(arrived, axis=0)
    projected = []
    for s in range(1, half):
        coming = one_way(arrived if s < half - 1 else arrived[:held])
        projected.append((near, across(far)))
        near, far = project([arrived, swap(arrived)])
        if s < half - 1:
            arrived, near, far, projected[-1] = stage((coming, near, far, projected[-1]))
    crossed = across(far)
    arrived, near, grad_out = stage((coming, near, grad_out))
    incoming = lax.all_to_all(
        grad_out.reshape(n_ctx, channels, held), "ctx", split_axis=0, concat_axis=0, tiled=True
    )
    shared, projected[-1] = stage((arrived, projected[-1]))
    last, far = project([arrived, swap(shared[: held // 2]), swap(shared[held // 2 :])])
    far, crossed = stage((far, crossed))
    projected += [(near, crossed), (last, across(far))]

    mixed, d_proj, grad_short, grad_long = mix(
        order,
        short_kernel,
        long_kernel,
        incoming,
        [[y.reshape(3, channels, -1) for y in side] for side in zip(*projected) if side[0] is not None],
        [[s] for s in range(half + 1)],
    )

    first, met, later = [meet(d_proj[s]) for s in (half, half - 1, half - 2)]
    mixed_out = lax.all_to_all(mixed, "ctx", split_axis=0, concat_axis=0, tiled=True).reshape(-1, held)
    keep, *give = unproject(first, held, *((80, 48) if held == 128 else (held // 2, held // 2)))
    total = add_kernel([keep], [swap(x) for x in give])
    total, met, rest = stage((total, met, d_proj[: half - 2]))
    for s in range(half - 1, 0, -1):
        coming = one_way(total[0], turned=True)
        if s < half - 1:
            later = meet(rest[-1])
            rest = rest[:-1]
        cuts = (96, 96, 64) if s == half - 1 and held == 128 else (held, held)
        keep, *give = unproject(met, 2 * held, *cuts)
        give[-1], later = stage((give[-1], later))
        total = add_kernel([keep], [swap(x) for x in give], [coming], cut=2 if s == 1 else 1)
        if s == half - 2:
            mixed_out = copy_kernel(mixed_out)
        total, met, rest, mixed_out = stage((total, later, rest, mixed_out))
    coming = [one_way(total[0], turned=True), one_way(total[1], turned=True, to_mate=True)]
    keep, *give = unproject(met, held, held // 2, held // 2)
    (grad_tokens,) = add_kernel([keep], [swap(x) for x in give], coming[:1], coming[1:])
    return (
        mixed_out,
        grad_tokens,
        grad_short.reshape(3, 1, -1, SHORT),
        grad_long.reshape(1, -1, LONG),
    )


def solution(mesh):
    placed = (
        P("ctx", "tp"),
        P(None, "ctx", "tp"),
        P(None, "ctx", "tp"),
        P(None, "ctx", "tp"),
        P(None, "tp", "ctx", None),
        P("tp", "ctx", None),
        P("tp", "ctx"),
    )
    return jax.shard_map(
        functools.partial(on_device, ring_of(mesh), mesh.shape["tp"]),
        mesh=mesh,
        in_specs=placed,
        out_specs=(
            P("tp", "ctx"),
            P("ctx", "tp"),
            P(None, "tp", "ctx", None),
            P("tp", "ctx", None),
        ),
        check_vma=False,
    )
```

```python
import functools

import jax
import jax.numpy as jnp
import numpy as np
from jax import lax
from jax.experimental import pallas as pl
from jax.experimental.pallas import tpu as pltpu
from jax.sharding import PartitionSpec as P

GROUP = 16
SHORT = 3
LONG = 128
F32 = jnp.float32
BF16 = jnp.bfloat16
MIB = 1024 * 1024
SMALL = pl.CostEstimate(flops=1, bytes_accessed=1, transcendentals=0)


def ring_of(mesh):
    chips = mesh.shape["ctx"] // 2
    plain = list(range(chips))
    devices = np.asarray(mesh.devices).reshape(mesh.shape["ctx"], -1)[:, 0]
    places = [getattr(devices[2 * chip], "coords", None) for chip in plain]
    if any(place is None for place in places):
        return plain
    places = np.array([list(place)[:3] for place in places])
    axes = [axis for axis in range(3) if len(set(places[:, axis])) > 1]
    if len(axes) != 2:
        return plain
    rung = min(axes, key=lambda axis: len(set(places[:, axis])))
    along = axes[0] if rung == axes[1] else axes[1]
    sides = sorted(set(places[:, rung]))
    if len(sides) != 2:
        return plain
    there = [c for c in plain if places[c, rung] == sides[0]]
    back = [c for c in plain if places[c, rung] == sides[1]]
    there.sort(key=lambda c: places[c, along])
    back.sort(key=lambda c: -places[c, along])
    return there + back


def dot(a, b, dims):
    return lax.dot_general(a, b, (dims, ((), ())), preferred_element_type=F32)


def mix_body(count, sets, per_step, grouped, order, short_ref, long_ref, g_ref, *refs):
    proj_refs = [refs[s * count : (s + 1) * count] for s in range(sets)]
    refs = refs[sets * count :]
    d_count = len(grouped)
    mixed_ref, d_refs, gs_ref, gl_ref = refs[0], refs[1 : 1 + d_count], refs[1 + d_count], refs[2 + d_count]
    p_s, f_s, x_s, y_s, d_s, e_s = refs[3 + d_count :]
    blocks = g_ref.shape[0]
    rows = blocks * GROUP
    step = pl.program_id(0)

    @pl.when(step == 0)
    def _():
        x_s[:, 0:GROUP, :] = jnp.zeros((per_step, GROUP, LONG), BF16)
        y_s[:, rows:, :] = jnp.zeros((per_step, GROUP, LONG), BF16)

    halves = [(a, h) for a in range(count) for h in range(proj_refs[0][a].shape[2] // LONG)]
    places = [(a, h, where) for where, (a, h) in enumerate(halves)]
    d_places = []
    for b, arrays in enumerate(grouped):
        inside = [where for array in arrays for a, _, where in places if a == array]
        d_places += [(b, h, where) for h, where in enumerate(inside)]
    lane = lax.broadcasted_iota(jnp.int32, (GROUP, LONG), 1)
    zero = jnp.zeros((GROUP, LONG), F32)
    at_block = [slice(n * GROUP, (n + 1) * GROUP) for n in range(blocks)]
    sub8 = lax.broadcasted_iota(jnp.int32, (8, LONG), 0)
    col = lax.broadcasted_iota(jnp.int32, (LONG, LONG), 1)
    row = lax.broadcasted_iota(jnp.int32, (LONG, LONG), 0)

    every = range(per_step)
    mine = [slice(j * GROUP, (j + 1) * GROUP) for j in every]
    taps = [
        [[short_ref[i, step * per_step + j, k] for k in range(SHORT)] for i in range(3)] for j in every
    ]
    for a, h, where in places:
        at = pl.multiple_of(order[where] * GROUP, GROUP)
        for j in every:
            for i in range(3):
                part = proj_refs[0][a][i, mine[j], h * LONG : (h + 1) * LONG].astype(F32)
                for s in range(1, sets):
                    part = part + proj_refs[s][a][i, mine[j], h * LONG : (h + 1) * LONG].astype(F32)
                p_s[j, i, pl.ds(at, GROUP), :] = part

    for j in every:
        before = [(zero, zero)] * 3
        for at in at_block:
            feat = []
            for i in range(3):
                here = p_s[j, i, at, :]
                one = pltpu.roll(here, 1, 1)
                two = pltpu.roll(here, 2, 1)
                past_one = jnp.where(lane < 1, before[i][0], one)
                past_two = jnp.where(lane < 2, before[i][1], two)
                before[i] = (one, two)
                feat.append(taps[j][i][0] * here + taps[j][i][1] * past_one + taps[j][i][2] * past_two)
                f_s[j, i, at, :] = feat[i]
            x_s[j, at.stop : at.stop + GROUP, :] = (feat[1] * feat[2]).astype(BF16)

    filters = []
    for j in every:
        base = jnp.broadcast_to(long_ref[0, j : j + 1, :], (8, LONG))
        for bit in (1, 2, 4):
            base = jnp.where((sub8 & bit) != 0, pltpu.roll(base, bit, 1), base)
        full = jnp.concatenate([base] + [pltpu.roll(base, 8 * m, 1) for m in range(1, LONG // 8)], axis=0)
        near = jnp.where(col >= row, full, 0.0).astype(BF16)
        far = jnp.where(col < row, full, 0.0).astype(BF16)
        filters.append((near, far))

    x_twos = [jnp.concatenate([x_s[j, GROUP:, :], x_s[j, :rows, :]], axis=1) for j in every]
    inners = [dot(x_twos[j], jnp.concatenate(filters[j], axis=0), ((1,), (0,))) for j in every]
    for j in every:
        for n, at in enumerate(at_block):
            g = g_ref[n, mine[j], :].astype(F32)
            feat, inner = f_s[j, 0, at, :], inners[j][at]
            mixed_ref[n, mine[j], :] = (feat * inner).astype(BF16)
            y_s[j, at, :] = (g * feat).astype(BF16)
            d_s[j, at, :] = g * inner
    d_products = []
    for j in every:
        y_two = jnp.concatenate([y_s[j, :rows, :], y_s[j, GROUP:, :]], axis=1)
        d_products.append(dot(y_two, jnp.concatenate(filters[j], axis=1), ((1,), (1,))))
    folds = [dot(y_s[j, :rows, :], x_twos[j], ((0,), (0,))) for j in every]
    for j in every:
        fold = jnp.where(col <= row, folds[j][:, :LONG], folds[j][:, LONG:])
        width = LONG
        while width > 8:
            width //= 2
            fold = fold[:width] + pltpu.roll(fold[width:], LONG - width, 1)
        for bit in (4, 2, 1):
            fold = jnp.where((sub8 & bit) != 0, pltpu.roll(fold, LONG - bit, 1), fold)
        gl_ref[0, j : j + 1, :] = jnp.sum(fold, axis=0, keepdims=True)

    for j in every:
        after = [(zero, zero)] * 3
        sums = [[zero] * SHORT for _ in range(3)]
        for at in at_block[::-1]:
            d_product = d_products[j][at]
            for i, d in enumerate((d_s[j, at, :], d_product * f_s[j, 2, at, :], d_product * f_s[j, 1, at, :])):
                one = pltpu.roll(d, LONG - 1, 1)
                two = pltpu.roll(d, LONG - 2, 1)
                next_one = jnp.where(lane >= LONG - 1, after[i][0], one)
                next_two = jnp.where(lane >= LONG - 2, after[i][1], two)
                after[i] = (one, two)
                p = p_s[j, i, at, :]
                sums[i] = [total + p * moved for total, moved in zip(sums[i], (d, next_one, next_two))]
                e_s[j, i, at, :] = (
                    taps[j][i][0] * d + taps[j][i][1] * next_one + taps[j][i][2] * next_two
                ).astype(BF16)
        for i in range(3):
            for k in range(SHORT):
                gs_ref[0, j, 3 * i + k : 3 * i + k + 1, :] = jnp.sum(sums[i][k], axis=0, keepdims=True)
    for a, h, where in d_places:
        at = pl.multiple_of(order[where] * GROUP, GROUP)
        for j in every:
            for i in range(3):
                d_refs[a][i, mine[j], h * LONG : (h + 1) * LONG] = e_s[j, i, pl.ds(at, GROUP), :]


def mix(order, short_kernel, long_kernel, g, proj_sets, grouped):
    blocks, channels, _ = g.shape
    count, sets = len(proj_sets[0]), len(proj_sets)
    groups = channels // GROUP
    per_step = next(n for n in (2, 1) if groups % n == 0)
    steps = groups // per_step
    rows = blocks * GROUP
    high = per_step * GROUP
    proj_specs = [pl.BlockSpec((3, high, x.shape[2]), lambda i, o: (0, i, 0)) for x in proj_sets[0]]
    d_widths = [sum(proj_sets[0][a].shape[2] for a in arrays) for arrays in grouped]
    d_specs = [pl.BlockSpec((3, high, w), lambda i, o: (0, i, 0)) for w in d_widths]
    token_spec = pl.BlockSpec((blocks, high, LONG), lambda i, o: (0, i, 0))
    outs = pl.pallas_call(
        functools.partial(mix_body, count, sets, per_step, grouped),
        grid_spec=pltpu.PrefetchScalarGridSpec(
            num_scalar_prefetch=1,
            grid=(steps,),
            in_specs=[
                pl.BlockSpec(memory_space=pltpu.SMEM),
                pl.BlockSpec((1, per_step, LONG), lambda i, o: (i, 0, 0)),
                token_spec,
            ]
            + proj_specs * sets,
            out_specs=[token_spec]
            + d_specs
            + [
                pl.BlockSpec((1, per_step, 3 * SHORT, LONG), lambda i, o: (i, 0, 0, 0)),
                pl.BlockSpec((1, per_step, LONG), lambda i, o: (i, 0, 0)),
            ],
            scratch_shapes=[
                pltpu.VMEM((per_step, 3, rows, LONG), F32),
                pltpu.VMEM((per_step, 3, rows, LONG), F32),
                pltpu.VMEM((per_step, rows + GROUP, LONG), BF16),
                pltpu.VMEM((per_step, rows + GROUP, LONG), BF16),
                pltpu.VMEM((per_step, rows, LONG), F32),
                pltpu.VMEM((per_step, 3, rows, LONG), BF16),
            ],
        ),
        out_shape=[jax.ShapeDtypeStruct((blocks, channels, LONG), BF16)]
        + [jax.ShapeDtypeStruct((3, channels, w), BF16) for w in d_widths]
        + [
            jax.ShapeDtypeStruct((steps, per_step, 3 * SHORT, LONG), F32),
            jax.ShapeDtypeStruct((steps, per_step, LONG), F32),
        ],
        compiler_params=pltpu.CompilerParams(vmem_limit_bytes=58 * MIB),
        cost_estimate=SMALL,
    )(order, short_kernel, long_kernel.reshape(steps, per_step, LONG), g, *[x for s in proj_sets for x in s])
    mixed, d_proj, (gs, gl) = outs[0], outs[1:-2], outs[-2:]
    grad_short = jnp.sum(gs, axis=-1).reshape(groups, 3, SHORT).transpose(1, 0, 2)
    grad_long = jnp.roll(jnp.flip(gl.reshape(groups, LONG), axis=1), 1, axis=1)
    return mixed, d_proj, grad_short, grad_long


def restack_body(t_ref, *refs):
    out_ref = refs[3]
    for i in range(3):
        out_ref[0, i] = refs[i][0]


def restack(t, weights):
    _, channels, width = weights[0].shape
    tile = min(128, channels)

    def source(side, part, t):
        return (jnp.where(side == 0, t[0], 1 - t[0]), part, 0)

    return pl.pallas_call(
        restack_body,
        grid_spec=pltpu.PrefetchScalarGridSpec(
            num_scalar_prefetch=1,
            grid=(2, channels // tile),
            in_specs=[pl.BlockSpec((1, tile, width), source)] * 3,
            out_specs=pl.BlockSpec((1, 3, tile, width), lambda side, part, t: (side, 0, part, 0)),
        ),
        out_shape=jax.ShapeDtypeStruct((2, 3, channels, width), BF16),
        compiler_params=pltpu.CompilerParams(vmem_limit_bytes=16 * MIB),
        cost_estimate=SMALL,
    )(t.reshape(1), *weights).reshape(6 * channels, width)


def project_body(pieces, *refs):
    x_refs, w_ref = refs[:pieces], refs[pieces]
    far_ref, near_ref, x_s, sems = refs[pieces + 1 :]
    step, steps = pl.program_id(0), pl.num_programs(0)

    @pl.when(step == 0)
    def _():
        copies, at = [], 0
        for n, x in enumerate(x_refs):
            copies.append(pltpu.make_async_copy(x, x_s.at[pl.ds(at, x.shape[0])], sems.at[n]))
            at += x.shape[0]
        for copy in copies:
            copy.start()
        for copy in copies:
            copy.wait()

    got = dot(w_ref[...], x_s[...], ((1,), (1,))).astype(BF16)

    @pl.when(step < steps // 2)
    def _():
        far_ref[...] = got

    @pl.when(step >= steps // 2)
    def _():
        near_ref[...] = got


def project_kernel(flat, pieces):
    rows, width = flat.shape
    tokens = sum(x.shape[0] for x in pieces)
    tile = rows // 4
    half = jax.ShapeDtypeStruct((rows // 2, tokens), BF16)
    far, near = pl.pallas_call(
        functools.partial(project_body, len(pieces)),
        grid=(4,),
        in_specs=[pl.BlockSpec(memory_space=pl.ANY)] * len(pieces)
        + [pl.BlockSpec((tile, width), lambda i: ((i + 2) % 4, 0))],
        out_specs=[
            pl.BlockSpec((tile, tokens), lambda i: (jnp.minimum(i, 1), 0)),
            pl.BlockSpec((tile, tokens), lambda i: (jnp.maximum(i - 2, 0), 0)),
        ],
        out_shape=[half, half],
        scratch_shapes=[pltpu.VMEM((tokens, width), BF16), pltpu.SemaphoreType.DMA((len(pieces),))],
        compiler_params=pltpu.CompilerParams(vmem_limit_bytes=16 * MIB),
        cost_estimate=SMALL,
    )(*pieces, flat)
    return near, far


def unproject_body(near_ref, far_ref, w_ref, *refs):
    out_refs, d_s = refs[:-1], refs[-1]
    stay = near_ref.shape[0]

    @pl.when(pl.program_id(0) == 0)
    def _():
        d_s[:, 0:stay] = near_ref[...].T
        d_s[:, stay:] = far_ref[...].T

    got = dot(d_s[...], w_ref[...], ((1,), (0,)))
    at = 0
    for out_ref in out_refs:
        out_ref[...] = got[at : at + out_ref.shape[0]].astype(BF16)
        at += out_ref.shape[0]


def unproject_kernel(flat, near, far, cuts):
    rows, width = flat.shape
    tokens = near.shape[1]
    tile = min(1024, width)
    return pl.pallas_call(
        unproject_body,
        grid=(width // tile,),
        in_specs=[
            pl.BlockSpec((rows // 2, tokens), lambda i: (0, 0)),
            pl.BlockSpec((rows // 2, tokens), lambda i: (0, 0)),
            pl.BlockSpec((rows, tile), lambda i: (0, i)),
        ],
        out_specs=[pl.BlockSpec((cut, tile), lambda i: (0, i)) for cut in cuts],
        out_shape=[jax.ShapeDtypeStruct((cut, width), BF16) for cut in cuts],
        scratch_shapes=[pltpu.VMEM((tokens, rows), BF16)],
        compiler_params=pltpu.CompilerParams(vmem_limit_bytes=20 * MIB),
        cost_estimate=SMALL,
    )(near, far, flat)


def add_body(heights, *refs):
    out_refs = refs[sum(heights) :]
    groups, at = [], 0
    for height in heights:
        groups.append(refs[at : at + height])
        at += height
    tops = [[sum(r.shape[0] for r in group[:n]) for n in range(len(group) + 1)] for group in groups]
    height = out_refs[0].shape[0]
    edges = {edge for top in tops for edge in top} | {n * height for n in range(len(out_refs) + 1)}
    edges = sorted(edges)
    for low, high in zip(edges[:-1], edges[1:]):
        total = None
        for group, top in zip(groups, tops):
            for n, ref in enumerate(group):
                if top[n] <= low and high <= top[n + 1]:
                    part = ref[low - top[n] : high - top[n], :].astype(F32)
                    total = part if total is None else total + part
        out_refs[low // height][low % height : low % height + high - low, :] = total.astype(BF16)


def add_kernel(*groups, cut=1):
    rows, width = sum(x.shape[0] for x in groups[0]) // cut, groups[0][0].shape[1]
    tile = min(1024, width)
    arrays = [x for group in groups for x in group]
    return pl.pallas_call(
        functools.partial(add_body, [len(group) for group in groups]),
        grid=(width // tile,),
        in_specs=[pl.BlockSpec((x.shape[0], tile), lambda i: (0, i)) for x in arrays],
        out_specs=[pl.BlockSpec((rows, tile), lambda i: (0, i))] * cut,
        out_shape=[jax.ShapeDtypeStruct((rows, width), BF16)] * cut,
        compiler_params=pltpu.CompilerParams(vmem_limit_bytes=8 * MIB),
        cost_estimate=SMALL,
    )(*arrays)


def copy_body(in_ref, out_ref):
    out_ref[...] = in_ref[...]


def copy_kernel(x):
    rows, width = x.shape
    tile = rows // 4
    return pl.pallas_call(
        copy_body,
        grid=(4,),
        in_specs=[pl.BlockSpec((tile, width), lambda i: (i, 0))],
        out_specs=pl.BlockSpec((tile, width), lambda i: (i, 0)),
        out_shape=jax.ShapeDtypeStruct(x.shape, x.dtype),
        compiler_params=pltpu.CompilerParams(vmem_limit_bytes=8 * MIB),
        cost_estimate=SMALL,
    )(x)


def on_device(ring, n_tp, tokens_in, w_query, w_key, w_value, short_taps, long_taps, grad_out):
    chips = len(ring)
    half = chips // 2
    n_ctx = 2 * chips
    held, width = tokens_in.shape
    channels = w_query.shape[1]
    weights = (w_query, w_key, w_value)

    def one_way(x, turned=False, to_mate=False):
        hops = []
        for j in range(chips):
            for core in range(2):
                chip = ring[(j + (1 if (core == 0) != turned else -1)) % chips]
                hops.append((2 * ring[j] + core, 2 * chip + (core ^ int(to_mate))))
        return lax.ppermute(x, "ctx", hops)

    def swap(x):
        return lax.ppermute(x, "ctx", [(d, d ^ 1) for d in range(n_ctx)])

    table = np.zeros((n_ctx, n_ctx), np.int32)
    for device in range(n_ctx):
        place, core = ring.index(device // 2), device % 2
        way = -1 if core == 0 else 1
        items = [(0, 0), (0, 1)]
        for s in range(1, half):
            items += [(way * s, 0), (way * s, 1), (-way * s, 1), (-way * s, 0)]
        items += [(half, 0), (half, 1)]
        table[device] = [2 * ring[(place + hop) % chips] + (core ^ other) for hop, other in items]
    order = lax.dynamic_index_in_dim(jnp.asarray(table), lax.axis_index("ctx"), 0, keepdims=False)
    short_kernel, long_kernel = short_taps.reshape(3, -1, SHORT), long_taps.reshape(-1, LONG)

    stay = 3 * channels
    if n_tp == 2:
        t = lax.axis_index("tp").astype(jnp.int32)
        t, order, short_kernel, long_kernel = lax.optimization_barrier((t, order, short_kernel, long_kernel))
        flat = restack(t, weights)
    else:
        flat = jnp.stack(weights).reshape(-1, width)

    def project(pieces):
        if n_tp == 2:
            return project_kernel(flat, pieces)
        y = dot(flat, jnp.concatenate(pieces, axis=0), ((1,), (1,))).astype(BF16).reshape(3, n_tp, channels, -1)
        return lax.psum_scatter(y, "tp", scatter_dimension=1, tiled=True).reshape(stay, -1), None

    def across(x):
        return None if x is None else lax.ppermute(x, "tp", [(0, 1), (1, 0)])

    def meet(d):
        if n_tp == 2:
            return d.reshape(stay, -1), across(d.reshape(stay, -1))
        d = lax.all_gather(d.reshape(3, 1, channels, -1), "tp", axis=1, tiled=True)
        return (d.reshape(-1, d.shape[-1]),)

    def unproject(d, *cuts):
        if n_tp == 2:
            return unproject_kernel(flat, *d, cuts)
        y = dot(d[0], flat, ((0,), (0,))).astype(BF16)
        return jnp.split(y, np.cumsum(cuts)[:-1], axis=0)

    stage = lax.optimization_barrier

    arrived = [one_way(tokens_in), one_way(tokens_in, to_mate=True, turned=True)]
    near, far = project([tokens_in, swap(tokens_in)])
    crossed = across(far)
    arrived, near = stage((arrived, near))
    arrived = jnp.concatenate(arrived, axis=0)
    projected = []
    for s in range(1, half):
        coming = one_way(arrived if s < half - 1 else arrived[:held])
        shared, crossed = stage((arrived, crossed))
        projected.append((near, crossed))
        cuts = (96, 80, 80) if s == half - 1 and held == 128 else (held, held)
        mates = [swap(x) for x in jnp.split(shared, np.cumsum(cuts)[:-1], axis=0)]
        if s < half - 1:
            near, far = project([arrived, *mates])
            crossed = across(far)
            arrived, near = stage((coming, near))
    here, far = project([arrived])
    first = across(far)
    near, far = project(mates)
    crossed = across(far)
    arrived, near, first, grad_out = stage((coming, near, first, grad_out))
    projected.append((here, first))
    incoming = lax.all_to_all(
        grad_out.reshape(n_ctx, channels, held), "ctx", split_axis=0, concat_axis=0, tiled=True
    )
    last, far = project([arrived, swap(arrived[: held // 2]), swap(arrived[held // 2 :])])
    far, crossed = stage((far, crossed))
    projected += [(near, crossed), (last, across(far))]

    mixed, d_proj, grad_short, grad_long = mix(
        order,
        short_kernel,
        long_kernel,
        incoming,
        [[y.reshape(3, channels, -1) for y in side] for side in zip(*projected) if side[0] is not None],
        [[s] for s in range(half - 1)] + [[half - 1, half], [half + 1]],
    )

    first, met, later = [meet(d_proj[s]) for s in (half, half - 1, half - 2)]
    mixed_out = lax.all_to_all(mixed, "ctx", split_axis=0, concat_axis=0, tiled=True).reshape(-1, held)
    keep, *give = unproject(first, held, *((80, 48) if held == 128 else (held // 2, held // 2)))
    total = add_kernel([keep], [swap(x) for x in give])
    total, met, rest = stage((total, met, d_proj[: half - 2]))
    for s in range(half - 1, 0, -1):
        coming = one_way(total[0], turned=True)
        if s < half - 1:
            later = meet(rest[-1])
            rest = rest[:-1]
        cuts = (96, 96, 64) if s == half - 1 and held == 128 else (held, held)
        keep, *give = unproject(met, 2 * held, *cuts)
        give[-1], later = stage((give[-1], later))
        total = add_kernel([keep], [swap(x) for x in give], [coming], cut=2 if s == 1 else 1)
        if s == half - 2:
            mixed_out = copy_kernel(mixed_out)
        total, met, rest, mixed_out = stage((total, later, rest, mixed_out))
    coming = [one_way(total[0], turned=True), one_way(total[1], turned=True, to_mate=True)]
    keep, *give = unproject(met, held, held // 2, held // 2)
    (grad_tokens,) = add_kernel([keep], [swap(x) for x in give], coming[:1], coming[1:])
    return (
        mixed_out,
        grad_tokens,
        grad_short.reshape(3, 1, -1, SHORT),
        grad_long.reshape(1, -1, LONG),
    )


def solution(mesh):
    placed = (
        P("ctx", "tp"),
        P(None, "ctx", "tp"),
        P(None, "ctx", "tp"),
        P(None, "ctx", "tp"),
        P(None, "tp", "ctx", None),
        P("tp", "ctx", None),
        P("tp", "ctx"),
    )
    return jax.shard_map(
        functools.partial(on_device, ring_of(mesh), mesh.shape["tp"]),
        mesh=mesh,
        in_specs=placed,
        out_specs=(
            P("tp", "ctx"),
            P("ctx", "tp"),
            P(None, "tp", "ctx", None),
            P("tp", "ctx", None),
        ),
        check_vma=False,
    )
```

```python
import functools

import jax
import jax.numpy as jnp
import numpy as np
from jax import lax
from jax.experimental import pallas as pl
from jax.experimental.pallas import tpu as pltpu
from jax.sharding import PartitionSpec as P

GROUP = 16
SHORT = 3
LONG = 128
F32 = jnp.float32
BF16 = jnp.bfloat16
MIB = 1024 * 1024
SMALL = pl.CostEstimate(flops=1, bytes_accessed=1, transcendentals=0)


def ring_of(mesh):
    chips = mesh.shape["ctx"] // 2
    plain = list(range(chips))
    devices = np.asarray(mesh.devices).reshape(mesh.shape["ctx"], -1)[:, 0]
    places = [getattr(devices[2 * chip], "coords", None) for chip in plain]
    if any(place is None for place in places):
        return plain
    places = np.array([list(place)[:3] for place in places])
    axes = [axis for axis in range(3) if len(set(places[:, axis])) > 1]
    if len(axes) != 2:
        return plain
    rung = min(axes, key=lambda axis: len(set(places[:, axis])))
    along = axes[0] if rung == axes[1] else axes[1]
    sides = sorted(set(places[:, rung]))
    if len(sides) != 2:
        return plain
    there = [c for c in plain if places[c, rung] == sides[0]]
    back = [c for c in plain if places[c, rung] == sides[1]]
    there.sort(key=lambda c: places[c, along])
    back.sort(key=lambda c: -places[c, along])
    return there + back


def dot(a, b, dims):
    return lax.dot_general(a, b, (dims, ((), ())), preferred_element_type=F32)


def turn_taps(taps):
    return jnp.roll(jnp.flip(taps, axis=1), 1, axis=1)


def mix_body(count, sets, per_turn, grouped, order, short_ref, long_ref, turned_ref, g_ref, *refs):
    proj_refs = [refs[s * count : (s + 1) * count] for s in range(sets)]
    refs = refs[sets * count :]
    d_count = len(grouped)
    mixed_ref, d_refs, gs_ref, gl_ref = refs[0], refs[1 : 1 + d_count], refs[1 + d_count], refs[2 + d_count]
    p_s, f_s, x_s, y_s, d_s, e_s = refs[3 + d_count :]
    blocks = g_ref.shape[0]
    rows = blocks * GROUP
    step = pl.program_id(0)

    @pl.when(step == 0)
    def _():
        x_s[:, 0:GROUP, :] = jnp.zeros((per_turn, GROUP, LONG), BF16)
        y_s[:, rows:, :] = jnp.zeros((per_turn, GROUP, LONG), BF16)

    halves = [(a, h) for a in range(count) for h in range(proj_refs[0][a].shape[2] // LONG)]
    places = [(a, h, where) for where, (a, h) in enumerate(halves)]
    d_places = []
    for b, arrays in enumerate(grouped):
        inside = [where for array in arrays for a, _, where in places if a == array]
        d_places += [(b, h, where) for h, where in enumerate(inside)]
    lane = lax.broadcasted_iota(jnp.int32, (GROUP, LONG), 1)
    zero = jnp.zeros((GROUP, LONG), F32)
    at_block = [slice(n * GROUP, (n + 1) * GROUP) for n in range(blocks)]
    sub8 = lax.broadcasted_iota(jnp.int32, (8, LONG), 0)
    col = lax.broadcasted_iota(jnp.int32, (LONG, LONG), 1)
    row = lax.broadcasted_iota(jnp.int32, (LONG, LONG), 0)

    per_step = gl_ref.shape[1]

    @pl.loop(0, per_step // per_turn)
    def _(turn):
        every = range(per_turn)
        mine = [pl.ds(pl.multiple_of((turn * per_turn + j) * GROUP, GROUP), GROUP) for j in every]
        lines = [turn * per_turn + j for j in every]
        taps = [
            [[short_ref[i, step * per_step + lines[j], k] for k in range(SHORT)] for i in range(3)] for j in every
        ]
        for a, h, where in places:
            at = pl.multiple_of(order[where] * GROUP, GROUP)
            for j in every:
                for i in range(3):
                    part = proj_refs[0][a][i, mine[j], h * LONG : (h + 1) * LONG].astype(F32)
                    for s in range(1, sets):
                        part = part + proj_refs[s][a][i, mine[j], h * LONG : (h + 1) * LONG].astype(F32)
                    p_s[j, i, pl.ds(at, GROUP), :] = part

        for j in every:
            before = [(zero, zero)] * 3
            for at in at_block:
                feat = []
                for i in range(3):
                    here = p_s[j, i, at, :]
                    one = pltpu.roll(here, 1, 1)
                    two = pltpu.roll(here, 2, 1)
                    past_one = jnp.where(lane < 1, before[i][0], one)
                    past_two = jnp.where(lane < 2, before[i][1], two)
                    before[i] = (one, two)
                    feat.append(taps[j][i][0] * here + taps[j][i][1] * past_one + taps[j][i][2] * past_two)
                    f_s[j, i, at, :] = feat[i]
                x_s[j, at.stop : at.stop + GROUP, :] = (feat[1] * feat[2]).astype(BF16)

        filters, turned = [], []
        for j in every:
            for ref, made in ((long_ref, filters), (turned_ref, turned)):
                base = jnp.broadcast_to(ref[0, pl.ds(lines[j], 1), :], (8, LONG))
                for bit in (1, 2, 4):
                    base = jnp.where((sub8 & bit) != 0, pltpu.roll(base, bit, 1), base)
                full = jnp.concatenate([base] + [pltpu.roll(base, 8 * m, 1) for m in range(1, LONG // 8)], axis=0)
                inside = col >= row if made is filters else col <= row
                near = jnp.where(inside, full, 0.0).astype(BF16)
                far = jnp.where(inside, 0.0, full).astype(BF16)
                made.append(jnp.concatenate([near, far], axis=0))

        x_twos = [jnp.concatenate([x_s[j, GROUP:, :], x_s[j, :rows, :]], axis=1) for j in every]
        inners = [dot(x_twos[j], filters[j], ((1,), (0,))) for j in every]
        for j in every:
            for n, at in enumerate(at_block):
                g = g_ref[n, mine[j], :].astype(F32)
                feat, inner = f_s[j, 0, at, :], inners[j][at]
                mixed_ref[n, mine[j], :] = (feat * inner).astype(BF16)
                y_s[j, at, :] = (g * feat).astype(BF16)
                d_s[j, at, :] = g * inner
        d_products = []
        for j in every:
            y_two = jnp.concatenate([y_s[j, :rows, :], y_s[j, GROUP:, :]], axis=1)
            d_products.append(dot(y_two, turned[j], ((1,), (0,))))
        folds = [dot(y_s[j, :rows, :], x_twos[j], ((0,), (0,))) for j in every]
        for j in every:
            fold = jnp.where(col <= row, folds[j][:, :LONG], folds[j][:, LONG:])
            width = LONG
            while width > 8:
                width //= 2
                fold = fold[:width] + pltpu.roll(fold[width:], LONG - width, 1)
            for bit in (4, 2, 1):
                fold = jnp.where((sub8 & bit) != 0, pltpu.roll(fold, LONG - bit, 1), fold)
            gl_ref[0, pl.ds(lines[j], 1), :] = jnp.sum(fold, axis=0, keepdims=True)

        for j in every:
            after = [(zero, zero)] * 3
            sums = [[zero] * SHORT for _ in range(3)]
            for at in at_block[::-1]:
                d_product = d_products[j][at]
                for i, d in enumerate((d_s[j, at, :], d_product * f_s[j, 2, at, :], d_product * f_s[j, 1, at, :])):
                    one = pltpu.roll(d, LONG - 1, 1)
                    two = pltpu.roll(d, LONG - 2, 1)
                    next_one = jnp.where(lane >= LONG - 1, after[i][0], one)
                    next_two = jnp.where(lane >= LONG - 2, after[i][1], two)
                    after[i] = (one, two)
                    p = p_s[j, i, at, :]
                    sums[i] = [total + p * moved for total, moved in zip(sums[i], (d, next_one, next_two))]
                    e_s[j, i, at, :] = (
                        taps[j][i][0] * d + taps[j][i][1] * next_one + taps[j][i][2] * next_two
                    ).astype(BF16)
            for i in range(3):
                for k in range(SHORT):
                    gs_ref[0, lines[j], 3 * i + k : 3 * i + k + 1, :] = jnp.sum(sums[i][k], axis=0, keepdims=True)
        for a, h, where in d_places:
            at = pl.multiple_of(order[where] * GROUP, GROUP)
            for j in every:
                for i in range(3):
                    d_refs[a][i, mine[j], h * LONG : (h + 1) * LONG] = e_s[j, i, pl.ds(at, GROUP), :]


def mix(order, short_kernel, long_kernel, turned_kernel, g, proj_sets, grouped):
    blocks, channels, _ = g.shape
    count, sets = len(proj_sets[0]), len(proj_sets)
    groups = channels // GROUP
    per_turn = next(n for n in (2, 1) if groups % n == 0)
    per_step = next(n for n in (4, 2, 1) if groups % n == 0)
    steps = groups // per_step
    rows = blocks * GROUP
    high = per_step * GROUP
    proj_specs = [pl.BlockSpec((3, high, x.shape[2]), lambda i, o: (0, i, 0)) for x in proj_sets[0]]
    d_widths = [sum(proj_sets[0][a].shape[2] for a in arrays) for arrays in grouped]
    d_specs = [pl.BlockSpec((3, high, w), lambda i, o: (0, i, 0)) for w in d_widths]
    token_spec = pl.BlockSpec((blocks, high, LONG), lambda i, o: (0, i, 0))
    outs = pl.pallas_call(
        functools.partial(mix_body, count, sets, per_turn, grouped),
        grid_spec=pltpu.PrefetchScalarGridSpec(
            num_scalar_prefetch=1,
            grid=(steps,),
            in_specs=[
                pl.BlockSpec(memory_space=pltpu.SMEM),
                pl.BlockSpec((1, per_step, LONG), lambda i, o: (i, 0, 0)),
                pl.BlockSpec((1, per_step, LONG), lambda i, o: (i, 0, 0)),
                token_spec,
            ]
            + proj_specs * sets,
            out_specs=[token_spec]
            + d_specs
            + [
                pl.BlockSpec((1, per_step, 3 * SHORT, LONG), lambda i, o: (i, 0, 0, 0)),
                pl.BlockSpec((1, per_step, LONG), lambda i, o: (i, 0, 0)),
            ],
            scratch_shapes=[
                pltpu.VMEM((per_turn, 3, rows, LONG), F32),
                pltpu.VMEM((per_turn, 3, rows, LONG), F32),
                pltpu.VMEM((per_turn, rows + GROUP, LONG), BF16),
                pltpu.VMEM((per_turn, rows + GROUP, LONG), BF16),
                pltpu.VMEM((per_turn, rows, LONG), F32),
                pltpu.VMEM((per_turn, 3, rows, LONG), BF16),
            ],
        ),
        out_shape=[jax.ShapeDtypeStruct((blocks, channels, LONG), BF16)]
        + [jax.ShapeDtypeStruct((3, channels, w), BF16) for w in d_widths]
        + [
            jax.ShapeDtypeStruct((steps, per_step, 3 * SHORT, LONG), F32),
            jax.ShapeDtypeStruct((steps, per_step, LONG), F32),
        ],
        compiler_params=pltpu.CompilerParams(vmem_limit_bytes=58 * MIB),
        cost_estimate=SMALL,
    )(order, short_kernel, long_kernel.reshape(steps, per_step, LONG), turned_kernel.reshape(steps, per_step, LONG), g, *[x for s in proj_sets for x in s])
    mixed, d_proj, (gs, gl) = outs[0], outs[1:-2], outs[-2:]
    grad_short = jnp.sum(gs, axis=-1).reshape(groups, 3, SHORT).transpose(1, 0, 2)
    grad_long = turn_taps(gl.reshape(groups, LONG))
    return mixed, d_proj, grad_short, grad_long


def restack_body(t_ref, *refs):
    out_ref = refs[3]
    for i in range(3):
        out_ref[0, i] = refs[i][0]


def restack(t, weights):
    _, channels, width = weights[0].shape
    tile = min(128, channels)

    def source(side, part, t):
        return (jnp.where(side == 0, t[0], 1 - t[0]), part, 0)

    return pl.pallas_call(
        restack_body,
        grid_spec=pltpu.PrefetchScalarGridSpec(
            num_scalar_prefetch=1,
            grid=(2, channels // tile),
            in_specs=[pl.BlockSpec((1, tile, width), source)] * 3,
            out_specs=pl.BlockSpec((1, 3, tile, width), lambda side, part, t: (side, 0, part, 0)),
        ),
        out_shape=jax.ShapeDtypeStruct((2, 3, channels, width), BF16),
        compiler_params=pltpu.CompilerParams(vmem_limit_bytes=16 * MIB),
        cost_estimate=SMALL,
    )(t.reshape(1), *weights).reshape(6 * channels, width)


def project_body(pieces, *refs):
    x_refs, w_ref = refs[:pieces], refs[pieces]
    far_ref, near_ref, x_s, sems = refs[pieces + 1 :]
    step, steps = pl.program_id(0), pl.num_programs(0)

    @pl.when(step == 0)
    def _():
        copies, at = [], 0
        for n, x in enumerate(x_refs):
            copies.append(pltpu.make_async_copy(x, x_s.at[pl.ds(at, x.shape[0])], sems.at[n]))
            at += x.shape[0]
        for copy in copies:
            copy.start()
        for copy in copies:
            copy.wait()

    got = dot(w_ref[...], x_s[...], ((1,), (1,))).astype(BF16)

    @pl.when(step < steps // 2)
    def _():
        far_ref[...] = got

    @pl.when(step >= steps // 2)
    def _():
        near_ref[...] = got


def project_kernel(flat, pieces):
    rows, width = flat.shape
    tokens = sum(x.shape[0] for x in pieces)
    tile = rows // 4
    half = jax.ShapeDtypeStruct((rows // 2, tokens), BF16)
    far, near = pl.pallas_call(
        functools.partial(project_body, len(pieces)),
        grid=(4,),
        in_specs=[pl.BlockSpec(memory_space=pl.ANY)] * len(pieces)
        + [pl.BlockSpec((tile, width), lambda i: ((i + 2) % 4, 0))],
        out_specs=[
            pl.BlockSpec((tile, tokens), lambda i: (jnp.minimum(i, 1), 0)),
            pl.BlockSpec((tile, tokens), lambda i: (jnp.maximum(i - 2, 0), 0)),
        ],
        out_shape=[half, half],
        scratch_shapes=[pltpu.VMEM((tokens, width), BF16), pltpu.SemaphoreType.DMA((len(pieces),))],
        compiler_params=pltpu.CompilerParams(vmem_limit_bytes=16 * MIB),
        cost_estimate=SMALL,
    )(*pieces, flat)
    return near, far


def unproject_body(near_ref, far_ref, w_ref, *refs):
    out_refs, d_s = refs[:-1], refs[-1]
    stay = near_ref.shape[0]

    @pl.when(pl.program_id(0) == 0)
    def _():
        d_s[:, 0:stay] = near_ref[...].T
        d_s[:, stay:] = far_ref[...].T

    got = dot(d_s[...], w_ref[...], ((1,), (0,)))
    at = 0
    for out_ref in out_refs:
        out_ref[...] = got[at : at + out_ref.shape[0]].astype(BF16)
        at += out_ref.shape[0]


def unproject_kernel(flat, near, far, cuts):
    rows, width = flat.shape
    tokens = near.shape[1]
    tile = min(1024, width)
    return pl.pallas_call(
        unproject_body,
        grid=(width // tile,),
        in_specs=[
            pl.BlockSpec((rows // 2, tokens), lambda i: (0, 0)),
            pl.BlockSpec((rows // 2, tokens), lambda i: (0, 0)),
            pl.BlockSpec((rows, tile), lambda i: (0, i)),
        ],
        out_specs=[pl.BlockSpec((cut, tile), lambda i: (0, i)) for cut in cuts],
        out_shape=[jax.ShapeDtypeStruct((cut, width), BF16) for cut in cuts],
        scratch_shapes=[pltpu.VMEM((tokens, rows), BF16)],
        compiler_params=pltpu.CompilerParams(vmem_limit_bytes=20 * MIB),
        cost_estimate=SMALL,
    )(near, far, flat)


def add_body(heights, *refs):
    out_refs = refs[sum(heights) :]
    groups, at = [], 0
    for height in heights:
        groups.append(refs[at : at + height])
        at += height
    tops = [[sum(r.shape[0] for r in group[:n]) for n in range(len(group) + 1)] for group in groups]
    height = out_refs[0].shape[0]
    edges = {edge for top in tops for edge in top} | {n * height for n in range(len(out_refs) + 1)}
    edges = sorted(edges)
    for low, high in zip(edges[:-1], edges[1:]):
        total = None
        for group, top in zip(groups, tops):
            for n, ref in enumerate(group):
                if top[n] <= low and high <= top[n + 1]:
                    part = ref[low - top[n] : high - top[n], :].astype(F32)
                    total = part if total is None else total + part
        out_refs[low // height][low % height : low % height + high - low, :] = total.astype(BF16)


def add_kernel(*groups, cut=1):
    rows, width = sum(x.shape[0] for x in groups[0]) // cut, groups[0][0].shape[1]
    tile = min(1024, width)
    arrays = [x for group in groups for x in group]
    return pl.pallas_call(
        functools.partial(add_body, [len(group) for group in groups]),
        grid=(width // tile,),
        in_specs=[pl.BlockSpec((x.shape[0], tile), lambda i: (0, i)) for x in arrays],
        out_specs=[pl.BlockSpec((rows, tile), lambda i: (0, i))] * cut,
        out_shape=[jax.ShapeDtypeStruct((rows, width), BF16)] * cut,
        compiler_params=pltpu.CompilerParams(vmem_limit_bytes=8 * MIB),
        cost_estimate=SMALL,
    )(*arrays)


def copy_body(in_ref, out_ref):
    out_ref[...] = in_ref[...]


def copy_kernel(x):
    rows, width = x.shape
    tile = rows // 4
    return pl.pallas_call(
        copy_body,
        grid=(4,),
        in_specs=[pl.BlockSpec((tile, width), lambda i: (i, 0))],
        out_specs=pl.BlockSpec((tile, width), lambda i: (i, 0)),
        out_shape=jax.ShapeDtypeStruct(x.shape, x.dtype),
        compiler_params=pltpu.CompilerParams(vmem_limit_bytes=8 * MIB),
        cost_estimate=SMALL,
    )(x)


def on_device(ring, n_tp, tokens_in, w_query, w_key, w_value, short_taps, long_taps, grad_out):
    chips = len(ring)
    half = chips // 2
    n_ctx = 2 * chips
    held, width = tokens_in.shape
    channels = w_query.shape[1]
    weights = (w_query, w_key, w_value)

    def one_way(x, turned=False, to_mate=False):
        hops = []
        for j in range(chips):
            for core in range(2):
                chip = ring[(j + (1 if (core == 0) != turned else -1)) % chips]
                hops.append((2 * ring[j] + core, 2 * chip + (core ^ int(to_mate))))
        return lax.ppermute(x, "ctx", hops)

    def swap(x):
        return lax.ppermute(x, "ctx", [(d, d ^ 1) for d in range(n_ctx)])

    table = np.zeros((n_ctx, n_ctx), np.int32)
    for device in range(n_ctx):
        place, core = ring.index(device // 2), device % 2
        way = -1 if core == 0 else 1
        items = [(0, 0), (0, 1)]
        for s in range(1, half):
            items += [(way * s, 0), (way * s, 1), (-way * s, 1), (-way * s, 0)]
        items += [(half, 0), (half, 1)]
        table[device] = [2 * ring[(place + hop) % chips] + (core ^ other) for hop, other in items]
    order = lax.dynamic_index_in_dim(jnp.asarray(table), lax.axis_index("ctx"), 0, keepdims=False)
    short_kernel, long_kernel = short_taps.reshape(3, -1, SHORT), long_taps.reshape(-1, LONG)
    turned_kernel = turn_taps(long_kernel)

    stay = 3 * channels
    if n_tp == 2:
        t = lax.axis_index("tp").astype(jnp.int32)
        t, order, short_kernel, turned_kernel = lax.optimization_barrier((t, order, short_kernel, turned_kernel))
        flat = restack(t, weights)
    else:
        flat = jnp.stack(weights).reshape(-1, width)

    def project(pieces):
        if n_tp == 2:
            return project_kernel(flat, pieces)
        y = dot(flat, jnp.concatenate(pieces, axis=0), ((1,), (1,))).astype(BF16).reshape(3, n_tp, channels, -1)
        return lax.psum_scatter(y, "tp", scatter_dimension=1, tiled=True).reshape(stay, -1), None

    def across(x):
        return None if x is None else lax.ppermute(x, "tp", [(0, 1), (1, 0)])

    def meet(d):
        if n_tp == 2:
            return d.reshape(stay, -1), across(d.reshape(stay, -1))
        d = lax.all_gather(d.reshape(3, 1, channels, -1), "tp", axis=1, tiled=True)
        return (d.reshape(-1, d.shape[-1]),)

    def unproject(d, *cuts):
        if n_tp == 2:
            return unproject_kernel(flat, *d, cuts)
        y = dot(d[0], flat, ((0,), (0,))).astype(BF16)
        return jnp.split(y, np.cumsum(cuts)[:-1], axis=0)

    stage = lax.optimization_barrier

    arrived = [one_way(tokens_in), one_way(tokens_in, to_mate=True, turned=True)]
    near, far = project([tokens_in, swap(tokens_in)])
    arrived, near, far = stage((arrived, near, far))
    arrived = jnp.concatenate(arrived, axis=0)
    projected = []
    for s in range(1, half):
        coming = one_way(arrived if s < half - 1 else arrived[:held])
        projected.append((near, across(far)))
        near, far = project([arrived, swap(arrived)])
        if s < half - 1:
            arrived, near, far, projected[-1] = stage((coming, near, far, projected[-1]))
    crossed = across(far)
    arrived, near, grad_out = stage((coming, near, grad_out))
    incoming = lax.all_to_all(
        grad_out.reshape(n_ctx, channels, held), "ctx", split_axis=0, concat_axis=0, tiled=True
    )
    shared, projected[-1] = stage((arrived, projected[-1]))
    last, far = project([arrived, swap(shared[: held // 2]), swap(shared[held // 2 :])])
    projected += [(near, crossed), (last, across(far))]

    mixed, d_proj, grad_short, grad_long = mix(
        order,
        short_kernel,
        long_kernel,
        turned_kernel,
        incoming,
        [[y.reshape(3, channels, -1) for y in side] for side in zip(*projected) if side[0] is not None],
        [[s] for s in range(half + 1)],
    )

    first, met, later = [meet(d_proj[s]) for s in (half, half - 1, half - 2)]
    mixed_out = lax.all_to_all(mixed, "ctx", split_axis=0, concat_axis=0, tiled=True).reshape(-1, held)
    keep, *give = unproject(first, held, *((80, 48) if held == 128 else (held // 2, held // 2)))
    total = add_kernel([keep], [swap(x) for x in give])
    total, met, rest = stage((total, met, d_proj[: half - 2]))
    for s in range(half - 1, 0, -1):
        coming = one_way(total[0], turned=True)
        if s < half - 1:
            later = meet(rest[-1])
            rest = rest[:-1]
        cuts = (96, 96, 64) if s == half - 1 and held == 128 else (held, held)
        keep, *give = unproject(met, 2 * held, *cuts)
        give[-1], later = stage((give[-1], later))
        total = add_kernel([keep], [swap(x) for x in give], [coming], cut=2 if s == 1 else 1)
        if s == half - 2:
            mixed_out = copy_kernel(mixed_out)
        total, met, rest, mixed_out = stage((total, later, rest, mixed_out))
    coming = [one_way(total[0], turned=True), one_way(total[1], turned=True, to_mate=True)]
    keep, *give = unproject(met, held, held // 2, held // 2)
    (grad_tokens,) = add_kernel([keep], [swap(x) for x in give], coming[:1], coming[1:])
    return (
        mixed_out,
        grad_tokens,
        grad_short.reshape(3, 1, -1, SHORT),
        grad_long.reshape(1, -1, LONG),
    )


def solution(mesh):
    placed = (
        P("ctx", "tp"),
        P(None, "ctx", "tp"),
        P(None, "ctx", "tp"),
        P(None, "ctx", "tp"),
        P(None, "tp", "ctx", None),
        P("tp", "ctx", None),
        P("tp", "ctx"),
    )
    return jax.shard_map(
        functools.partial(on_device, ring_of(mesh), mesh.shape["tp"]),
        mesh=mesh,
        in_specs=placed,
        out_specs=(
            P("tp", "ctx"),
            P("ctx", "tp"),
            P(None, "tp", "ctx", None),
            P("tp", "ctx", None),
        ),
        check_vma=False,
    )
```

```python
import functools

import jax
import jax.numpy as jnp
import numpy as np
from jax import lax
from jax.experimental import pallas as pl
from jax.experimental.pallas import tpu as pltpu
from jax.sharding import PartitionSpec as P

GROUP = 16
SHORT = 3
LONG = 128
F32 = jnp.float32
BF16 = jnp.bfloat16
MIB = 1024 * 1024
SMALL = pl.CostEstimate(flops=1, bytes_accessed=1, transcendentals=0)


def ring_of(mesh):
    chips = mesh.shape["ctx"] // 2
    plain = list(range(chips))
    devices = np.asarray(mesh.devices).reshape(mesh.shape["ctx"], -1)[:, 0]
    places = [getattr(devices[2 * chip], "coords", None) for chip in plain]
    if any(place is None for place in places):
        return plain
    places = np.array([list(place)[:3] for place in places])
    axes = [axis for axis in range(3) if len(set(places[:, axis])) > 1]
    if len(axes) != 2:
        return plain
    rung = min(axes, key=lambda axis: len(set(places[:, axis])))
    along = axes[0] if rung == axes[1] else axes[1]
    sides = sorted(set(places[:, rung]))
    if len(sides) != 2:
        return plain
    there = [c for c in plain if places[c, rung] == sides[0]]
    back = [c for c in plain if places[c, rung] == sides[1]]
    there.sort(key=lambda c: places[c, along])
    back.sort(key=lambda c: -places[c, along])
    return there + back


def dot(a, b, dims):
    return lax.dot_general(a, b, (dims, ((), ())), preferred_element_type=F32)


def turn_taps(taps):
    return jnp.roll(jnp.flip(taps, axis=1), 1, axis=1)


def shift_matrix(way):
    at = np.arange(2 * LONG)
    place = np.where(at < LONG, at, at - (2 * LONG if way < 0 else 0))
    out = np.arange(LONG)
    return np.concatenate([place[:, None] - out[None, :] == way * k for k in (1, 2)], axis=1).astype(np.float32)


def mix_body(count, sets, per_turn, grouped, order, short_ref, long_ref, turned_ref, past_ref, next_ref, g_ref, *refs):
    proj_refs = [refs[s * count : (s + 1) * count] for s in range(sets)]
    refs = refs[sets * count :]
    d_count = len(grouped)
    mixed_ref, d_refs, gs_ref, gl_ref = refs[0], refs[1 : 1 + d_count], refs[1 + d_count], refs[2 + d_count]
    p_s, m_s, f_s, x_s, y_s, q_s, d_s, e_s = refs[3 + d_count :]
    blocks = g_ref.shape[0]
    rows = blocks * GROUP
    step = pl.program_id(0)

    @pl.when(step == 0)
    def _():
        p_s[:, :, 0:GROUP, :] = jnp.zeros((per_turn, 3, GROUP, LONG), BF16)
        x_s[:, 0:GROUP, :] = jnp.zeros((per_turn, GROUP, LONG), BF16)
        y_s[:, rows:, :] = jnp.zeros((per_turn, GROUP, LONG), BF16)
        d_s[:, :, rows:, :] = jnp.zeros((per_turn, 3, GROUP, LONG), BF16)

    halves = [(a, h) for a in range(count) for h in range(proj_refs[0][a].shape[2] // LONG)]
    places = [(a, h, where) for where, (a, h) in enumerate(halves)]
    d_places = []
    for b, arrays in enumerate(grouped):
        inside = [where for array in arrays for a, _, where in places if a == array]
        d_places += [(b, h, where) for h, where in enumerate(inside)]
    zero = jnp.zeros((GROUP, LONG), F32)
    at_block = [slice(n * GROUP, (n + 1) * GROUP) for n in range(blocks)]
    sub8 = lax.broadcasted_iota(jnp.int32, (8, LONG), 0)
    col = lax.broadcasted_iota(jnp.int32, (LONG, LONG), 1)
    row = lax.broadcasted_iota(jnp.int32, (LONG, LONG), 0)

    per_step = gl_ref.shape[1]

    @pl.loop(0, per_step // per_turn)
    def _(turn):
        every = range(per_turn)
        mine = [pl.ds(pl.multiple_of((turn * per_turn + j) * GROUP, GROUP), GROUP) for j in every]
        lines = [turn * per_turn + j for j in every]
        taps = [
            [[short_ref[i, step * per_step + lines[j], k] for k in range(SHORT)] for i in range(3)] for j in every
        ]
        for a, h, where in places:
            at = pl.multiple_of((order[where] + 1) * GROUP, GROUP)
            for j in every:
                for i in range(3):
                    part = proj_refs[0][a][i, mine[j], h * LONG : (h + 1) * LONG].astype(F32)
                    for s in range(1, sets):
                        part = part + proj_refs[s][a][i, mine[j], h * LONG : (h + 1) * LONG].astype(F32)
                    p_s[j, i, pl.ds(at, GROUP), :] = part.astype(BF16)

        for j in every:
            for i in range(3):
                two_blocks = jnp.concatenate([p_s[j, i, GROUP:, :], p_s[j, i, :rows, :]], axis=1)
                m_s[j, i] = dot(two_blocks, past_ref[...], ((1,), (0,))).astype(BF16)
        for j in every:
            for at in at_block:
                feat = []
                for i in range(3):
                    here = p_s[j, i, at.stop : at.stop + GROUP, :].astype(F32)
                    past = m_s[j, i, at, :].astype(F32)
                    feat.append(taps[j][i][0] * here + taps[j][i][1] * past[:, :LONG] + taps[j][i][2] * past[:, LONG:])
                    f_s[j, i, at, :] = feat[i]
                x_s[j, at.stop : at.stop + GROUP, :] = (feat[1] * feat[2]).astype(BF16)

        filters, turned = [], []
        for j in every:
            for ref, made in ((long_ref, filters), (turned_ref, turned)):
                base = jnp.broadcast_to(ref[0, pl.ds(lines[j], 1), :], (8, LONG))
                for bit in (1, 2, 4):
                    base = jnp.where((sub8 & bit) != 0, pltpu.roll(base, bit, 1), base)
                full = jnp.concatenate([base] + [pltpu.roll(base, 8 * m, 1) for m in range(1, LONG // 8)], axis=0)
                inside = col >= row if made is filters else col <= row
                near = jnp.where(inside, full, 0.0).astype(BF16)
                far = jnp.where(inside, 0.0, full).astype(BF16)
                made.append(jnp.concatenate([near, far], axis=0))

        x_twos = [jnp.concatenate([x_s[j, GROUP:, :], x_s[j, :rows, :]], axis=1) for j in every]
        inners = [dot(x_twos[j], filters[j], ((1,), (0,))) for j in every]
        for j in every:
            for n, at in enumerate(at_block):
                g = g_ref[n, mine[j], :].astype(F32)
                feat, inner = f_s[j, 0, at, :], inners[j][at]
                mixed_ref[n, mine[j], :] = (feat * inner).astype(BF16)
                y_s[j, at, :] = (g * feat).astype(BF16)
                q_s[j, at, :] = g * inner
        d_products = []
        for j in every:
            y_two = jnp.concatenate([y_s[j, :rows, :], y_s[j, GROUP:, :]], axis=1)
            d_products.append(dot(y_two, turned[j], ((1,), (0,))))
        folds = [dot(y_s[j, :rows, :], x_twos[j], ((0,), (0,))) for j in every]
        for j in every:
            fold = jnp.where(col <= row, folds[j][:, :LONG], folds[j][:, LONG:])
            width = LONG
            while width > 8:
                width //= 2
                fold = fold[:width] + pltpu.roll(fold[width:], LONG - width, 1)
            for bit in (4, 2, 1):
                fold = jnp.where((sub8 & bit) != 0, pltpu.roll(fold, LONG - bit, 1), fold)
            gl_ref[0, pl.ds(lines[j], 1), :] = jnp.sum(fold, axis=0, keepdims=True)

        for j in every:
            sums = [[zero] * SHORT for _ in range(3)]
            for at in at_block:
                d_product = d_products[j][at]
                for i, d in enumerate((q_s[j, at, :], d_product * f_s[j, 2, at, :], d_product * f_s[j, 1, at, :])):
                    here = p_s[j, i, at.stop : at.stop + GROUP, :].astype(F32)
                    past = m_s[j, i, at, :].astype(F32)
                    seen = (here, past[:, :LONG], past[:, LONG:])
                    sums[i] = [total + d * p for total, p in zip(sums[i], seen)]
                    d_s[j, i, at, :] = d.astype(BF16)
            for i in range(3):
                for k in range(SHORT):
                    gs_ref[0, lines[j], 3 * i + k : 3 * i + k + 1, :] = jnp.sum(sums[i][k], axis=0, keepdims=True)
        for j in every:
            for i in range(3):
                two_blocks = jnp.concatenate([d_s[j, i, :rows, :], d_s[j, i, GROUP:, :]], axis=1)
                coming = dot(two_blocks, next_ref[...], ((1,), (0,)))
                for at in at_block:
                    here = d_s[j, i, at, :].astype(F32)
                    near, far = coming[at, :LONG], coming[at, LONG:]
                    e_s[j, i, at, :] = (
                        taps[j][i][0] * here + taps[j][i][1] * near + taps[j][i][2] * far
                    ).astype(BF16)
        for a, h, where in d_places:
            at = pl.multiple_of(order[where] * GROUP, GROUP)
            for j in every:
                for i in range(3):
                    d_refs[a][i, mine[j], h * LONG : (h + 1) * LONG] = e_s[j, i, pl.ds(at, GROUP), :]


def mix(order, short_kernel, long_kernel, turned_kernel, g, proj_sets, grouped):
    blocks, channels, _ = g.shape
    count, sets = len(proj_sets[0]), len(proj_sets)
    groups = channels // GROUP
    per_turn = next(n for n in (2, 1) if groups % n == 0)
    per_step = next(n for n in (4, 2, 1) if groups % n == 0)
    steps = groups // per_step
    rows = blocks * GROUP
    high = per_step * GROUP
    proj_specs = [pl.BlockSpec((3, high, x.shape[2]), lambda i, o: (0, i, 0)) for x in proj_sets[0]]
    d_widths = [sum(proj_sets[0][a].shape[2] for a in arrays) for arrays in grouped]
    d_specs = [pl.BlockSpec((3, high, w), lambda i, o: (0, i, 0)) for w in d_widths]
    token_spec = pl.BlockSpec((blocks, high, LONG), lambda i, o: (0, i, 0))
    shifts = [jnp.asarray(shift_matrix(way), BF16) for way in (-1, 1)]
    outs = pl.pallas_call(
        functools.partial(mix_body, count, sets, per_turn, grouped),
        grid_spec=pltpu.PrefetchScalarGridSpec(
            num_scalar_prefetch=1,
            grid=(steps,),
            in_specs=[
                pl.BlockSpec(memory_space=pltpu.SMEM),
                pl.BlockSpec((1, per_step, LONG), lambda i, o: (i, 0, 0)),
                pl.BlockSpec((1, per_step, LONG), lambda i, o: (i, 0, 0)),
                pl.BlockSpec((2 * LONG, 2 * LONG), lambda i, o: (0, 0)),
                pl.BlockSpec((2 * LONG, 2 * LONG), lambda i, o: (0, 0)),
                token_spec,
            ]
            + proj_specs * sets,
            out_specs=[token_spec]
            + d_specs
            + [
                pl.BlockSpec((1, per_step, 3 * SHORT, LONG), lambda i, o: (i, 0, 0, 0)),
                pl.BlockSpec((1, per_step, LONG), lambda i, o: (i, 0, 0)),
            ],
            scratch_shapes=[
                pltpu.VMEM((per_turn, 3, rows + GROUP, LONG), BF16),
                pltpu.VMEM((per_turn, 3, rows, 2 * LONG), BF16),
                pltpu.VMEM((per_turn, 3, rows, LONG), F32),
                pltpu.VMEM((per_turn, rows + GROUP, LONG), BF16),
                pltpu.VMEM((per_turn, rows + GROUP, LONG), BF16),
                pltpu.VMEM((per_turn, rows, LONG), F32),
                pltpu.VMEM((per_turn, 3, rows + GROUP, LONG), BF16),
                pltpu.VMEM((per_turn, 3, rows, LONG), BF16),
            ],
        ),
        out_shape=[jax.ShapeDtypeStruct((blocks, channels, LONG), BF16)]
        + [jax.ShapeDtypeStruct((3, channels, w), BF16) for w in d_widths]
        + [
            jax.ShapeDtypeStruct((steps, per_step, 3 * SHORT, LONG), F32),
            jax.ShapeDtypeStruct((steps, per_step, LONG), F32),
        ],
        compiler_params=pltpu.CompilerParams(vmem_limit_bytes=58 * MIB),
        cost_estimate=SMALL,
    )(order, short_kernel, long_kernel.reshape(steps, per_step, LONG), turned_kernel.reshape(steps, per_step, LONG), *shifts, g, *[x for s in proj_sets for x in s])
    mixed, d_proj, (gs, gl) = outs[0], outs[1:-2], outs[-2:]
    grad_short = jnp.sum(gs, axis=-1).reshape(groups, 3, SHORT).transpose(1, 0, 2)
    grad_long = turn_taps(gl.reshape(groups, LONG))
    return mixed, d_proj, grad_short, grad_long


def restack_body(t_ref, *refs):
    out_ref = refs[3]
    for i in range(3):
        out_ref[0, i] = refs[i][0]


def restack(t, weights):
    _, channels, width = weights[0].shape
    tile = min(128, channels)

    def source(side, part, t):
        return (jnp.where(side == 0, t[0], 1 - t[0]), part, 0)

    return pl.pallas_call(
        restack_body,
        grid_spec=pltpu.PrefetchScalarGridSpec(
            num_scalar_prefetch=1,
            grid=(2, channels // tile),
            in_specs=[pl.BlockSpec((1, tile, width), source)] * 3,
            out_specs=pl.BlockSpec((1, 3, tile, width), lambda side, part, t: (side, 0, part, 0)),
        ),
        out_shape=jax.ShapeDtypeStruct((2, 3, channels, width), BF16),
        compiler_params=pltpu.CompilerParams(vmem_limit_bytes=16 * MIB),
        cost_estimate=SMALL,
    )(t.reshape(1), *weights).reshape(6 * channels, width)


def project_body(pieces, *refs):
    x_refs, w_ref = refs[:pieces], refs[pieces]
    far_ref, near_ref, x_s, sems = refs[pieces + 1 :]
    step, steps = pl.program_id(0), pl.num_programs(0)

    @pl.when(step == 0)
    def _():
        copies, at = [], 0
        for n, x in enumerate(x_refs):
            copies.append(pltpu.make_async_copy(x, x_s.at[pl.ds(at, x.shape[0])], sems.at[n]))
            at += x.shape[0]
        for copy in copies:
            copy.start()
        for copy in copies:
            copy.wait()

    got = dot(w_ref[...], x_s[...], ((1,), (1,))).astype(BF16)

    @pl.when(step < steps // 2)
    def _():
        far_ref[...] = got

    @pl.when(step >= steps // 2)
    def _():
        near_ref[...] = got


def project_kernel(flat, pieces):
    rows, width = flat.shape
    tokens = sum(x.shape[0] for x in pieces)
    tile = rows // 4
    half = jax.ShapeDtypeStruct((rows // 2, tokens), BF16)
    far, near = pl.pallas_call(
        functools.partial(project_body, len(pieces)),
        grid=(4,),
        in_specs=[pl.BlockSpec(memory_space=pl.ANY)] * len(pieces)
        + [pl.BlockSpec((tile, width), lambda i: ((i + 2) % 4, 0))],
        out_specs=[
            pl.BlockSpec((tile, tokens), lambda i: (jnp.minimum(i, 1), 0)),
            pl.BlockSpec((tile, tokens), lambda i: (jnp.maximum(i - 2, 0), 0)),
        ],
        out_shape=[half, half],
        scratch_shapes=[pltpu.VMEM((tokens, width), BF16), pltpu.SemaphoreType.DMA((len(pieces),))],
        compiler_params=pltpu.CompilerParams(vmem_limit_bytes=16 * MIB),
        cost_estimate=SMALL,
    )(*pieces, flat)
    return near, far


def unproject_body(near_ref, far_ref, w_ref, *refs):
    out_refs, d_s = refs[:-1], refs[-1]
    stay = near_ref.shape[0]

    @pl.when(pl.program_id(0) == 0)
    def _():
        d_s[:, 0:stay] = near_ref[...].T
        d_s[:, stay:] = far_ref[...].T

    got = dot(d_s[...], w_ref[...], ((1,), (0,)))
    at = 0
    for out_ref in out_refs:
        out_ref[...] = got[at : at + out_ref.shape[0]].astype(BF16)
        at += out_ref.shape[0]


def unproject_kernel(flat, near, far, cuts):
    rows, width = flat.shape
    tokens = near.shape[1]
    tile = min(1024, width)
    return pl.pallas_call(
        unproject_body,
        grid=(width // tile,),
        in_specs=[
            pl.BlockSpec((rows // 2, tokens), lambda i: (0, 0)),
            pl.BlockSpec((rows // 2, tokens), lambda i: (0, 0)),
            pl.BlockSpec((rows, tile), lambda i: (0, i)),
        ],
        out_specs=[pl.BlockSpec((cut, tile), lambda i: (0, i)) for cut in cuts],
        out_shape=[jax.ShapeDtypeStruct((cut, width), BF16) for cut in cuts],
        scratch_shapes=[pltpu.VMEM((tokens, rows), BF16)],
        compiler_params=pltpu.CompilerParams(vmem_limit_bytes=20 * MIB),
        cost_estimate=SMALL,
    )(near, far, flat)


def add_body(heights, *refs):
    out_refs = refs[sum(heights) :]
    groups, at = [], 0
    for height in heights:
        groups.append(refs[at : at + height])
        at += height
    tops = [[sum(r.shape[0] for r in group[:n]) for n in range(len(group) + 1)] for group in groups]
    height = out_refs[0].shape[0]
    edges = {edge for top in tops for edge in top} | {n * height for n in range(len(out_refs) + 1)}
    edges = sorted(edges)
    for low, high in zip(edges[:-1], edges[1:]):
        total = None
        for group, top in zip(groups, tops):
            for n, ref in enumerate(group):
                if top[n] <= low and high <= top[n + 1]:
                    part = ref[low - top[n] : high - top[n], :].astype(F32)
                    total = part if total is None else total + part
        out_refs[low // height][low % height : low % height + high - low, :] = total.astype(BF16)


def add_kernel(*groups, cut=1):
    rows, width = sum(x.shape[0] for x in groups[0]) // cut, groups[0][0].shape[1]
    tile = min(1024, width)
    arrays = [x for group in groups for x in group]
    return pl.pallas_call(
        functools.partial(add_body, [len(group) for group in groups]),
        grid=(width // tile,),
        in_specs=[pl.BlockSpec((x.shape[0], tile), lambda i: (0, i)) for x in arrays],
        out_specs=[pl.BlockSpec((rows, tile), lambda i: (0, i))] * cut,
        out_shape=[jax.ShapeDtypeStruct((rows, width), BF16)] * cut,
        compiler_params=pltpu.CompilerParams(vmem_limit_bytes=8 * MIB),
        cost_estimate=SMALL,
    )(*arrays)


def copy_body(in_ref, out_ref):
    out_ref[...] = in_ref[...]


def copy_kernel(x):
    rows, width = x.shape
    tile = rows // 4
    return pl.pallas_call(
        copy_body,
        grid=(4,),
        in_specs=[pl.BlockSpec((tile, width), lambda i: (i, 0))],
        out_specs=pl.BlockSpec((tile, width), lambda i: (i, 0)),
        out_shape=jax.ShapeDtypeStruct(x.shape, x.dtype),
        compiler_params=pltpu.CompilerParams(vmem_limit_bytes=8 * MIB),
        cost_estimate=SMALL,
    )(x)


def on_device(ring, n_tp, tokens_in, w_query, w_key, w_value, short_taps, long_taps, grad_out):
    chips = len(ring)
    half = chips // 2
    n_ctx = 2 * chips
    held, width = tokens_in.shape
    channels = w_query.shape[1]
    weights = (w_query, w_key, w_value)

    def one_way(x, turned=False, to_mate=False):
        hops = []
        for j in range(chips):
            for core in range(2):
                chip = ring[(j + (1 if (core == 0) != turned else -1)) % chips]
                hops.append((2 * ring[j] + core, 2 * chip + (core ^ int(to_mate))))
        return lax.ppermute(x, "ctx", hops)

    def swap(x):
        return lax.ppermute(x, "ctx", [(d, d ^ 1) for d in range(n_ctx)])

    table = np.zeros((n_ctx, n_ctx), np.int32)
    for device in range(n_ctx):
        place, core = ring.index(device // 2), device % 2
        way = -1 if core == 0 else 1
        items = [(0, 0), (0, 1)]
        for s in range(1, half):
            items += [(way * s, 0), (way * s, 1), (-way * s, 1), (-way * s, 0)]
        items += [(half, 0), (half, 1)]
        table[device] = [2 * ring[(place + hop) % chips] + (core ^ other) for hop, other in items]
    order = lax.dynamic_index_in_dim(jnp.asarray(table), lax.axis_index("ctx"), 0, keepdims=False)
    short_kernel, long_kernel = short_taps.reshape(3, -1, SHORT), long_taps.reshape(-1, LONG)
    turned_kernel = turn_taps(long_kernel)

    stay = 3 * channels
    if n_tp == 2:
        t = lax.axis_index("tp").astype(jnp.int32)
        t, order, short_kernel, turned_kernel = lax.optimization_barrier((t, order, short_kernel, turned_kernel))
        flat = restack(t, weights)
    else:
        flat = jnp.stack(weights).reshape(-1, width)

    def project(pieces):
        if n_tp == 2:
            return project_kernel(flat, pieces)
        y = dot(flat, jnp.concatenate(pieces, axis=0), ((1,), (1,))).astype(BF16).reshape(3, n_tp, channels, -1)
        return lax.psum_scatter(y, "tp", scatter_dimension=1, tiled=True).reshape(stay, -1), None

    def across(x):
        return None if x is None else lax.ppermute(x, "tp", [(0, 1), (1, 0)])

    def meet(d):
        if n_tp == 2:
            return d.reshape(stay, -1), across(d.reshape(stay, -1))
        d = lax.all_gather(d.reshape(3, 1, channels, -1), "tp", axis=1, tiled=True)
        return (d.reshape(-1, d.shape[-1]),)

    def unproject(d, *cuts):
        if n_tp == 2:
            return unproject_kernel(flat, *d, cuts)
        y = dot(d[0], flat, ((0,), (0,))).astype(BF16)
        return jnp.split(y, np.cumsum(cuts)[:-1], axis=0)

    stage = lax.optimization_barrier

    arrived = [one_way(tokens_in), one_way(tokens_in, to_mate=True, turned=True)]
    near, far = project([tokens_in, swap(tokens_in)])
    arrived, near, far = stage((arrived, near, far))
    arrived = jnp.concatenate(arrived, axis=0)
    projected = []
    for s in range(1, half):
        coming = one_way(arrived if s < half - 1 else arrived[:held])
        projected.append((near, across(far)))
        near, far = project([arrived, swap(arrived)])
        if s < half - 1:
            arrived, near, far, projected[-1] = stage((coming, near, far, projected[-1]))
    crossed = across(far)
    arrived, near, grad_out = stage((coming, near, grad_out))
    incoming = lax.all_to_all(
        grad_out.reshape(n_ctx, channels, held), "ctx", split_axis=0, concat_axis=0, tiled=True
    )
    shared, projected[-1] = stage((arrived, projected[-1]))
    last, far = project([arrived, swap(shared[: held // 2]), swap(shared[held // 2 :])])
    projected += [(near, crossed), (last, across(far))]

    mixed, d_proj, grad_short, grad_long = mix(
        order,
        short_kernel,
        long_kernel,
        turned_kernel,
        incoming,
        [[y.reshape(3, channels, -1) for y in side] for side in zip(*projected) if side[0] is not None],
        [[s] for s in range(half + 1)],
    )

    first, met, later = [meet(d_proj[s]) for s in (half, half - 1, half - 2)]
    mixed_out = lax.all_to_all(mixed, "ctx", split_axis=0, concat_axis=0, tiled=True).reshape(-1, held)
    keep, *give = unproject(first, held, *((80, 48) if held == 128 else (held // 2, held // 2)))
    total = add_kernel([keep], [swap(x) for x in give])
    total, met, rest = stage((total, met, d_proj[: half - 2]))
    for s in range(half - 1, 0, -1):
        coming = one_way(total[0], turned=True)
        if s < half - 1:
            later = meet(rest[-1])
            rest = rest[:-1]
        cuts = (96, 96, 64) if s == half - 1 and held == 128 else (held, held)
        keep, *give = unproject(met, 2 * held, *cuts)
        give[-1], later = stage((give[-1], later))
        total = add_kernel([keep], [swap(x) for x in give], [coming], cut=2 if s == 1 else 1)
        if s == half - 2:
            mixed_out = copy_kernel(mixed_out)
        total, met, rest, mixed_out = stage((total, later, rest, mixed_out))
    coming = [one_way(total[0], turned=True), one_way(total[1], turned=True, to_mate=True)]
    keep, *give = unproject(met, held, held // 2, held // 2)
    (grad_tokens,) = add_kernel([keep], [swap(x) for x in give], coming[:1], coming[1:])
    return (
        mixed_out,
        grad_tokens,
        grad_short.reshape(3, 1, -1, SHORT),
        grad_long.reshape(1, -1, LONG),
    )


def solution(mesh):
    placed = (
        P("ctx", "tp"),
        P(None, "ctx", "tp"),
        P(None, "ctx", "tp"),
        P(None, "ctx", "tp"),
        P(None, "tp", "ctx", None),
        P("tp", "ctx", None),
        P("tp", "ctx"),
    )
    return jax.shard_map(
        functools.partial(on_device, ring_of(mesh), mesh.shape["tp"]),
        mesh=mesh,
        in_specs=placed,
        out_specs=(
            P("tp", "ctx"),
            P("ctx", "tp"),
            P(None, "tp", "ctx", None),
            P("tp", "ctx", None),
        ),
        check_vma=False,
    )
```

```python
import functools

import jax
import jax.numpy as jnp
import numpy as np
from jax import lax
from jax.experimental import pallas as pl
from jax.experimental.pallas import tpu as pltpu
from jax.sharding import PartitionSpec as P

GROUP = 16
SHORT = 3
LONG = 128
F32 = jnp.float32
BF16 = jnp.bfloat16
MIB = 1024 * 1024
SMALL = pl.CostEstimate(flops=1, bytes_accessed=1, transcendentals=0)


def ring_of(mesh):
    chips = mesh.shape["ctx"] // 2
    plain = list(range(chips))
    devices = np.asarray(mesh.devices).reshape(mesh.shape["ctx"], -1)[:, 0]
    places = [getattr(devices[2 * chip], "coords", None) for chip in plain]
    if any(place is None for place in places):
        return plain
    places = np.array([list(place)[:3] for place in places])
    axes = [axis for axis in range(3) if len(set(places[:, axis])) > 1]
    if len(axes) != 2:
        return plain
    rung = min(axes, key=lambda axis: len(set(places[:, axis])))
    along = axes[0] if rung == axes[1] else axes[1]
    sides = sorted(set(places[:, rung]))
    if len(sides) != 2:
        return plain
    there = [c for c in plain if places[c, rung] == sides[0]]
    back = [c for c in plain if places[c, rung] == sides[1]]
    there.sort(key=lambda c: places[c, along])
    back.sort(key=lambda c: -places[c, along])
    return there + back


def dot(a, b, dims):
    return lax.dot_general(a, b, (dims, ((), ())), preferred_element_type=F32)


def turn_taps(taps):
    return jnp.roll(jnp.flip(taps, axis=1), 1, axis=1)


def shift_matrix(way):
    at = np.arange(2 * LONG)
    place = np.where(at < LONG, at, at - (2 * LONG if way < 0 else 0))
    out = np.arange(LONG)
    return np.concatenate([place[:, None] - out[None, :] == way * k for k in (1, 2)], axis=1).astype(np.float32)


def mix_body(count, sets, per_turn, grouped, order, short_ref, long_ref, turned_ref, past_ref, next_ref, g_ref, *refs):
    proj_refs = [refs[s * count : (s + 1) * count] for s in range(sets)]
    refs = refs[sets * count :]
    d_count = len(grouped)
    mixed_ref, d_refs, gs_ref, gl_ref = refs[0], refs[1 : 1 + d_count], refs[1 + d_count], refs[2 + d_count]
    p_s, m_s, f_s, x_s, y_s, q_s, d_s, e_s = refs[3 + d_count :]
    blocks = g_ref.shape[0]
    rows = blocks * GROUP
    step = pl.program_id(0)

    @pl.when(step == 0)
    def _():
        p_s[:, :, 0:GROUP, :] = jnp.zeros((per_turn, 3, GROUP, LONG), BF16)
        x_s[:, 0:GROUP, :] = jnp.zeros((per_turn, GROUP, LONG), BF16)
        y_s[:, rows:, :] = jnp.zeros((per_turn, GROUP, LONG), BF16)
        d_s[:, :, rows:, :] = jnp.zeros((per_turn, 3, GROUP, LONG), BF16)

    halves = [(a, h) for a in range(count) for h in range(proj_refs[0][a].shape[2] // LONG)]
    places = [(a, h, where) for where, (a, h) in enumerate(halves)]
    d_places = []
    for b, arrays in enumerate(grouped):
        inside = [where for array in arrays for a, _, where in places if a == array]
        d_places += [(b, h, where) for h, where in enumerate(inside)]
    zero = jnp.zeros((GROUP, LONG), F32)
    at_block = [slice(n * GROUP, (n + 1) * GROUP) for n in range(blocks)]
    sub8 = lax.broadcasted_iota(jnp.int32, (8, LONG), 0)
    col = lax.broadcasted_iota(jnp.int32, (LONG, LONG), 1)
    row = lax.broadcasted_iota(jnp.int32, (LONG, LONG), 0)

    per_step = gl_ref.shape[1]

    @pl.loop(0, per_step // per_turn)
    def _(turn):
        every = range(per_turn)
        mine = [pl.ds(pl.multiple_of((turn * per_turn + j) * GROUP, GROUP), GROUP) for j in every]
        lines = [turn * per_turn + j for j in every]
        taps = [
            [[short_ref[i, step * per_step + lines[j], k] for k in range(SHORT)] for i in range(3)] for j in every
        ]
        for a, h, where in places:
            at = pl.multiple_of((order[where] + 1) * GROUP, GROUP)
            for j in every:
                for i in range(3):
                    part = proj_refs[0][a][i, mine[j], h * LONG : (h + 1) * LONG].astype(F32)
                    for s in range(1, sets):
                        part = part + proj_refs[s][a][i, mine[j], h * LONG : (h + 1) * LONG].astype(F32)
                    p_s[j, i, pl.ds(at, GROUP), :] = part.astype(BF16)

        for j in every:
            for i in range(3):
                two_blocks = jnp.concatenate([p_s[j, i, GROUP:, :], p_s[j, i, :rows, :]], axis=1)
                m_s[j, i] = dot(two_blocks, past_ref[...], ((1,), (0,))).astype(BF16)
        for j in every:
            for at in at_block:
                feat = []
                for i in range(3):
                    here = p_s[j, i, at.stop : at.stop + GROUP, :].astype(F32)
                    past = m_s[j, i, at, :].astype(F32)
                    feat.append(taps[j][i][0] * here + taps[j][i][1] * past[:, :LONG] + taps[j][i][2] * past[:, LONG:])
                    f_s[j, i, at, :] = feat[i]
                x_s[j, at.stop : at.stop + GROUP, :] = (feat[1] * feat[2]).astype(BF16)

        filters, turned = [], []
        for j in every:
            for ref, made in ((long_ref, filters), (turned_ref, turned)):
                base = jnp.broadcast_to(ref[0, pl.ds(lines[j], 1), :], (8, LONG))
                for bit in (1, 2, 4):
                    base = jnp.where((sub8 & bit) != 0, pltpu.roll(base, bit, 1), base)
                full = jnp.concatenate([base] + [pltpu.roll(base, 8 * m, 1) for m in range(1, LONG // 8)], axis=0)
                inside = col >= row if made is filters else col <= row
                near = jnp.where(inside, full, 0.0).astype(BF16)
                far = jnp.where(inside, 0.0, full).astype(BF16)
                made.append(jnp.concatenate([near, far], axis=0))

        x_twos = [jnp.concatenate([x_s[j, GROUP:, :], x_s[j, :rows, :]], axis=1) for j in every]
        inners = [dot(x_twos[j], filters[j], ((1,), (0,))) for j in every]
        for j in every:
            for n, at in enumerate(at_block):
                g = g_ref[n, mine[j], :].astype(F32)
                feat, inner = f_s[j, 0, at, :], inners[j][at]
                mixed_ref[n, mine[j], :] = (feat * inner).astype(BF16)
                y_s[j, at, :] = (g * feat).astype(BF16)
                q_s[j, at, :] = g * inner
        d_products = []
        for j in every:
            y_two = jnp.concatenate([y_s[j, :rows, :], y_s[j, GROUP:, :]], axis=1)
            d_products.append(dot(y_two, turned[j], ((1,), (0,))))
        folds = [dot(y_s[j, :rows, :], x_twos[j], ((0,), (0,))) for j in every]
        for j in every:
            fold = jnp.where(col <= row, folds[j][:, :LONG], folds[j][:, LONG:])
            width = LONG
            while width > 8:
                width //= 2
                fold = fold[:width] + pltpu.roll(fold[width:], LONG - width, 1)
            for bit in (4, 2, 1):
                fold = jnp.where((sub8 & bit) != 0, pltpu.roll(fold, LONG - bit, 1), fold)
            gl_ref[0, pl.ds(lines[j], 1), :] = jnp.sum(fold, axis=0, keepdims=True)

        for j in every:
            sums = [[zero] * SHORT for _ in range(3)]
            for at in at_block:
                d_product = d_products[j][at]
                for i, d in enumerate((q_s[j, at, :], d_product * f_s[j, 2, at, :], d_product * f_s[j, 1, at, :])):
                    here = p_s[j, i, at.stop : at.stop + GROUP, :].astype(F32)
                    past = m_s[j, i, at, :].astype(F32)
                    seen = (here, past[:, :LONG], past[:, LONG:])
                    sums[i] = [total + d * p for total, p in zip(sums[i], seen)]
                    d_s[j, i, at, :] = d.astype(BF16)
            for i in range(3):
                for k in range(SHORT):
                    gs_ref[0, lines[j], 3 * i + k : 3 * i + k + 1, :] = jnp.sum(sums[i][k], axis=0, keepdims=True)
        for j in every:
            for i in range(3):
                two_blocks = jnp.concatenate([d_s[j, i, :rows, :], d_s[j, i, GROUP:, :]], axis=1)
                coming = dot(two_blocks, next_ref[...], ((1,), (0,)))
                for at in at_block:
                    here = d_s[j, i, at, :].astype(F32)
                    near, far = coming[at, :LONG], coming[at, LONG:]
                    e_s[j, i, at, :] = (
                        taps[j][i][0] * here + taps[j][i][1] * near + taps[j][i][2] * far
                    ).astype(BF16)
        for a, h, where in d_places:
            at = pl.multiple_of(order[where] * GROUP, GROUP)
            for j in every:
                for i in range(3):
                    d_refs[a][i, mine[j], h * LONG : (h + 1) * LONG] = e_s[j, i, pl.ds(at, GROUP), :]


def mix(order, short_kernel, long_kernel, turned_kernel, g, proj_sets, grouped):
    blocks, channels, _ = g.shape
    count, sets = len(proj_sets[0]), len(proj_sets)
    groups = channels // GROUP
    per_turn = next(n for n in (2, 1) if groups % n == 0)
    per_step = next(n for n in (4, 2, 1) if groups % n == 0)
    steps = groups // per_step
    rows = blocks * GROUP
    high = per_step * GROUP
    proj_specs = [pl.BlockSpec((3, high, x.shape[2]), lambda i, o: (0, i, 0)) for x in proj_sets[0]]
    d_widths = [sum(proj_sets[0][a].shape[2] for a in arrays) for arrays in grouped]
    d_specs = [pl.BlockSpec((3, high, w), lambda i, o: (0, i, 0)) for w in d_widths]
    token_spec = pl.BlockSpec((blocks, high, LONG), lambda i, o: (0, i, 0))
    shifts = [jnp.asarray(shift_matrix(way), BF16) for way in (-1, 1)]
    outs = pl.pallas_call(
        functools.partial(mix_body, count, sets, per_turn, grouped),
        grid_spec=pltpu.PrefetchScalarGridSpec(
            num_scalar_prefetch=1,
            grid=(steps,),
            in_specs=[
                pl.BlockSpec(memory_space=pltpu.SMEM),
                pl.BlockSpec((1, per_step, LONG), lambda i, o: (i, 0, 0)),
                pl.BlockSpec((1, per_step, LONG), lambda i, o: (i, 0, 0)),
                pl.BlockSpec((2 * LONG, 2 * LONG), lambda i, o: (0, 0)),
                pl.BlockSpec((2 * LONG, 2 * LONG), lambda i, o: (0, 0)),
                token_spec,
            ]
            + proj_specs * sets,
            out_specs=[token_spec]
            + d_specs
            + [
                pl.BlockSpec((1, per_step, 3 * SHORT, LONG), lambda i, o: (i, 0, 0, 0)),
                pl.BlockSpec((1, per_step, LONG), lambda i, o: (i, 0, 0)),
            ],
            scratch_shapes=[
                pltpu.VMEM((per_turn, 3, rows + GROUP, LONG), BF16),
                pltpu.VMEM((per_turn, 3, rows, 2 * LONG), BF16),
                pltpu.VMEM((per_turn, 3, rows, LONG), F32),
                pltpu.VMEM((per_turn, rows + GROUP, LONG), BF16),
                pltpu.VMEM((per_turn, rows + GROUP, LONG), BF16),
                pltpu.VMEM((per_turn, rows, LONG), F32),
                pltpu.VMEM((per_turn, 3, rows + GROUP, LONG), BF16),
                pltpu.VMEM((per_turn, 3, rows, LONG), BF16),
            ],
        ),
        out_shape=[jax.ShapeDtypeStruct((blocks, channels, LONG), BF16)]
        + [jax.ShapeDtypeStruct((3, channels, w), BF16) for w in d_widths]
        + [
            jax.ShapeDtypeStruct((steps, per_step, 3 * SHORT, LONG), F32),
            jax.ShapeDtypeStruct((steps, per_step, LONG), F32),
        ],
        compiler_params=pltpu.CompilerParams(vmem_limit_bytes=58 * MIB),
        cost_estimate=SMALL,
    )(order, short_kernel, long_kernel.reshape(steps, per_step, LONG), turned_kernel.reshape(steps, per_step, LONG), *shifts, g, *[x for s in proj_sets for x in s])
    mixed, d_proj, (gs, gl) = outs[0], outs[1:-2], outs[-2:]
    grad_short = jnp.sum(gs, axis=-1).reshape(groups, 3, SHORT).transpose(1, 0, 2)
    grad_long = turn_taps(gl.reshape(groups, LONG))
    return mixed, d_proj, grad_short, grad_long


def restack_body(t_ref, *refs):
    out_ref = refs[3]
    for i in range(3):
        out_ref[0, i] = refs[i][0]


def restack(t, weights):
    _, channels, width = weights[0].shape
    tile = min(128, channels)

    def source(side, part, t):
        return (jnp.where(side == 0, t[0], 1 - t[0]), part, 0)

    return pl.pallas_call(
        restack_body,
        grid_spec=pltpu.PrefetchScalarGridSpec(
            num_scalar_prefetch=1,
            grid=(2, channels // tile),
            in_specs=[pl.BlockSpec((1, tile, width), source)] * 3,
            out_specs=pl.BlockSpec((1, 3, tile, width), lambda side, part, t: (side, 0, part, 0)),
        ),
        out_shape=jax.ShapeDtypeStruct((2, 3, channels, width), BF16),
        compiler_params=pltpu.CompilerParams(vmem_limit_bytes=16 * MIB),
        cost_estimate=SMALL,
    )(t.reshape(1), *weights).reshape(6 * channels, width)


def project_body(pieces, *refs):
    x_refs, w_ref = refs[:pieces], refs[pieces]
    far_ref, near_ref, x_s, sems = refs[pieces + 1 :]
    step, steps = pl.program_id(0), pl.num_programs(0)

    @pl.when(step == 0)
    def _():
        copies, at = [], 0
        for n, x in enumerate(x_refs):
            copies.append(pltpu.make_async_copy(x, x_s.at[pl.ds(at, x.shape[0])], sems.at[n]))
            at += x.shape[0]
        for copy in copies:
            copy.start()
        for copy in copies:
            copy.wait()

    got = dot(w_ref[...], x_s[...], ((1,), (1,))).astype(BF16)

    @pl.when(step < steps // 2)
    def _():
        far_ref[...] = got

    @pl.when(step >= steps // 2)
    def _():
        near_ref[...] = got


def project_kernel(flat, pieces):
    rows, width = flat.shape
    tokens = sum(x.shape[0] for x in pieces)
    tile = rows // 4
    half = jax.ShapeDtypeStruct((rows // 2, tokens), BF16)
    far, near = pl.pallas_call(
        functools.partial(project_body, len(pieces)),
        grid=(4,),
        in_specs=[pl.BlockSpec(memory_space=pl.ANY)] * len(pieces)
        + [pl.BlockSpec((tile, width), lambda i: ((i + 2) % 4, 0))],
        out_specs=[
            pl.BlockSpec((tile, tokens), lambda i: (jnp.minimum(i, 1), 0)),
            pl.BlockSpec((tile, tokens), lambda i: (jnp.maximum(i - 2, 0), 0)),
        ],
        out_shape=[half, half],
        scratch_shapes=[pltpu.VMEM((tokens, width), BF16), pltpu.SemaphoreType.DMA((len(pieces),))],
        compiler_params=pltpu.CompilerParams(vmem_limit_bytes=16 * MIB),
        cost_estimate=SMALL,
    )(*pieces, flat)
    return near, far


def unproject_body(near_ref, far_ref, w_ref, *refs):
    out_refs, d_s = refs[:-1], refs[-1]
    stay = near_ref.shape[0]

    @pl.when(pl.program_id(0) == 0)
    def _():
        d_s[:, 0:stay] = near_ref[...].T
        d_s[:, stay:] = far_ref[...].T

    got = dot(d_s[...], w_ref[...], ((1,), (0,)))
    at = 0
    for out_ref in out_refs:
        out_ref[...] = got[at : at + out_ref.shape[0]].astype(BF16)
        at += out_ref.shape[0]


def unproject_kernel(flat, near, far, cuts):
    rows, width = flat.shape
    tokens = near.shape[1]
    tile = min(1024, width)
    return pl.pallas_call(
        unproject_body,
        grid=(width // tile,),
        in_specs=[
            pl.BlockSpec((rows // 2, tokens), lambda i: (0, 0)),
            pl.BlockSpec((rows // 2, tokens), lambda i: (0, 0)),
            pl.BlockSpec((rows, tile), lambda i: (0, i)),
        ],
        out_specs=[pl.BlockSpec((cut, tile), lambda i: (0, i)) for cut in cuts],
        out_shape=[jax.ShapeDtypeStruct((cut, width), BF16) for cut in cuts],
        scratch_shapes=[pltpu.VMEM((tokens, rows), BF16)],
        compiler_params=pltpu.CompilerParams(vmem_limit_bytes=20 * MIB),
        cost_estimate=SMALL,
    )(near, far, flat)


def add_body(heights, *refs):
    out_refs = refs[sum(heights) :]
    groups, at = [], 0
    for height in heights:
        groups.append(refs[at : at + height])
        at += height
    tops = [[sum(r.shape[0] for r in group[:n]) for n in range(len(group) + 1)] for group in groups]
    height = out_refs[0].shape[0]
    edges = {edge for top in tops for edge in top} | {n * height for n in range(len(out_refs) + 1)}
    edges = sorted(edges)
    for low, high in zip(edges[:-1], edges[1:]):
        total = None
        for group, top in zip(groups, tops):
            for n, ref in enumerate(group):
                if top[n] <= low and high <= top[n + 1]:
                    part = ref[low - top[n] : high - top[n], :].astype(F32)
                    total = part if total is None else total + part
        out_refs[low // height][low % height : low % height + high - low, :] = total.astype(BF16)


def add_kernel(*groups, cut=1):
    rows, width = sum(x.shape[0] for x in groups[0]) // cut, groups[0][0].shape[1]
    tile = min(1024, width)
    arrays = [x for group in groups for x in group]
    return pl.pallas_call(
        functools.partial(add_body, [len(group) for group in groups]),
        grid=(width // tile,),
        in_specs=[pl.BlockSpec((x.shape[0], tile), lambda i: (0, i)) for x in arrays],
        out_specs=[pl.BlockSpec((rows, tile), lambda i: (0, i))] * cut,
        out_shape=[jax.ShapeDtypeStruct((rows, width), BF16)] * cut,
        compiler_params=pltpu.CompilerParams(vmem_limit_bytes=8 * MIB),
        cost_estimate=SMALL,
    )(*arrays)


def copy_body(in_ref, out_ref):
    out_ref[...] = in_ref[...]


def copy_kernel(x):
    rows, width = x.shape
    tile = rows // 4
    return pl.pallas_call(
        copy_body,
        grid=(4,),
        in_specs=[pl.BlockSpec((tile, width), lambda i: (i, 0))],
        out_specs=pl.BlockSpec((tile, width), lambda i: (i, 0)),
        out_shape=jax.ShapeDtypeStruct(x.shape, x.dtype),
        compiler_params=pltpu.CompilerParams(vmem_limit_bytes=8 * MIB),
        cost_estimate=SMALL,
    )(x)


def on_device(ring, n_tp, tokens_in, w_query, w_key, w_value, short_taps, long_taps, grad_out):
    chips = len(ring)
    half = chips // 2
    n_ctx = 2 * chips
    held, width = tokens_in.shape
    channels = w_query.shape[1]
    weights = (w_query, w_key, w_value)

    def one_way(x, turned=False, to_mate=False):
        hops = []
        for j in range(chips):
            for core in range(2):
                chip = ring[(j + (1 if (core == 0) != turned else -1)) % chips]
                hops.append((2 * ring[j] + core, 2 * chip + (core ^ int(to_mate))))
        return lax.ppermute(x, "ctx", hops)

    def swap(x):
        return lax.ppermute(x, "ctx", [(d, d ^ 1) for d in range(n_ctx)])

    table = np.zeros((n_ctx, n_ctx), np.int32)
    for device in range(n_ctx):
        place, core = ring.index(device // 2), device % 2
        way = -1 if core == 0 else 1
        items = [(0, 0), (0, 1)]
        for s in range(1, half):
            items += [(way * s, 0), (way * s, 1), (-way * s, 1), (-way * s, 0)]
        items += [(half, 0), (half, 1)]
        table[device] = [2 * ring[(place + hop) % chips] + (core ^ other) for hop, other in items]
    order = lax.dynamic_index_in_dim(jnp.asarray(table), lax.axis_index("ctx"), 0, keepdims=False)
    short_kernel, long_kernel = short_taps.reshape(3, -1, SHORT), long_taps.reshape(-1, LONG)
    turned_kernel = turn_taps(long_kernel)

    stay = 3 * channels
    if n_tp == 2:
        t = lax.axis_index("tp").astype(jnp.int32)
        t, order, short_kernel, turned_kernel = lax.optimization_barrier((t, order, short_kernel, turned_kernel))
        flat = restack(t, weights)
    else:
        flat = jnp.stack(weights).reshape(-1, width)

    def project(pieces):
        if n_tp == 2:
            return project_kernel(flat, pieces)
        y = dot(flat, jnp.concatenate(pieces, axis=0), ((1,), (1,))).astype(BF16).reshape(3, n_tp, channels, -1)
        return lax.psum_scatter(y, "tp", scatter_dimension=1, tiled=True).reshape(stay, -1), None

    def across(x):
        return None if x is None else lax.ppermute(x, "tp", [(0, 1), (1, 0)])

    def meet(d):
        if n_tp == 2:
            return d.reshape(stay, -1), across(d.reshape(stay, -1))
        d = lax.all_gather(d.reshape(3, 1, channels, -1), "tp", axis=1, tiled=True)
        return (d.reshape(-1, d.shape[-1]),)

    def unproject(d, *cuts):
        if n_tp == 2:
            return unproject_kernel(flat, *d, cuts)
        y = dot(d[0], flat, ((0,), (0,))).astype(BF16)
        return jnp.split(y, np.cumsum(cuts)[:-1], axis=0)

    stage = lax.optimization_barrier

    arrived = [one_way(tokens_in), one_way(tokens_in, to_mate=True, turned=True)]
    near, far = project([tokens_in, swap(tokens_in)])
    arrived, near, far = stage((arrived, near, far))
    arrived = jnp.concatenate(arrived, axis=0)
    projected = []
    for s in range(1, half):
        coming = one_way(arrived if s < half - 1 else arrived[:held])
        projected.append((near, across(far)))
        near, far = project([arrived, swap(arrived)])
        if s < half - 1:
            arrived, near, far, projected[-1] = stage((coming, near, far, projected[-1]))
    crossed = across(far)
    arrived, near, grad_out = stage((coming, near, grad_out))
    incoming = lax.all_to_all(
        grad_out.reshape(n_ctx, channels, held), "ctx", split_axis=0, concat_axis=0, tiled=True
    )
    shared, projected[-1] = stage((arrived, projected[-1]))
    last, far = project([arrived, swap(shared[: held // 2]), swap(shared[held // 2 :])])
    projected += [(near, crossed), (last, across(far))]

    mixed, d_proj, grad_short, grad_long = mix(
        order,
        short_kernel,
        long_kernel,
        turned_kernel,
        incoming,
        [[y.reshape(3, channels, -1) for y in side] for side in zip(*projected) if side[0] is not None],
        [[s] for s in range(half + 1)],
    )

    first, met, later = [meet(d_proj[s]) for s in (half, half - 1, half - 2)]
    mixed_out = lax.all_to_all(mixed, "ctx", split_axis=0, concat_axis=0, tiled=True).reshape(-1, held)
    first, grad_short, grad_long = stage((first, grad_short, grad_long))
    keep, *give = unproject(first, held, *((80, 48) if held == 128 else (held // 2, held // 2)))
    total = add_kernel([keep], [swap(x) for x in give])
    total, met, rest = stage((total, met, d_proj[: half - 2]))
    for s in range(half - 1, 0, -1):
        coming = one_way(total[0], turned=True)
        if s < half - 1:
            later = meet(rest[-1])
            rest = rest[:-1]
        cuts = (96, 96, 64) if s == half - 1 and held == 128 else (held, held)
        keep, *give = unproject(met, 2 * held, *cuts)
        give[-1], later = stage((give[-1], later))
        total = add_kernel([keep], [swap(x) for x in give], [coming], cut=2 if s == 1 else 1)
        if s == half - 2:
            mixed_out = copy_kernel(mixed_out)
        total, met, rest, mixed_out = stage((total, later, rest, mixed_out))
    coming = [one_way(total[0], turned=True), one_way(total[1], turned=True, to_mate=True)]
    keep, *give = unproject(met, held, held // 2, held // 2)
    (grad_tokens,) = add_kernel([keep], [swap(x) for x in give], coming[:1], coming[1:])
    return (
        mixed_out,
        grad_tokens,
        grad_short.reshape(3, 1, -1, SHORT),
        grad_long.reshape(1, -1, LONG),
    )


def solution(mesh):
    placed = (
        P("ctx", "tp"),
        P(None, "ctx", "tp"),
        P(None, "ctx", "tp"),
        P(None, "ctx", "tp"),
        P(None, "tp", "ctx", None),
        P("tp", "ctx", None),
        P("tp", "ctx"),
    )
    return jax.shard_map(
        functools.partial(on_device, ring_of(mesh), mesh.shape["tp"]),
        mesh=mesh,
        in_specs=placed,
        out_specs=(
            P("tp", "ctx"),
            P("ctx", "tp"),
            P(None, "tp", "ctx", None),
            P("tp", "ctx", None),
        ),
        check_vma=False,
    )
```

```python
import functools

import jax
import jax.numpy as jnp
import numpy as np
from jax import lax
from jax.experimental import pallas as pl
from jax.experimental.pallas import tpu as pltpu
from jax.sharding import PartitionSpec as P

GROUP = 16
SHORT = 3
LONG = 128
F32 = jnp.float32
BF16 = jnp.bfloat16
MIB = 1024 * 1024
SMALL = pl.CostEstimate(flops=1, bytes_accessed=1, transcendentals=0)


def ring_of(mesh):
    chips = mesh.shape["ctx"] // 2
    plain = list(range(chips))
    devices = np.asarray(mesh.devices).reshape(mesh.shape["ctx"], -1)[:, 0]
    places = [getattr(devices[2 * chip], "coords", None) for chip in plain]
    if any(place is None for place in places):
        return plain
    places = np.array([list(place)[:3] for place in places])
    axes = [axis for axis in range(3) if len(set(places[:, axis])) > 1]
    if len(axes) != 2:
        return plain
    rung = min(axes, key=lambda axis: len(set(places[:, axis])))
    along = axes[0] if rung == axes[1] else axes[1]
    sides = sorted(set(places[:, rung]))
    if len(sides) != 2:
        return plain
    there = [c for c in plain if places[c, rung] == sides[0]]
    back = [c for c in plain if places[c, rung] == sides[1]]
    there.sort(key=lambda c: places[c, along])
    back.sort(key=lambda c: -places[c, along])
    return there + back


def dot(a, b, dims):
    return lax.dot_general(a, b, (dims, ((), ())), preferred_element_type=F32)


def turn_taps(taps):
    return jnp.roll(jnp.flip(taps, axis=1), 1, axis=1)


def shift_matrix(way):
    at = np.arange(2 * LONG)
    place = np.where(at < LONG, at, at - (2 * LONG if way < 0 else 0))
    out = np.arange(LONG)
    return np.concatenate([place[:, None] - out[None, :] == way * k for k in (1, 2)], axis=1).astype(np.float32)


def mix_body(count, sets, per_turn, grouped, order, short_ref, long_ref, turned_ref, past_ref, next_ref, g_ref, *refs):
    proj_refs = [refs[s * count : (s + 1) * count] for s in range(sets)]
    refs = refs[sets * count :]
    d_count = len(grouped)
    mixed_ref, d_refs, gs_ref, gl_ref = refs[0], refs[1 : 1 + d_count], refs[1 + d_count], refs[2 + d_count]
    p_s, m_s, f_s, x_s, y_s, q_s, d_s, e_s = refs[3 + d_count :]
    blocks = g_ref.shape[0]
    rows = blocks * GROUP
    step = pl.program_id(0)

    @pl.when(step == 0)
    def _():
        p_s[:, :, 0:GROUP, :] = jnp.zeros((per_turn, 3, GROUP, LONG), BF16)
        x_s[:, 0:GROUP, :] = jnp.zeros((per_turn, GROUP, LONG), BF16)
        y_s[:, rows:, :] = jnp.zeros((per_turn, GROUP, LONG), BF16)
        d_s[:, :, rows:, :] = jnp.zeros((per_turn, 3, GROUP, LONG), BF16)

    halves = [(a, h) for a in range(count) for h in range(proj_refs[0][a].shape[2] // LONG)]
    places = [(a, h, where) for where, (a, h) in enumerate(halves)]
    d_places = []
    for b, arrays in enumerate(grouped):
        inside = [where for array in arrays for a, _, where in places if a == array]
        d_places += [(b, h, where) for h, where in enumerate(inside)]
    zero = jnp.zeros((GROUP, LONG), F32)
    at_block = [slice(n * GROUP, (n + 1) * GROUP) for n in range(blocks)]
    sub8 = lax.broadcasted_iota(jnp.int32, (8, LONG), 0)
    col = lax.broadcasted_iota(jnp.int32, (LONG, LONG), 1)
    row = lax.broadcasted_iota(jnp.int32, (LONG, LONG), 0)

    per_step = gl_ref.shape[1]

    @pl.loop(0, per_step // per_turn)
    def _(turn):
        every = range(per_turn)
        mine = [pl.ds(pl.multiple_of((turn * per_turn + j) * GROUP, GROUP), GROUP) for j in every]
        lines = [turn * per_turn + j for j in every]
        taps = [
            [[short_ref[i, step * per_step + lines[j], k] for k in range(SHORT)] for i in range(3)] for j in every
        ]
        for a, h, where in places:
            at = pl.multiple_of((order[where] + 1) * GROUP, GROUP)
            for j in every:
                for i in range(3):
                    part = proj_refs[0][a][i, mine[j], h * LONG : (h + 1) * LONG].astype(F32)
                    for s in range(1, sets):
                        part = part + proj_refs[s][a][i, mine[j], h * LONG : (h + 1) * LONG].astype(F32)
                    p_s[j, i, pl.ds(at, GROUP), :] = part.astype(BF16)

        signals = [(j, i) for j in every for i in range(3)]
        two_blocks = [jnp.concatenate([p_s[j, i, GROUP:, :], p_s[j, i, :rows, :]], axis=1) for j, i in signals]
        past = dot(jnp.concatenate(two_blocks, axis=0), past_ref[...], ((1,), (0,))).astype(BF16)
        for n, (j, i) in enumerate(signals):
            m_s[j, i] = past[n * rows : (n + 1) * rows]
        for j in every:
            for at in at_block:
                feat = []
                for i in range(3):
                    here = p_s[j, i, at.stop : at.stop + GROUP, :].astype(F32)
                    past = m_s[j, i, at, :].astype(F32)
                    feat.append(taps[j][i][0] * here + taps[j][i][1] * past[:, :LONG] + taps[j][i][2] * past[:, LONG:])
                    f_s[j, i, at, :] = feat[i]
                x_s[j, at.stop : at.stop + GROUP, :] = (feat[1] * feat[2]).astype(BF16)

        filters, turned = [], []
        for j in every:
            for ref, made in ((long_ref, filters), (turned_ref, turned)):
                base = jnp.broadcast_to(ref[0, pl.ds(lines[j], 1), :], (8, LONG))
                for bit in (1, 2, 4):
                    base = jnp.where((sub8 & bit) != 0, pltpu.roll(base, bit, 1), base)
                full = jnp.concatenate([base] + [pltpu.roll(base, 8 * m, 1) for m in range(1, LONG // 8)], axis=0)
                inside = col >= row if made is filters else col <= row
                near = jnp.where(inside, full, 0.0).astype(BF16)
                far = jnp.where(inside, 0.0, full).astype(BF16)
                made.append(jnp.concatenate([near, far], axis=0))

        x_twos = [jnp.concatenate([x_s[j, GROUP:, :], x_s[j, :rows, :]], axis=1) for j in every]
        inners = [dot(x_twos[j], filters[j], ((1,), (0,))) for j in every]
        for j in every:
            for n, at in enumerate(at_block):
                g = g_ref[n, mine[j], :].astype(F32)
                feat, inner = f_s[j, 0, at, :], inners[j][at]
                mixed_ref[n, mine[j], :] = (feat * inner).astype(BF16)
                y_s[j, at, :] = (g * feat).astype(BF16)
                q_s[j, at, :] = g * inner
        d_products = []
        for j in every:
            y_two = jnp.concatenate([y_s[j, :rows, :], y_s[j, GROUP:, :]], axis=1)
            d_products.append(dot(y_two, turned[j], ((1,), (0,))))
        folds = [dot(y_s[j, :rows, :], x_twos[j], ((0,), (0,))) for j in every]
        for j in every:
            fold = jnp.where(col <= row, folds[j][:, :LONG], folds[j][:, LONG:])
            width = LONG
            while width > 8:
                width //= 2
                fold = fold[:width] + pltpu.roll(fold[width:], LONG - width, 1)
            for bit in (4, 2, 1):
                fold = jnp.where((sub8 & bit) != 0, pltpu.roll(fold, LONG - bit, 1), fold)
            gl_ref[0, pl.ds(lines[j], 1), :] = jnp.sum(fold, axis=0, keepdims=True)

        for j in every:
            sums = [[zero] * SHORT for _ in range(3)]
            for at in at_block:
                d_product = d_products[j][at]
                for i, d in enumerate((q_s[j, at, :], d_product * f_s[j, 2, at, :], d_product * f_s[j, 1, at, :])):
                    here = p_s[j, i, at.stop : at.stop + GROUP, :].astype(F32)
                    past = m_s[j, i, at, :].astype(F32)
                    seen = (here, past[:, :LONG], past[:, LONG:])
                    sums[i] = [total + d * p for total, p in zip(sums[i], seen)]
                    d_s[j, i, at, :] = d.astype(BF16)
            for i in range(3):
                for k in range(SHORT):
                    gs_ref[0, lines[j], 3 * i + k : 3 * i + k + 1, :] = jnp.sum(sums[i][k], axis=0, keepdims=True)
        two_blocks = [jnp.concatenate([d_s[j, i, :rows, :], d_s[j, i, GROUP:, :]], axis=1) for j, i in signals]
        coming = dot(jnp.concatenate(two_blocks, axis=0), next_ref[...], ((1,), (0,)))
        for n, (j, i) in enumerate(signals):
            for at in at_block:
                here = d_s[j, i, at, :].astype(F32)
                moved = coming[n * rows + at.start : n * rows + at.stop]
                e_s[j, i, at, :] = (
                    taps[j][i][0] * here + taps[j][i][1] * moved[:, :LONG] + taps[j][i][2] * moved[:, LONG:]
                ).astype(BF16)
        for a, h, where in d_places:
            at = pl.multiple_of(order[where] * GROUP, GROUP)
            for j in every:
                for i in range(3):
                    d_refs[a][i, mine[j], h * LONG : (h + 1) * LONG] = e_s[j, i, pl.ds(at, GROUP), :]


def mix(order, short_kernel, long_kernel, turned_kernel, g, proj_sets, grouped):
    blocks, channels, _ = g.shape
    count, sets = len(proj_sets[0]), len(proj_sets)
    groups = channels // GROUP
    per_turn = next(n for n in (2, 1) if groups % n == 0)
    per_step = next(n for n in (4, 2, 1) if groups % n == 0)
    steps = groups // per_step
    rows = blocks * GROUP
    high = per_step * GROUP
    proj_specs = [pl.BlockSpec((3, high, x.shape[2]), lambda i, o: (0, i, 0)) for x in proj_sets[0]]
    d_widths = [sum(proj_sets[0][a].shape[2] for a in arrays) for arrays in grouped]
    d_specs = [pl.BlockSpec((3, high, w), lambda i, o: (0, i, 0)) for w in d_widths]
    token_spec = pl.BlockSpec((blocks, high, LONG), lambda i, o: (0, i, 0))
    shifts = [jnp.asarray(shift_matrix(way), BF16) for way in (-1, 1)]
    outs = pl.pallas_call(
        functools.partial(mix_body, count, sets, per_turn, grouped),
        grid_spec=pltpu.PrefetchScalarGridSpec(
            num_scalar_prefetch=1,
            grid=(steps,),
            in_specs=[
                pl.BlockSpec(memory_space=pltpu.SMEM),
                pl.BlockSpec((1, per_step, LONG), lambda i, o: (i, 0, 0)),
                pl.BlockSpec((1, per_step, LONG), lambda i, o: (i, 0, 0)),
                pl.BlockSpec((2 * LONG, 2 * LONG), lambda i, o: (0, 0)),
                pl.BlockSpec((2 * LONG, 2 * LONG), lambda i, o: (0, 0)),
                token_spec,
            ]
            + proj_specs * sets,
            out_specs=[token_spec]
            + d_specs
            + [
                pl.BlockSpec((1, per_step, 3 * SHORT, LONG), lambda i, o: (i, 0, 0, 0)),
                pl.BlockSpec((1, per_step, LONG), lambda i, o: (i, 0, 0)),
            ],
            scratch_shapes=[
                pltpu.VMEM((per_turn, 3, rows + GROUP, LONG), BF16),
                pltpu.VMEM((per_turn, 3, rows, 2 * LONG), BF16),
                pltpu.VMEM((per_turn, 3, rows, LONG), F32),
                pltpu.VMEM((per_turn, rows + GROUP, LONG), BF16),
                pltpu.VMEM((per_turn, rows + GROUP, LONG), BF16),
                pltpu.VMEM((per_turn, rows, LONG), F32),
                pltpu.VMEM((per_turn, 3, rows + GROUP, LONG), BF16),
                pltpu.VMEM((per_turn, 3, rows, LONG), BF16),
            ],
        ),
        out_shape=[jax.ShapeDtypeStruct((blocks, channels, LONG), BF16)]
        + [jax.ShapeDtypeStruct((3, channels, w), BF16) for w in d_widths]
        + [
            jax.ShapeDtypeStruct((steps, per_step, 3 * SHORT, LONG), F32),
            jax.ShapeDtypeStruct((steps, per_step, LONG), F32),
        ],
        compiler_params=pltpu.CompilerParams(vmem_limit_bytes=58 * MIB),
        cost_estimate=SMALL,
    )(order, short_kernel, long_kernel.reshape(steps, per_step, LONG), turned_kernel.reshape(steps, per_step, LONG), *shifts, g, *[x for s in proj_sets for x in s])
    mixed, d_proj, (gs, gl) = outs[0], outs[1:-2], outs[-2:]
    grad_short = jnp.sum(gs, axis=-1).reshape(groups, 3, SHORT).transpose(1, 0, 2)
    grad_long = turn_taps(gl.reshape(groups, LONG))
    return mixed, d_proj, grad_short, grad_long


def restack_body(t_ref, *refs):
    out_ref = refs[3]
    for i in range(3):
        out_ref[0, i] = refs[i][0]


def restack(t, weights):
    _, channels, width = weights[0].shape
    tile = min(128, channels)

    def source(side, part, t):
        return (jnp.where(side == 0, t[0], 1 - t[0]), part, 0)

    return pl.pallas_call(
        restack_body,
        grid_spec=pltpu.PrefetchScalarGridSpec(
            num_scalar_prefetch=1,
            grid=(2, channels // tile),
            in_specs=[pl.BlockSpec((1, tile, width), source)] * 3,
            out_specs=pl.BlockSpec((1, 3, tile, width), lambda side, part, t: (side, 0, part, 0)),
        ),
        out_shape=jax.ShapeDtypeStruct((2, 3, channels, width), BF16),
        compiler_params=pltpu.CompilerParams(vmem_limit_bytes=16 * MIB),
        cost_estimate=SMALL,
    )(t.reshape(1), *weights).reshape(6 * channels, width)


def project_body(pieces, *refs):
    x_refs, w_ref = refs[:pieces], refs[pieces]
    far_ref, near_ref, x_s, sems = refs[pieces + 1 :]
    step, steps = pl.program_id(0), pl.num_programs(0)

    @pl.when(step == 0)
    def _():
        copies, at = [], 0
        for n, x in enumerate(x_refs):
            copies.append(pltpu.make_async_copy(x, x_s.at[pl.ds(at, x.shape[0])], sems.at[n]))
            at += x.shape[0]
        for copy in copies:
            copy.start()
        for copy in copies:
            copy.wait()

    got = dot(w_ref[...], x_s[...], ((1,), (1,))).astype(BF16)

    @pl.when(step < steps // 2)
    def _():
        far_ref[...] = got

    @pl.when(step >= steps // 2)
    def _():
        near_ref[...] = got


def project_kernel(flat, pieces):
    rows, width = flat.shape
    tokens = sum(x.shape[0] for x in pieces)
    tile = rows // 4
    half = jax.ShapeDtypeStruct((rows // 2, tokens), BF16)
    far, near = pl.pallas_call(
        functools.partial(project_body, len(pieces)),
        grid=(4,),
        in_specs=[pl.BlockSpec(memory_space=pl.ANY)] * len(pieces)
        + [pl.BlockSpec((tile, width), lambda i: ((i + 2) % 4, 0))],
        out_specs=[
            pl.BlockSpec((tile, tokens), lambda i: (jnp.minimum(i, 1), 0)),
            pl.BlockSpec((tile, tokens), lambda i: (jnp.maximum(i - 2, 0), 0)),
        ],
        out_shape=[half, half],
        scratch_shapes=[pltpu.VMEM((tokens, width), BF16), pltpu.SemaphoreType.DMA((len(pieces),))],
        compiler_params=pltpu.CompilerParams(vmem_limit_bytes=16 * MIB),
        cost_estimate=SMALL,
    )(*pieces, flat)
    return near, far


def unproject_body(near_ref, far_ref, w_ref, *refs):
    out_refs, d_s = refs[:-1], refs[-1]
    stay = near_ref.shape[0]

    @pl.when(pl.program_id(0) == 0)
    def _():
        d_s[:, 0:stay] = near_ref[...].T
        d_s[:, stay:] = far_ref[...].T

    got = dot(d_s[...], w_ref[...], ((1,), (0,)))
    at = 0
    for out_ref in out_refs:
        out_ref[...] = got[at : at + out_ref.shape[0]].astype(BF16)
        at += out_ref.shape[0]


def unproject_kernel(flat, near, far, cuts):
    rows, width = flat.shape
    tokens = near.shape[1]
    tile = min(1024, width)
    return pl.pallas_call(
        unproject_body,
        grid=(width // tile,),
        in_specs=[
            pl.BlockSpec((rows // 2, tokens), lambda i: (0, 0)),
            pl.BlockSpec((rows // 2, tokens), lambda i: (0, 0)),
            pl.BlockSpec((rows, tile), lambda i: (0, i)),
        ],
        out_specs=[pl.BlockSpec((cut, tile), lambda i: (0, i)) for cut in cuts],
        out_shape=[jax.ShapeDtypeStruct((cut, width), BF16) for cut in cuts],
        scratch_shapes=[pltpu.VMEM((tokens, rows), BF16)],
        compiler_params=pltpu.CompilerParams(vmem_limit_bytes=20 * MIB),
        cost_estimate=SMALL,
    )(near, far, flat)


def add_body(heights, *refs):
    out_refs = refs[sum(heights) :]
    groups, at = [], 0
    for height in heights:
        groups.append(refs[at : at + height])
        at += height
    tops = [[sum(r.shape[0] for r in group[:n]) for n in range(len(group) + 1)] for group in groups]
    height = out_refs[0].shape[0]
    edges = {edge for top in tops for edge in top} | {n * height for n in range(len(out_refs) + 1)}
    edges = sorted(edges)
    for low, high in zip(edges[:-1], edges[1:]):
        total = None
        for group, top in zip(groups, tops):
            for n, ref in enumerate(group):
                if top[n] <= low and high <= top[n + 1]:
                    part = ref[low - top[n] : high - top[n], :].astype(F32)
                    total = part if total is None else total + part
        out_refs[low // height][low % height : low % height + high - low, :] = total.astype(BF16)


def add_kernel(*groups, cut=1):
    rows, width = sum(x.shape[0] for x in groups[0]) // cut, groups[0][0].shape[1]
    tile = min(1024, width)
    arrays = [x for group in groups for x in group]
    return pl.pallas_call(
        functools.partial(add_body, [len(group) for group in groups]),
        grid=(width // tile,),
        in_specs=[pl.BlockSpec((x.shape[0], tile), lambda i: (0, i)) for x in arrays],
        out_specs=[pl.BlockSpec((rows, tile), lambda i: (0, i))] * cut,
        out_shape=[jax.ShapeDtypeStruct((rows, width), BF16)] * cut,
        compiler_params=pltpu.CompilerParams(vmem_limit_bytes=8 * MIB),
        cost_estimate=SMALL,
    )(*arrays)


def copy_body(in_ref, out_ref):
    out_ref[...] = in_ref[...]


def copy_kernel(x):
    rows, width = x.shape
    tile = rows // 4
    return pl.pallas_call(
        copy_body,
        grid=(4,),
        in_specs=[pl.BlockSpec((tile, width), lambda i: (i, 0))],
        out_specs=pl.BlockSpec((tile, width), lambda i: (i, 0)),
        out_shape=jax.ShapeDtypeStruct(x.shape, x.dtype),
        compiler_params=pltpu.CompilerParams(vmem_limit_bytes=8 * MIB),
        cost_estimate=SMALL,
    )(x)


def on_device(ring, n_tp, tokens_in, w_query, w_key, w_value, short_taps, long_taps, grad_out):
    chips = len(ring)
    half = chips // 2
    n_ctx = 2 * chips
    held, width = tokens_in.shape
    channels = w_query.shape[1]
    weights = (w_query, w_key, w_value)

    def one_way(x, turned=False, to_mate=False):
        hops = []
        for j in range(chips):
            for core in range(2):
                chip = ring[(j + (1 if (core == 0) != turned else -1)) % chips]
                hops.append((2 * ring[j] + core, 2 * chip + (core ^ int(to_mate))))
        return lax.ppermute(x, "ctx", hops)

    def swap(x):
        return lax.ppermute(x, "ctx", [(d, d ^ 1) for d in range(n_ctx)])

    table = np.zeros((n_ctx, n_ctx), np.int32)
    for device in range(n_ctx):
        place, core = ring.index(device // 2), device % 2
        way = -1 if core == 0 else 1
        items = [(0, 0), (0, 1)]
        for s in range(1, half):
            items += [(way * s, 0), (way * s, 1), (-way * s, 1), (-way * s, 0)]
        items += [(half, 0), (half, 1)]
        table[device] = [2 * ring[(place + hop) % chips] + (core ^ other) for hop, other in items]
    order = lax.dynamic_index_in_dim(jnp.asarray(table), lax.axis_index("ctx"), 0, keepdims=False)
    short_kernel, long_kernel = short_taps.reshape(3, -1, SHORT), long_taps.reshape(-1, LONG)
    turned_kernel = turn_taps(long_kernel)

    stay = 3 * channels
    if n_tp == 2:
        t = lax.axis_index("tp").astype(jnp.int32)
        t, order, short_kernel, turned_kernel = lax.optimization_barrier((t, order, short_kernel, turned_kernel))
        flat = restack(t, weights)
    else:
        flat = jnp.stack(weights).reshape(-1, width)

    def project(pieces):
        if n_tp == 2:
            return project_kernel(flat, pieces)
        y = dot(flat, jnp.concatenate(pieces, axis=0), ((1,), (1,))).astype(BF16).reshape(3, n_tp, channels, -1)
        return lax.psum_scatter(y, "tp", scatter_dimension=1, tiled=True).reshape(stay, -1), None

    def across(x):
        return None if x is None else lax.ppermute(x, "tp", [(0, 1), (1, 0)])

    def meet(d):
        if n_tp == 2:
            return d.reshape(stay, -1), across(d.reshape(stay, -1))
        d = lax.all_gather(d.reshape(3, 1, channels, -1), "tp", axis=1, tiled=True)
        return (d.reshape(-1, d.shape[-1]),)

    def unproject(d, *cuts):
        if n_tp == 2:
            return unproject_kernel(flat, *d, cuts)
        y = dot(d[0], flat, ((0,), (0,))).astype(BF16)
        return jnp.split(y, np.cumsum(cuts)[:-1], axis=0)

    stage = lax.optimization_barrier

    arrived = [one_way(tokens_in), one_way(tokens_in, to_mate=True, turned=True)]
    near, far = project([tokens_in, swap(tokens_in)])
    arrived, near, far = stage((arrived, near, far))
    arrived = jnp.concatenate(arrived, axis=0)
    projected = []
    for s in range(1, half):
        coming = one_way(arrived if s < half - 1 else arrived[:held])
        projected.append((near, across(far)))
        near, far = project([arrived, swap(arrived)])
        if s < half - 1:
            arrived, near, far, projected[-1] = stage((coming, near, far, projected[-1]))
    crossed = across(far)
    arrived, near, grad_out = stage((coming, near, grad_out))
    incoming = lax.all_to_all(
        grad_out.reshape(n_ctx, channels, held), "ctx", split_axis=0, concat_axis=0, tiled=True
    )
    shared, projected[-1] = stage((arrived, projected[-1]))
    last, far = project([arrived, swap(shared[: held // 2]), swap(shared[held // 2 :])])
    projected += [(near, crossed), (last, across(far))]

    mixed, d_proj, grad_short, grad_long = mix(
        order,
        short_kernel,
        long_kernel,
        turned_kernel,
        incoming,
        [[y.reshape(3, channels, -1) for y in side] for side in zip(*projected) if side[0] is not None],
        [[s] for s in range(half + 1)],
    )

    first, met, later = [meet(d_proj[s]) for s in (half, half - 1, half - 2)]
    mixed_out = lax.all_to_all(mixed, "ctx", split_axis=0, concat_axis=0, tiled=True).reshape(-1, held)
    first, grad_short, grad_long = stage((first, grad_short, grad_long))
    keep, *give = unproject(first, held, *((80, 48) if held == 128 else (held // 2, held // 2)))
    total = add_kernel([keep], [swap(x) for x in give])
    total, met, rest = stage((total, met, d_proj[: half - 2]))
    for s in range(half - 1, 0, -1):
        coming = one_way(total[0], turned=True)
        if s < half - 1:
            later = meet(rest[-1])
            rest = rest[:-1]
        cuts = (96, 96, 64) if s == half - 1 and held == 128 else (held, held)
        keep, *give = unproject(met, 2 * held, *cuts)
        give[-1], later = stage((give[-1], later))
        total = add_kernel([keep], [swap(x) for x in give], [coming], cut=2 if s == 1 else 1)
        if s == half - 2:
            mixed_out = copy_kernel(mixed_out)
        total, met, rest, mixed_out = stage((total, later, rest, mixed_out))
    coming = [one_way(total[0], turned=True), one_way(total[1], turned=True, to_mate=True)]
    keep, *give = unproject(met, held, held // 2, held // 2)
    (grad_tokens,) = add_kernel([keep], [swap(x) for x in give], coming[:1], coming[1:])
    return (
        mixed_out,
        grad_tokens,
        grad_short.reshape(3, 1, -1, SHORT),
        grad_long.reshape(1, -1, LONG),
    )


def solution(mesh):
    placed = (
        P("ctx", "tp"),
        P(None, "ctx", "tp"),
        P(None, "ctx", "tp"),
        P(None, "ctx", "tp"),
        P(None, "tp", "ctx", None),
        P("tp", "ctx", None),
        P("tp", "ctx"),
    )
    return jax.shard_map(
        functools.partial(on_device, ring_of(mesh), mesh.shape["tp"]),
        mesh=mesh,
        in_specs=placed,
        out_specs=(
            P("tp", "ctx"),
            P("ctx", "tp"),
            P(None, "tp", "ctx", None),
            P("tp", "ctx", None),
        ),
        check_vma=False,
    )
```

```python
import functools

import jax
import jax.numpy as jnp
import numpy as np
from jax import lax
from jax.experimental import pallas as pl
from jax.experimental.pallas import tpu as pltpu
from jax.sharding import PartitionSpec as P

GROUP = 16
SHORT = 3
LONG = 128
F32 = jnp.float32
BF16 = jnp.bfloat16
MIB = 1024 * 1024
SMALL = pl.CostEstimate(flops=1, bytes_accessed=1, transcendentals=0)


def ring_of(mesh):
    chips = mesh.shape["ctx"] // 2
    plain = list(range(chips))
    devices = np.asarray(mesh.devices).reshape(mesh.shape["ctx"], -1)[:, 0]
    places = [getattr(devices[2 * chip], "coords", None) for chip in plain]
    if any(place is None for place in places):
        return plain
    places = np.array([list(place)[:3] for place in places])
    axes = [axis for axis in range(3) if len(set(places[:, axis])) > 1]
    if len(axes) != 2:
        return plain
    rung = min(axes, key=lambda axis: len(set(places[:, axis])))
    along = axes[0] if rung == axes[1] else axes[1]
    sides = sorted(set(places[:, rung]))
    if len(sides) != 2:
        return plain
    there = [c for c in plain if places[c, rung] == sides[0]]
    back = [c for c in plain if places[c, rung] == sides[1]]
    there.sort(key=lambda c: places[c, along])
    back.sort(key=lambda c: -places[c, along])
    return there + back


def dot(a, b, dims):
    return lax.dot_general(a, b, (dims, ((), ())), preferred_element_type=F32)


def turn_taps(taps):
    return jnp.roll(jnp.flip(taps, axis=1), 1, axis=1)


def shift_matrix(way):
    at = np.arange(2 * LONG)
    place = np.where(at < LONG, at, at - (2 * LONG if way < 0 else 0))
    out = np.arange(LONG)
    return np.concatenate([place[:, None] - out[None, :] == way * k for k in (1, 2)], axis=1).astype(np.float32)


def mix_body(count, sets, per_turn, grouped, order, short_ref, long_ref, turned_ref, past_ref, next_ref, g_ref, *refs):
    proj_refs = [refs[s * count : (s + 1) * count] for s in range(sets)]
    refs = refs[sets * count :]
    d_count = len(grouped)
    mixed_ref, d_refs, gs_ref, gl_ref = refs[0], refs[1 : 1 + d_count], refs[1 + d_count], refs[2 + d_count]
    p_s, m_s, f_s, x_s, y_s, q_s, d_s, e_s = refs[3 + d_count :]
    blocks = g_ref.shape[0]
    rows = blocks * GROUP
    step = pl.program_id(0)

    @pl.when(step == 0)
    def _():
        p_s[:, :, 0:GROUP, :] = jnp.zeros((per_turn, 3, GROUP, LONG), BF16)
        x_s[:, 0:GROUP, :] = jnp.zeros((per_turn, GROUP, LONG), BF16)
        y_s[:, rows:, :] = jnp.zeros((per_turn, GROUP, LONG), BF16)
        d_s[:, :, rows:, :] = jnp.zeros((per_turn, 3, GROUP, LONG), BF16)

    halves = [(a, h) for a in range(count) for h in range(proj_refs[0][a].shape[2] // LONG)]
    places = [(a, h, where) for where, (a, h) in enumerate(halves)]
    d_places = []
    for b, arrays in enumerate(grouped):
        inside = [where for array in arrays for a, _, where in places if a == array]
        d_places += [(b, h, where) for h, where in enumerate(inside)]
    zero = jnp.zeros((GROUP, LONG), F32)
    at_block = [slice(n * GROUP, (n + 1) * GROUP) for n in range(blocks)]
    sub8 = lax.broadcasted_iota(jnp.int32, (8, LONG), 0)
    col = lax.broadcasted_iota(jnp.int32, (LONG, LONG), 1)
    row = lax.broadcasted_iota(jnp.int32, (LONG, LONG), 0)

    per_step = gl_ref.shape[1]

    @pl.loop(0, per_step // per_turn)
    def _(turn):
        every = range(per_turn)
        mine = [pl.ds(pl.multiple_of((turn * per_turn + j) * GROUP, GROUP), GROUP) for j in every]
        lines = [turn * per_turn + j for j in every]
        taps = [
            [[short_ref[i, step * per_step + lines[j], k] for k in range(SHORT)] for i in range(3)] for j in every
        ]
        for a, h, where in places:
            at = pl.multiple_of((order[where] + 1) * GROUP, GROUP)
            for j in every:
                for i in range(3):
                    part = proj_refs[0][a][i, mine[j], h * LONG : (h + 1) * LONG].astype(F32)
                    for s in range(1, sets):
                        part = part + proj_refs[s][a][i, mine[j], h * LONG : (h + 1) * LONG].astype(F32)
                    p_s[j, i, pl.ds(at, GROUP), :] = part.astype(BF16)

        for j in every:
            for i in range(3):
                two_blocks = jnp.concatenate([p_s[j, i, GROUP:, :], p_s[j, i, :rows, :]], axis=1)
                m_s[j, i] = dot(two_blocks, past_ref[...], ((1,), (0,))).astype(BF16)
        for j in every:
            for at in at_block:
                feat = []
                for i in range(3):
                    here = p_s[j, i, at.stop : at.stop + GROUP, :].astype(F32)
                    past = m_s[j, i, at, :].astype(F32)
                    feat.append(taps[j][i][0] * here + taps[j][i][1] * past[:, :LONG] + taps[j][i][2] * past[:, LONG:])
                    f_s[j, i, at, :] = feat[i]
                x_s[j, at.stop : at.stop + GROUP, :] = (feat[1] * feat[2]).astype(BF16)

        filters, turned = [], []
        for j in every:
            for ref, made in ((long_ref, filters), (turned_ref, turned)):
                base = jnp.broadcast_to(ref[0, pl.ds(lines[j], 1), :], (8, LONG))
                for bit in (1, 2, 4):
                    base = jnp.where((sub8 & bit) != 0, pltpu.roll(base, bit, 1), base)
                full = jnp.concatenate([base] + [pltpu.roll(base, 8 * m, 1) for m in range(1, LONG // 8)], axis=0)
                inside = col >= row if made is filters else col <= row
                near = jnp.where(inside, full, 0.0).astype(BF16)
                far = jnp.where(inside, 0.0, full).astype(BF16)
                made.append(jnp.concatenate([near, far], axis=0))

        x_twos = [jnp.concatenate([x_s[j, GROUP:, :], x_s[j, :rows, :]], axis=1) for j in every]
        inners = [dot(x_twos[j], filters[j], ((1,), (0,))) for j in every]
        for j in every:
            for n, at in enumerate(at_block):
                g = g_ref[n, mine[j], :].astype(F32)
                feat, inner = f_s[j, 0, at, :], inners[j][at]
                mixed_ref[n, mine[j], :] = (feat * inner).astype(BF16)
                y_s[j, at, :] = (g * feat).astype(BF16)
                q_s[j, at, :] = g * inner
        d_products = []
        for j in every:
            y_two = jnp.concatenate([y_s[j, :rows, :], y_s[j, GROUP:, :]], axis=1)
            d_products.append(dot(y_two, turned[j], ((1,), (0,))))
        folds = [dot(y_s[j, :rows, :], x_twos[j], ((0,), (0,))) for j in every]
        for j in every:
            fold = jnp.where(col <= row, folds[j][:, :LONG], folds[j][:, LONG:])
            width = LONG
            while width > 8:
                width //= 2
                fold = fold[:width] + pltpu.roll(fold[width:], LONG - width, 1)
            for bit in (4, 2, 1):
                fold = jnp.where((sub8 & bit) != 0, pltpu.roll(fold, LONG - bit, 1), fold)
            gl_ref[0, pl.ds(lines[j], 1), :] = jnp.sum(fold, axis=0, keepdims=True)

        for j in every:
            sums = [[zero] * SHORT for _ in range(3)]
            for at in at_block:
                d_product = d_products[j][at]
                for i, d in enumerate((q_s[j, at, :], d_product * f_s[j, 2, at, :], d_product * f_s[j, 1, at, :])):
                    here = p_s[j, i, at.stop : at.stop + GROUP, :].astype(F32)
                    past = m_s[j, i, at, :].astype(F32)
                    seen = (here, past[:, :LONG], past[:, LONG:])
                    sums[i] = [total + d * p for total, p in zip(sums[i], seen)]
                    d_s[j, i, at, :] = d.astype(BF16)
            for i in range(3):
                for k in range(SHORT):
                    gs_ref[0, lines[j], 3 * i + k : 3 * i + k + 1, :] = jnp.sum(sums[i][k], axis=0, keepdims=True)
        for j in every:
            for i in range(3):
                two_blocks = jnp.concatenate([d_s[j, i, :rows, :], d_s[j, i, GROUP:, :]], axis=1)
                coming = dot(two_blocks, next_ref[...], ((1,), (0,)))
                for at in at_block:
                    here = d_s[j, i, at, :].astype(F32)
                    near, far = coming[at, :LONG], coming[at, LONG:]
                    e_s[j, i, at, :] = (
                        taps[j][i][0] * here + taps[j][i][1] * near + taps[j][i][2] * far
                    ).astype(BF16)
        for a, h, where in d_places:
            at = pl.multiple_of(order[where] * GROUP, GROUP)
            for j in every:
                for i in range(3):
                    d_refs[a][i, mine[j], h * LONG : (h + 1) * LONG] = e_s[j, i, pl.ds(at, GROUP), :]


def mix(order, short_kernel, long_kernel, turned_kernel, g, proj_sets, grouped):
    blocks, channels, _ = g.shape
    count, sets = len(proj_sets[0]), len(proj_sets)
    groups = channels // GROUP
    per_turn = 1
    per_step = next(n for n in (4, 2, 1) if groups % n == 0)
    steps = groups // per_step
    rows = blocks * GROUP
    high = per_step * GROUP
    proj_specs = [pl.BlockSpec((3, high, x.shape[2]), lambda i, o: (0, i, 0)) for x in proj_sets[0]]
    d_widths = [sum(proj_sets[0][a].shape[2] for a in arrays) for arrays in grouped]
    d_specs = [pl.BlockSpec((3, high, w), lambda i, o: (0, i, 0)) for w in d_widths]
    token_spec = pl.BlockSpec((blocks, high, LONG), lambda i, o: (0, i, 0))
    shifts = [jnp.asarray(shift_matrix(way), BF16) for way in (-1, 1)]
    outs = pl.pallas_call(
        functools.partial(mix_body, count, sets, per_turn, grouped),
        grid_spec=pltpu.PrefetchScalarGridSpec(
            num_scalar_prefetch=1,
            grid=(steps,),
            in_specs=[
                pl.BlockSpec(memory_space=pltpu.SMEM),
                pl.BlockSpec((1, per_step, LONG), lambda i, o: (i, 0, 0)),
                pl.BlockSpec((1, per_step, LONG), lambda i, o: (i, 0, 0)),
                pl.BlockSpec((2 * LONG, 2 * LONG), lambda i, o: (0, 0)),
                pl.BlockSpec((2 * LONG, 2 * LONG), lambda i, o: (0, 0)),
                token_spec,
            ]
            + proj_specs * sets,
            out_specs=[token_spec]
            + d_specs
            + [
                pl.BlockSpec((1, per_step, 3 * SHORT, LONG), lambda i, o: (i, 0, 0, 0)),
                pl.BlockSpec((1, per_step, LONG), lambda i, o: (i, 0, 0)),
            ],
            scratch_shapes=[
                pltpu.VMEM((per_turn, 3, rows + GROUP, LONG), BF16),
                pltpu.VMEM((per_turn, 3, rows, 2 * LONG), BF16),
                pltpu.VMEM((per_turn, 3, rows, LONG), F32),
                pltpu.VMEM((per_turn, rows + GROUP, LONG), BF16),
                pltpu.VMEM((per_turn, rows + GROUP, LONG), BF16),
                pltpu.VMEM((per_turn, rows, LONG), F32),
                pltpu.VMEM((per_turn, 3, rows + GROUP, LONG), BF16),
                pltpu.VMEM((per_turn, 3, rows, LONG), BF16),
            ],
        ),
        out_shape=[jax.ShapeDtypeStruct((blocks, channels, LONG), BF16)]
        + [jax.ShapeDtypeStruct((3, channels, w), BF16) for w in d_widths]
        + [
            jax.ShapeDtypeStruct((steps, per_step, 3 * SHORT, LONG), F32),
            jax.ShapeDtypeStruct((steps, per_step, LONG), F32),
        ],
        compiler_params=pltpu.CompilerParams(vmem_limit_bytes=58 * MIB),
        cost_estimate=SMALL,
    )(order, short_kernel, long_kernel.reshape(steps, per_step, LONG), turned_kernel.reshape(steps, per_step, LONG), *shifts, g, *[x for s in proj_sets for x in s])
    mixed, d_proj, (gs, gl) = outs[0], outs[1:-2], outs[-2:]
    grad_short = jnp.sum(gs, axis=-1).reshape(groups, 3, SHORT).transpose(1, 0, 2)
    grad_long = turn_taps(gl.reshape(groups, LONG))
    return mixed, d_proj, grad_short, grad_long


def restack_body(t_ref, *refs):
    out_ref = refs[3]
    for i in range(3):
        out_ref[0, i] = refs[i][0]


def restack(t, weights):
    _, channels, width = weights[0].shape
    tile = min(128, channels)

    def source(side, part, t):
        return (jnp.where(side == 0, t[0], 1 - t[0]), part, 0)

    return pl.pallas_call(
        restack_body,
        grid_spec=pltpu.PrefetchScalarGridSpec(
            num_scalar_prefetch=1,
            grid=(2, channels // tile),
            in_specs=[pl.BlockSpec((1, tile, width), source)] * 3,
            out_specs=pl.BlockSpec((1, 3, tile, width), lambda side, part, t: (side, 0, part, 0)),
        ),
        out_shape=jax.ShapeDtypeStruct((2, 3, channels, width), BF16),
        compiler_params=pltpu.CompilerParams(vmem_limit_bytes=16 * MIB),
        cost_estimate=SMALL,
    )(t.reshape(1), *weights).reshape(6 * channels, width)


def project_body(pieces, *refs):
    x_refs, w_ref = refs[:pieces], refs[pieces]
    far_ref, near_ref, x_s, sems = refs[pieces + 1 :]
    step, steps = pl.program_id(0), pl.num_programs(0)

    @pl.when(step == 0)
    def _():
        copies, at = [], 0
        for n, x in enumerate(x_refs):
            copies.append(pltpu.make_async_copy(x, x_s.at[pl.ds(at, x.shape[0])], sems.at[n]))
            at += x.shape[0]
        for copy in copies:
            copy.start()
        for copy in copies:
            copy.wait()

    got = dot(w_ref[...], x_s[...], ((1,), (1,))).astype(BF16)

    @pl.when(step < steps // 2)
    def _():
        far_ref[...] = got

    @pl.when(step >= steps // 2)
    def _():
        near_ref[...] = got


def project_kernel(flat, pieces):
    rows, width = flat.shape
    tokens = sum(x.shape[0] for x in pieces)
    tile = rows // 4
    half = jax.ShapeDtypeStruct((rows // 2, tokens), BF16)
    far, near = pl.pallas_call(
        functools.partial(project_body, len(pieces)),
        grid=(4,),
        in_specs=[pl.BlockSpec(memory_space=pl.ANY)] * len(pieces)
        + [pl.BlockSpec((tile, width), lambda i: ((i + 2) % 4, 0))],
        out_specs=[
            pl.BlockSpec((tile, tokens), lambda i: (jnp.minimum(i, 1), 0)),
            pl.BlockSpec((tile, tokens), lambda i: (jnp.maximum(i - 2, 0), 0)),
        ],
        out_shape=[half, half],
        scratch_shapes=[pltpu.VMEM((tokens, width), BF16), pltpu.SemaphoreType.DMA((len(pieces),))],
        compiler_params=pltpu.CompilerParams(vmem_limit_bytes=16 * MIB),
        cost_estimate=SMALL,
    )(*pieces, flat)
    return near, far


def unproject_body(near_ref, far_ref, w_ref, *refs):
    out_refs, d_s = refs[:-1], refs[-1]
    stay = near_ref.shape[0]

    @pl.when(pl.program_id(0) == 0)
    def _():
        d_s[:, 0:stay] = near_ref[...].T
        d_s[:, stay:] = far_ref[...].T

    got = dot(d_s[...], w_ref[...], ((1,), (0,)))
    at = 0
    for out_ref in out_refs:
        out_ref[...] = got[at : at + out_ref.shape[0]].astype(BF16)
        at += out_ref.shape[0]


def unproject_kernel(flat, near, far, cuts):
    rows, width = flat.shape
    tokens = near.shape[1]
    tile = min(1024, width)
    return pl.pallas_call(
        unproject_body,
        grid=(width // tile,),
        in_specs=[
            pl.BlockSpec((rows // 2, tokens), lambda i: (0, 0)),
            pl.BlockSpec((rows // 2, tokens), lambda i: (0, 0)),
            pl.BlockSpec((rows, tile), lambda i: (0, i)),
        ],
        out_specs=[pl.BlockSpec((cut, tile), lambda i: (0, i)) for cut in cuts],
        out_shape=[jax.ShapeDtypeStruct((cut, width), BF16) for cut in cuts],
        scratch_shapes=[pltpu.VMEM((tokens, rows), BF16)],
        compiler_params=pltpu.CompilerParams(vmem_limit_bytes=20 * MIB),
        cost_estimate=SMALL,
    )(near, far, flat)


def add_body(heights, *refs):
    out_refs = refs[sum(heights) :]
    groups, at = [], 0
    for height in heights:
        groups.append(refs[at : at + height])
        at += height
    tops = [[sum(r.shape[0] for r in group[:n]) for n in range(len(group) + 1)] for group in groups]
    height = out_refs[0].shape[0]
    edges = {edge for top in tops for edge in top} | {n * height for n in range(len(out_refs) + 1)}
    edges = sorted(edges)
    for low, high in zip(edges[:-1], edges[1:]):
        total = None
        for group, top in zip(groups, tops):
            for n, ref in enumerate(group):
                if top[n] <= low and high <= top[n + 1]:
                    part = ref[low - top[n] : high - top[n], :].astype(F32)
                    total = part if total is None else total + part
        out_refs[low // height][low % height : low % height + high - low, :] = total.astype(BF16)


def add_kernel(*groups, cut=1):
    rows, width = sum(x.shape[0] for x in groups[0]) // cut, groups[0][0].shape[1]
    tile = min(1024, width)
    arrays = [x for group in groups for x in group]
    return pl.pallas_call(
        functools.partial(add_body, [len(group) for group in groups]),
        grid=(width // tile,),
        in_specs=[pl.BlockSpec((x.shape[0], tile), lambda i: (0, i)) for x in arrays],
        out_specs=[pl.BlockSpec((rows, tile), lambda i: (0, i))] * cut,
        out_shape=[jax.ShapeDtypeStruct((rows, width), BF16)] * cut,
        compiler_params=pltpu.CompilerParams(vmem_limit_bytes=8 * MIB),
        cost_estimate=SMALL,
    )(*arrays)


def copy_body(in_ref, out_ref):
    out_ref[...] = in_ref[...]


def copy_kernel(x):
    rows, width = x.shape
    tile = rows // 4
    return pl.pallas_call(
        copy_body,
        grid=(4,),
        in_specs=[pl.BlockSpec((tile, width), lambda i: (i, 0))],
        out_specs=pl.BlockSpec((tile, width), lambda i: (i, 0)),
        out_shape=jax.ShapeDtypeStruct(x.shape, x.dtype),
        compiler_params=pltpu.CompilerParams(vmem_limit_bytes=8 * MIB),
        cost_estimate=SMALL,
    )(x)


def on_device(ring, n_tp, tokens_in, w_query, w_key, w_value, short_taps, long_taps, grad_out):
    chips = len(ring)
    half = chips // 2
    n_ctx = 2 * chips
    held, width = tokens_in.shape
    channels = w_query.shape[1]
    weights = (w_query, w_key, w_value)

    def one_way(x, turned=False, to_mate=False):
        hops = []
        for j in range(chips):
            for core in range(2):
                chip = ring[(j + (1 if (core == 0) != turned else -1)) % chips]
                hops.append((2 * ring[j] + core, 2 * chip + (core ^ int(to_mate))))
        return lax.ppermute(x, "ctx", hops)

    def swap(x):
        return lax.ppermute(x, "ctx", [(d, d ^ 1) for d in range(n_ctx)])

    table = np.zeros((n_ctx, n_ctx), np.int32)
    for device in range(n_ctx):
        place, core = ring.index(device // 2), device % 2
        way = -1 if core == 0 else 1
        items = [(0, 0), (0, 1)]
        for s in range(1, half):
            items += [(way * s, 0), (way * s, 1), (-way * s, 1), (-way * s, 0)]
        items += [(half, 0), (half, 1)]
        table[device] = [2 * ring[(place + hop) % chips] + (core ^ other) for hop, other in items]
    order = lax.dynamic_index_in_dim(jnp.asarray(table), lax.axis_index("ctx"), 0, keepdims=False)
    short_kernel, long_kernel = short_taps.reshape(3, -1, SHORT), long_taps.reshape(-1, LONG)
    turned_kernel = turn_taps(long_kernel)

    stay = 3 * channels
    if n_tp == 2:
        t = lax.axis_index("tp").astype(jnp.int32)
        t, order, short_kernel, turned_kernel = lax.optimization_barrier((t, order, short_kernel, turned_kernel))
        flat = restack(t, weights)
    else:
        flat = jnp.stack(weights).reshape(-1, width)

    def project(pieces):
        if n_tp == 2:
            return project_kernel(flat, pieces)
        y = dot(flat, jnp.concatenate(pieces, axis=0), ((1,), (1,))).astype(BF16).reshape(3, n_tp, channels, -1)
        return lax.psum_scatter(y, "tp", scatter_dimension=1, tiled=True).reshape(stay, -1), None

    def across(x):
        return None if x is None else lax.ppermute(x, "tp", [(0, 1), (1, 0)])

    def meet(d):
        if n_tp == 2:
            return d.reshape(stay, -1), across(d.reshape(stay, -1))
        d = lax.all_gather(d.reshape(3, 1, channels, -1), "tp", axis=1, tiled=True)
        return (d.reshape(-1, d.shape[-1]),)

    def unproject(d, *cuts):
        if n_tp == 2:
            return unproject_kernel(flat, *d, cuts)
        y = dot(d[0], flat, ((0,), (0,))).astype(BF16)
        return jnp.split(y, np.cumsum(cuts)[:-1], axis=0)

    stage = lax.optimization_barrier

    arrived = [one_way(tokens_in), one_way(tokens_in, to_mate=True, turned=True)]
    near, far = project([tokens_in, swap(tokens_in)])
    arrived, near, far = stage((arrived, near, far))
    arrived = jnp.concatenate(arrived, axis=0)
    projected = []
    for s in range(1, half):
        coming = one_way(arrived if s < half - 1 else arrived[:held])
        projected.append((near, across(far)))
        near, far = project([arrived, swap(arrived)])
        if s < half - 1:
            arrived, near, far, projected[-1] = stage((coming, near, far, projected[-1]))
    crossed = across(far)
    arrived, near, grad_out = stage((coming, near, grad_out))
    incoming = lax.all_to_all(
        grad_out.reshape(n_ctx, channels, held), "ctx", split_axis=0, concat_axis=0, tiled=True
    )
    shared, projected[-1] = stage((arrived, projected[-1]))
    last, far = project([arrived, swap(shared[: held // 2]), swap(shared[held // 2 :])])
    projected += [(near, crossed), (last, across(far))]

    mixed, d_proj, grad_short, grad_long = mix(
        order,
        short_kernel,
        long_kernel,
        turned_kernel,
        incoming,
        [[y.reshape(3, channels, -1) for y in side] for side in zip(*projected) if side[0] is not None],
        [[s] for s in range(half + 1)],
    )

    first, met, later = [meet(d_proj[s]) for s in (half, half - 1, half - 2)]
    mixed_out = lax.all_to_all(mixed, "ctx", split_axis=0, concat_axis=0, tiled=True).reshape(-1, held)
    first, grad_short, grad_long = stage((first, grad_short, grad_long))
    keep, *give = unproject(first, held, *((80, 48) if held == 128 else (held // 2, held // 2)))
    total = add_kernel([keep], [swap(x) for x in give])
    total, met, rest = stage((total, met, d_proj[: half - 2]))
    for s in range(half - 1, 0, -1):
        coming = one_way(total[0], turned=True)
        if s < half - 1:
            later = meet(rest[-1])
            rest = rest[:-1]
        cuts = (96, 96, 64) if s == half - 1 and held == 128 else (held, held)
        keep, *give = unproject(met, 2 * held, *cuts)
        give[-1], later = stage((give[-1], later))
        total = add_kernel([keep], [swap(x) for x in give], [coming], cut=2 if s == 1 else 1)
        if s == half - 2:
            mixed_out = copy_kernel(mixed_out)
        total, met, rest, mixed_out = stage((total, later, rest, mixed_out))
    coming = [one_way(total[0], turned=True), one_way(total[1], turned=True, to_mate=True)]
    keep, *give = unproject(met, held, held // 2, held // 2)
    (grad_tokens,) = add_kernel([keep], [swap(x) for x in give], coming[:1], coming[1:])
    return (
        mixed_out,
        grad_tokens,
        grad_short.reshape(3, 1, -1, SHORT),
        grad_long.reshape(1, -1, LONG),
    )


def solution(mesh):
    placed = (
        P("ctx", "tp"),
        P(None, "ctx", "tp"),
        P(None, "ctx", "tp"),
        P(None, "ctx", "tp"),
        P(None, "tp", "ctx", None),
        P("tp", "ctx", None),
        P("tp", "ctx"),
    )
    return jax.shard_map(
        functools.partial(on_device, ring_of(mesh), mesh.shape["tp"]),
        mesh=mesh,
        in_specs=placed,
        out_specs=(
            P("tp", "ctx"),
            P("ctx", "tp"),
            P(None, "tp", "ctx", None),
            P("tp", "ctx", None),
        ),
        check_vma=False,
    )
```
